128 devices in a mesh: row: 8 (over x, core), col: 16 (over z, y).
Axes of the slice: x: 4, y: 4, z: 4, core: 2. Of those that a mesh axis runs over, the one named last changes fastest.
Arguments:
- object_field: float32 [2, 6144, 12288], P(None, 'row', 'col'), may hold values from -1.5 to 1.5, as said below
- probe_modes: float32 [2, 2, 256, 256], replicated, may hold values from -3 to 3
- counts: int32 [8, 16], replicated, may hold values from 1 to 12, 64 in all within a row
- centers: int32 [8, 16, 2, 12], P('row', 'col'), may hold values from 0 to 767
- patterns: bfloat16 [8, 16, 12, 256, 256], P('row', 'col'), may hold values from 1 to 32
Outputs:
- new_object: float32 [2, 6144, 12288], P(None, 'row', 'col')
- new_probe: float32 [2, 2, 256, 256], replicated
The draws below stay inside these ranges and needn't reach their ends.
Inputs may be any that keep to these rules, and one draw needn't show every extreme that they name: Each row of counts sums to 64 and its largest entry is 12. `centers`: slot s of tile (r, c) is used only if s < counts[r, c]. `object_field`: each pixel is a complex value of magnitude between 0.5 and 1.5.
All inputs are finite; a program needn't handle non-finite values.
Results may differ from the reference program's by a relative error of at most 0.0038.
The reference program's roundings to bfloat16 on the way count: a program that leaves them out, or rounds other values in their place, can miss the bound.
Values may be sent and summed in bfloat16 or wider, within the bound.
A program may use at most 128 MiB of HBM per device.

```python
import math
import jax
import jax.numpy as jnp
import numpy as np
from jax import lax

TILE = 768
P_SIZE = 256
MODES = 2
SLOTS = 12
ROW_POSITIONS = 64
OBJ_ROWS = 6144
OBJ_COLS = 12288
N_ROW = 8
N_COL = 16


def draw_object_field(key, part):
    key = jax.random.fold_in(key, 11)
    key_size, key_angle = jax.random.split(key, 2)
    grid_shape = (OBJ_ROWS, OBJ_COLS)
    magnitude = jax.random.uniform(key_size, grid_shape, jnp.float32, 0.5, 1.5)
    phase_angle = jax.random.uniform(key_angle, grid_shape, jnp.float32, -math.pi, math.pi)
    return jnp.stack([magnitude * jnp.cos(phase_angle), magnitude * jnp.sin(phase_angle)])


def place_ends(drawn, stream_key, smallest, largest):
    shape = drawn.shape
    place = [jax.random.randint(jax.random.fold_in(stream_key, axis), (), 0, shape[axis]) for axis in range(len(shape))]
    drawn = drawn.at[tuple(place)].set(smallest)
    longest = shape.index(max(shape))
    place[longest] = (place[longest] + 1) % shape[longest]
    return drawn.at[tuple(place)].set(largest)


def levels(stream_key, extent, cuts, smallest, top_value):
    factor_of, own = 1.0, jax.random.fold_in(stream_key, 6)
    for dim, parts in cuts:
        steps = jnp.exp(jax.random.uniform(jax.random.fold_in(own, dim), (parts,), jnp.float32, smallest / len(cuts), top_value / len(cuts)))
        factor_of = factor_of * jnp.repeat(steps, extent[dim] // parts).reshape([-1 if axis == dim else 1 for axis in range(len(extent))])
    return factor_of


def split_up(amount, total, most, lean):
    weights = [(1 << 20) // math.isqrt(standing ** lean) + 1 for standing in range(2, amount + 1)]
    spare, holding = total - most - (amount - 1), [1] * (amount - 1)
    while spare > 0:
        candidates = [i for i in range(amount - 1) if holding[i] < most]
        pool, budget = sum([weights[i] for i in candidates]), spare
        for i in candidates:
            more = min(most - holding[i], max(1, budget * weights[i] // pool), spare)
            holding[i] = holding[i] + more
            spare = spare - more
    return np.array([most] + holding)


def ragged_sizes(stream_key, number_of, total, limit, skew):
    if number_of == 2:
        one = jax.random.randint(stream_key, (), max(1, total - limit), min(limit, total - 1) + 1)
        return jnp.stack([one, total - one])
    sizes = jnp.asarray(split_up(number_of, total, limit, skew), jnp.int32)
    couples = (number_of - 1) // 2
    source_of, receiver = sizes[1:1 + 2 * couples:2], sizes[2:2 + 2 * couples:2]
    room = jnp.minimum(source_of - 1, limit - receiver)
    shifted = jax.random.randint(jax.random.fold_in(stream_key, 1), (couples,), 0, 1 << 20) % (room + 1)
    sizes = sizes.at[1:1 + 2 * couples:2].set(source_of - shifted).at[2:2 + 2 * couples:2].set(receiver + shifted)
    return sizes[jax.random.permutation(jax.random.fold_in(stream_key, 2), number_of)]


def normal_values(stream_key, extent, spread, most, held_as=jnp.bfloat16):
    return jnp.clip(spread * jax.random.normal(stream_key, extent, jnp.float32), -most, most).astype(held_as)


def setup_inputs(seed: int = 0) -> dict:
    streams_of = jax.random.split(jax.random.key(seed), 6)
    return {
        "object_field": draw_object_field(jax.random.fold_in(streams_of[5], 71), 0),
        "probe_modes": normal_values(streams_of[1], (MODES, 2, P_SIZE, P_SIZE), 0.5, 3.0, jnp.float32),
        "counts": jax.vmap(lambda own: ragged_sizes(own, N_COL, ROW_POSITIONS, SLOTS, 2))(jax.random.split(streams_of[2], N_ROW)).reshape((N_ROW, N_COL)).astype(jnp.int32),
        "centers": place_ends(jax.random.randint(streams_of[3], (N_ROW, N_COL, 2, SLOTS), 0, TILE), jax.random.fold_in(streams_of[3], 1), 0, TILE - 1).astype(jnp.int32),
        "patterns": jnp.clip(jnp.exp(math.log(32.0) - 3.465736 * jax.random.uniform(streams_of[4], (N_ROW, N_COL, SLOTS, P_SIZE, P_SIZE), jnp.float32) ** levels(streams_of[4], (N_ROW, N_COL, SLOTS, P_SIZE, P_SIZE), ((0, 8), (1, 16)), -0.2, 0.2)), 1.0, 32.0).astype(jnp.bfloat16),
    }


def dft_pair(length):
    indices = jnp.arange(length, dtype=jnp.int32)
    product = indices[:, None] * indices[None, :] % length
    angles = product.astype(jnp.float32) * (2.0 * jnp.pi / length)
    factor = 1.0 / jnp.sqrt(jnp.float32(length))
    cosine_table = (jnp.cos(angles) * factor).astype(jnp.bfloat16)
    sine_table = (jnp.sin(angles) * factor).astype(jnp.bfloat16)
    return (cosine_table, sine_table)

def matmul(left_side, right_side):
    return jnp.dot(left_side, right_side, preferred_element_type=jnp.float32)

def position_terms(patch_window, amplitude, probe_lower_edge, cosine_table, sine_table):
    patch_real = patch_window[0].astype(jnp.float32)
    patch_imag = patch_window[1].astype(jnp.float32)
    spectra = []
    total_power = jnp.zeros(patch_real.shape, jnp.float32)
    for mode_index in range(MODES):
        probe_real = probe_lower_edge[mode_index, 0].astype(jnp.float32)
        probe_imag = probe_lower_edge[mode_index, 1].astype(jnp.float32)
        wave_real = (probe_real * patch_real - probe_imag * patch_imag).astype(jnp.bfloat16)
        wave_imag = (probe_real * patch_imag + probe_imag * patch_real).astype(jnp.bfloat16)
        half_real = (matmul(wave_real, cosine_table) + matmul(wave_imag, sine_table)).astype(jnp.bfloat16)
        half_imag = (matmul(wave_imag, cosine_table) - matmul(wave_real, sine_table)).astype(jnp.bfloat16)
        spec_real = matmul(cosine_table, half_real) + matmul(sine_table, half_imag)
        spec_imag = matmul(cosine_table, half_imag) - matmul(sine_table, half_real)
        spectra.append((spec_real, spec_imag))
        total_power = total_power + spec_real * spec_real + spec_imag * spec_imag
    factor = amplitude.astype(jnp.float32) / jnp.sqrt(jnp.maximum(total_power, 0.5)) - 1.0
    object_real = jnp.zeros(patch_real.shape, jnp.float32)
    object_imag = jnp.zeros(patch_real.shape, jnp.float32)
    probe_parts = []
    for mode_index in range(MODES):
        probe_real = probe_lower_edge[mode_index, 0].astype(jnp.float32)
        probe_imag = probe_lower_edge[mode_index, 1].astype(jnp.float32)
        spec_real, spec_imag = spectra[mode_index]
        shift_real = (factor * spec_real).astype(jnp.bfloat16)
        shift_imag = (factor * spec_imag).astype(jnp.bfloat16)
        back_real = (matmul(shift_real, cosine_table) - matmul(shift_imag, sine_table)).astype(jnp.bfloat16)
        back_imag = (matmul(shift_imag, cosine_table) + matmul(shift_real, sine_table)).astype(jnp.bfloat16)
        change_real = matmul(cosine_table, back_real) - matmul(sine_table, back_imag)
        change_imag = matmul(cosine_table, back_imag) + matmul(sine_table, back_real)
        object_real = object_real + probe_real * change_real + probe_imag * change_imag
        object_imag = object_imag + probe_real * change_imag - probe_imag * change_real
        probe_parts.append(jnp.stack([patch_real * change_real + patch_imag * change_imag, patch_real * change_imag - patch_imag * change_real]))
    object_term = jnp.stack([object_real, object_imag]).astype(jnp.bfloat16)
    coverage = patch_real * patch_real + patch_imag * patch_imag
    return (object_term, jnp.stack(probe_parts), coverage)

def reference(object_field, probe_modes, counts, centers, patterns):
    cosine_table, sine_table = dft_pair(P_SIZE)
    half_width = P_SIZE // 2
    object_low = object_field.astype(jnp.bfloat16)
    probe_lower_edge = probe_modes.astype(jnp.bfloat16)
    padded = jnp.pad(object_low, ((0, 0), (half_width, half_width), (half_width, half_width)))
    row_base = (jnp.arange(N_ROW, dtype=jnp.int32) * TILE)[:, None, None]
    col_base = (jnp.arange(N_COL, dtype=jnp.int32) * TILE)[None, :, None]
    row_offsets = (centers[:, :, 0, :].astype(jnp.int32) + row_base).reshape(-1)
    column_offsets = (centers[:, :, 1, :].astype(jnp.int32) + col_base).reshape(-1)
    slot_numbers = jnp.arange(SLOTS, dtype=jnp.int32)[None, None, :]
    activity_flags = (slot_numbers < counts[:, :, None].astype(jnp.int32)).astype(jnp.float32).reshape(-1)
    measured_amplitudes = patterns.reshape(-1, P_SIZE, P_SIZE)
    zero_index = jnp.zeros((), jnp.int32)
    starting_guess = (jnp.zeros(padded.shape, jnp.float32), jnp.zeros((MODES, 2, P_SIZE, P_SIZE), jnp.float32), jnp.zeros((P_SIZE, P_SIZE), jnp.float32))

    def handle_scan_position(running, inputs):
        canvas, probe_total, cover_total = running
        row_start, col_start, amplitude, alive_flag = inputs
        patch_window = lax.dynamic_slice(padded, (zero_index, row_start, col_start), (2, P_SIZE, P_SIZE))
        object_term, probe_part, coverage = position_terms(patch_window, amplitude, probe_lower_edge, cosine_table, sine_table)
        placed = lax.dynamic_slice(canvas, (zero_index, row_start, col_start), (2, P_SIZE, P_SIZE))
        placed = placed + object_term.astype(jnp.float32) * alive_flag
        canvas = lax.dynamic_update_slice(canvas, placed, (zero_index, row_start, col_start))
        return ((canvas, probe_total + alive_flag * probe_part, cover_total + alive_flag * coverage), None)
    final_results, ignored_value = lax.scan(handle_scan_position, starting_guess, (row_offsets, column_offsets, measured_amplitudes, activity_flags))
    canvas, probe_total, cover_total = final_results
    gradient = canvas[:, half_width:half_width + OBJ_ROWS, half_width:half_width + OBJ_COLS]
    intensity = lax.optimization_barrier(jnp.sum(probe_modes * probe_modes, axis=(0, 1)))
    peak = jnp.max(intensity) + 1e-06
    new_object = object_field + gradient / peak
    new_probe = probe_modes + probe_total / jnp.sqrt(cover_total)
    return (new_object, new_probe)
```

```python
import functools
import math

import jax
import jax.numpy as jnp
import ml_dtypes
import numpy as np
from jax import lax
from jax.experimental import pallas as pl
from jax.experimental.pallas import tpu as pltpu
from jax.sharding import PartitionSpec as P

MESH = pl.DeviceIdType.MESH
F32, BF16 = jnp.float32, jnp.bfloat16
SIZE, TILE, HALF, LANES = 256, 768, 128, 128
EXT = TILE + 2 * HALF
PANELS = TILE // LANES
MODES = 2
PLANES = 2 * MODES
N_ROW, N_COL = 8, 16
UNITS = 128
VMEM = pl.BlockSpec(memory_space=pltpu.VMEM)
SMEM = pl.BlockSpec(memory_space=pltpu.SMEM)
ANY = pl.BlockSpec(memory_space=pl.ANY)
LIMIT = 40 * 2**20


def dft_tables():
    indices = np.arange(SIZE)
    product = indices[:, None] * indices[None, :] % SIZE
    angles = product.astype(np.float32) * np.float32(2.0 * np.pi / SIZE)
    scale = np.float32(1.0 / math.sqrt(SIZE))
    cosine = (np.cos(angles) * scale).astype(ml_dtypes.bfloat16)
    sine = (np.sin(angles) * scale).astype(ml_dtypes.bfloat16)
    positive = np.block([[cosine, -sine], [sine, cosine]])
    negative = np.block([[cosine, sine], [-sine, cosine]])
    return positive, negative


def around(row, col):
    up, down = lax.rem(row + N_ROW - 1, N_ROW), lax.rem(row + 1, N_ROW)
    left, right = lax.rem(col + N_COL - 1, N_COL), lax.rem(col + 1, N_COL)
    return [(up, col), (down, col), (row, left), (row, right), (up, left), (up, right), (down, left), (down, right)]


def greet(targets):
    barrier = pltpu.get_barrier_semaphore()
    for target in targets:
        pl.semaphore_signal(barrier, inc=1, device_id=target, device_id_type=MESH)
    return barrier


def remote(src, dst, send, recv, target):
    return pltpu.make_async_remote_copy(
        src_ref=src, dst_ref=dst, send_sem=send, recv_sem=recv, device_id=target, device_id_type=MESH
    )


def inside(row, col):
    up, down, left, right = row > 0, row < N_ROW - 1, col > 0, col < N_COL - 1
    return [up, down, left, right, up & left, up & right, down & left, down & right]


def rim_copies(out, got, send, recv, row, col):
    opposite = (1, 0, 3, 2, 7, 6, 5, 4)
    return [
        remote(out[i], got[opposite[i]], send.at[i], recv.at[opposite[i]], target)
        for i, target in enumerate(around(row, col))
    ]


def exchange_object(obj, wide, held, low_v, low_h, got_v, got_h, got_c, load, send, recv):
    row, col = lax.axis_index("row"), lax.axis_index("col")
    order = (0, PANELS - 1) + tuple(range(1, PANELS - 1))
    loads = [
        pltpu.make_async_copy(obj.at[:, :, k * LANES : (k + 1) * LANES], held.at[:, k], load.at[k])
        for k in range(PANELS)
    ]
    for k in order:
        loads[k].start()
    barrier = greet(around(row, col))
    rims = rim_copies(
        [low_v.at[0], low_v.at[1], low_h.at[0], low_h.at[1]]
        + [low_h.at[0, :, 0:HALF], low_h.at[1, :, 0:HALF], low_h.at[0, :, TILE - HALF :], low_h.at[1, :, TILE - HALF :]],
        [got_v.at[0], got_v.at[1], got_h.at[0], got_h.at[1]] + [got_c.at[i] for i in range(4)],
        send,
        recv,
        row,
        col,
    )
    for step, k in enumerate(order):
        loads[k].wait()

        @pl.loop(0, TILE // HALF)
        def _(i, k=k):
            rows = pl.ds(pl.multiple_of(i * HALF, HALF), HALF)
            for p in range(2):
                low = held[p, k, rows, :].astype(BF16)
                wide[p, k + 1, pl.ds(pl.multiple_of(i * HALF + HALF, HALF), HALF), :] = low.astype(F32)
                if k == 0:
                    low_h[0, p, rows, :] = low
                if k == PANELS - 1:
                    low_h[1, p, rows, :] = low

        for p in range(2):
            low_v[0, p, k] = held[p, k, 0:HALF, :].astype(BF16)
            low_v[1, p, k] = held[p, k, TILE - HALF :, :].astype(BF16)
        if step == 1:
            pl.semaphore_wait(barrier, 8)
            for i in (2, 3, 4, 5, 6, 7):
                rims[i].start()
    for i in (0, 1):
        rims[i].start()
    have = inside(row, col)

    def keep(i, value):
        return jnp.where(have[i], value.astype(F32), 0.0)

    for i in (0, 1, 4, 5, 6, 7, 2, 3):
        rims[i].wait()
    for p in range(2):
        for k in range(PANELS):
            wide[p, k + 1, 0:HALF, :] = keep(0, got_v[0, p, k])
            wide[p, k + 1, EXT - HALF :, :] = keep(1, got_v[1, p, k])
        for corner in range(4):
            rows = slice(0, HALF) if corner < 2 else slice(EXT - HALF, EXT)
            wide[p, (corner % 2) * (PANELS + 1), rows, :] = keep(4 + corner, got_c[corner, p])

    @pl.loop(0, TILE // HALF)
    def _(i):
        rows = pl.ds(pl.multiple_of(i * HALF, HALF), HALF)
        to = pl.ds(pl.multiple_of(i * HALF + HALF, HALF), HALF)
        for p in range(2):
            wide[p, 0, to, :] = keep(2, got_h[0, p, rows, :])
            wide[p, PANELS + 1, to, :] = keep(3, got_h[1, p, rows, :])


def process_slots(counts, centers, wide, probe, patterns, positive, negative, units, canvas, low, sums, patch, wave, half, shift, back):
    row_id, col_id = lax.axis_index("row"), lax.axis_index("col")

    @pl.loop(0, EXT // 32)
    def _(i):
        rows = pl.ds(pl.multiple_of(i * 32, 32), 32)
        for p in range(2):
            for k in range(PANELS + 2):
                canvas[p, k, rows, :] = jnp.zeros((32, LANES), F32)

    low[...] = probe[...].astype(BF16).astype(F32)
    sums[...] = jnp.zeros_like(sums)
    lane = lax.broadcasted_iota(jnp.int32, (SIZE, LANES), 1)
    real, imag = slice(0, SIZE), slice(SIZE, 2 * SIZE)

    @pl.loop(0, counts[row_id, col_id])
    def _(s):
        row, col = centers[0, s], centers[1, s]
        panel = col // LANES
        turn = col - panel * LANES
        rows = pl.ds(row, SIZE)
        field = []
        for p in range(2):
            parts = [pltpu.roll(wide[p, panel + k, rows, :], lax.rem(LANES - turn, LANES), 1) for k in range(3)]
            whole = jnp.concatenate(
                [jnp.where(lane < LANES - turn, parts[k], parts[k + 1]) for k in range(2)], 1
            )
            patch[p] = whole
            field.append(whole)
        sums[PLANES] += field[0] * field[0] + field[1] * field[1]
        for m in range(MODES):
            wave[m, :, real] = (low[m, 0] * field[0] - low[m, 1] * field[1]).astype(BF16)
            wave[m, :, imag] = (low[m, 0] * field[1] + low[m, 1] * field[0]).astype(BF16)
        for m in range(MODES):
            product = jnp.dot(wave[m], positive[...], preferred_element_type=F32)
            half[m, real, :] = product[:, real].astype(BF16)
            half[m, imag, :] = product[:, imag].astype(BF16)
        spectra = []
        for m in range(MODES):
            spectra.append(
                (
                    jnp.dot(negative[real, :], half[m], preferred_element_type=F32),
                    jnp.dot(negative[imag, :], half[m], preferred_element_type=F32),
                )
            )
        power = (
            spectra[0][0] * spectra[0][0]
            + spectra[0][1] * spectra[0][1]
            + spectra[1][0] * spectra[1][0]
            + spectra[1][1] * spectra[1][1]
        )
        factor = patterns[s].astype(F32) * lax.rsqrt(jnp.maximum(power, 0.5)) - 1.0
        for m in range(MODES):
            shift[m, :, real] = (factor * spectra[m][0]).astype(BF16)
            shift[m, :, imag] = (factor * spectra[m][1]).astype(BF16)
        for m in range(MODES):
            product = jnp.dot(shift[m], negative[...], preferred_element_type=F32)
            back[m, real, :] = product[:, real].astype(BF16)
            back[m, imag, :] = product[:, imag].astype(BF16)
        terms = [0.0, 0.0]
        for m in range(MODES):
            change_real = jnp.dot(positive[real, :], back[m], preferred_element_type=F32)
            change_imag = jnp.dot(positive[imag, :], back[m], preferred_element_type=F32)
            terms[0] = terms[0] + low[m, 0] * change_real + low[m, 1] * change_imag
            terms[1] = terms[1] + low[m, 0] * change_imag - low[m, 1] * change_real
            sums[2 * m] += patch[0] * change_real + patch[1] * change_imag
            sums[2 * m + 1] += patch[0] * change_imag - patch[1] * change_real
        for p in range(2):
            term = terms[p].astype(BF16).astype(F32)
            first = pltpu.roll(term[:, :LANES], turn, 1)
            second = pltpu.roll(term[:, LANES:], turn, 1)
            canvas[p, panel, rows, :] += jnp.where(lane < turn, 0.0, first)
            canvas[p, panel + 1, rows, :] += jnp.where(lane < turn, first, second)
            canvas[p, panel + 2, rows, :] += jnp.where(lane < turn, second, 0.0)

    @pl.loop(0, SIZE // 8)
    def _(i):
        for q in range(PLANES + 1):
            for k in range(2):
                value = sums[q, pl.ds(pl.multiple_of(i * 8, 8), 8), k * LANES : (k + 1) * LANES]
                units[k * 64 + 2 * i, q] = value[0:4]
                units[k * 64 + 2 * i + 1, q] = value[4:8]


def exchange_sums(
    canvas, units, probe, got_v, got_h, got_c, update, peak,
    low_v, low_h, low_c, pair, half, from_x, quarter, from_col,
    send, recv, pair_send, pair_recv, x_send, x_recv, col_send, col_recv,
):
    row, col = lax.axis_index("row"), lax.axis_index("col")
    x, core = row // 2, lax.rem(row, 2)
    sibling = (row + 1 - 2 * core, col)
    x_peers = [(lax.rem(row + 2 * j, N_ROW), col) for j in (1, 2, 3)]
    col_peers = [(row, lax.rem(col + j, N_COL)) for j in range(1, N_COL)]
    tiles = around(row, col)
    others = jnp.where(core == 0, tiles[0][0], tiles[1][0])
    barrier = greet([sibling, (others, col)] + tiles[4:] + x_peers + col_peers)
    pl.semaphore_wait(barrier, 2 + 4 + 3 + N_COL - 1)

    mine = core * 64
    to_pair = remote(units.at[pl.ds(64 - mine, 64)], pair, pair_send.at[0], pair_recv.at[0], sibling)
    to_pair.start()

    @pl.loop(0, TILE // HALF)
    def _(i):
        rows = pl.ds(pl.multiple_of(i * HALF, HALF), HALF)
        at = pl.ds(pl.multiple_of(i * HALF + HALF, HALF), HALF)
        for p in range(2):
            low_h[0, p, rows, :] = canvas[p, 0, at, :].astype(BF16)
            low_h[1, p, rows, :] = canvas[p, PANELS + 1, at, :].astype(BF16)

    for p in range(2):
        for corner in range(4):
            at = slice(0, HALF) if corner < 2 else slice(EXT - HALF, EXT)
            low_c[corner, p] = canvas[p, (corner % 2) * (PANELS + 1), at, :].astype(BF16)
        for k in range(PANELS):
            low_v[0, p, k] = canvas[p, k + 1, 0:HALF, :].astype(BF16)
            low_v[1, p, k] = canvas[p, k + 1, EXT - HALF :, :].astype(BF16)
    rims = rim_copies(
        [low_v.at[0], low_v.at[1], low_h.at[0], low_h.at[1]] + [low_c.at[i] for i in range(4)],
        [got_v.at[0], got_v.at[1], got_h.at[0], got_h.at[1]] + [got_c.at[i] for i in range(4)],
        send,
        recv,
        row,
        col,
    )
    for i in (2, 3, 4, 5, 6, 7, 0, 1):
        rims[i].start()
    squares = probe[0, 0] * probe[0, 0] + probe[0, 1] * probe[0, 1]
    squares = squares + probe[1, 0] * probe[1, 0] + probe[1, 1] * probe[1, 1]
    peak[...] = jnp.broadcast_to(jnp.max(squares, keepdims=True) + 1e-06, peak.shape)

    to_pair.wait()

    @pl.loop(0, 64)
    def _(i):
        half[i] = units[mine + i] + pair[i]

    to_x = [
        remote(half.at[pl.ds(16 * (peer[0] // 2), 16)], from_x.at[j], x_send.at[j], x_recv.at[j], peer)
        for j, peer in enumerate(x_peers)
    ]
    for copy in to_x:
        copy.start()
    for copy in to_x:
        copy.wait()

    @pl.loop(0, 16)
    def _(i):
        quarter[i] = half[16 * x + i] + from_x[0, i] + from_x[1, i] + from_x[2, i]

    to_col = [
        remote(quarter.at[peer[1]], from_col.at[j], col_send.at[j], col_recv.at[j], peer)
        for j, peer in enumerate(col_peers)
    ]
    for copy in to_col:
        copy.start()
    for copy in to_col:
        copy.wait()
    total = quarter[col]
    for j in range(N_COL - 1):
        total = total + from_col[j]
    spread = lax.rsqrt(total[PLANES])
    fresh = jnp.concatenate([total[q] * spread for q in range(PLANES)], 0).astype(BF16)
    unit = mine + 16 * x + col
    update[unit] = fresh
    to_col = [
        remote(update.at[unit], update.at[unit], col_send.at[N_COL - 1 + j], col_recv.at[N_COL - 1 + j], peer)
        for j, peer in enumerate(col_peers)
    ]
    for copy in to_col:
        copy.start()
    for copy in to_col:
        copy.wait()
    block = update.at[pl.ds(mine + 16 * x, 16)]
    to_x = [remote(block, block, x_send.at[3 + j], x_recv.at[3 + j], peer) for j, peer in enumerate(x_peers)]
    for copy in to_x:
        copy.start()
    for copy in to_x:
        copy.wait()
    block = update.at[pl.ds(mine, 64)]
    to_pair = remote(block, block, pair_send.at[1], pair_recv.at[1], sibling)
    to_pair.start()
    to_pair.wait()
    for copy in rims:
        copy.wait()


def write_results(canvas, held, got_v, got_h, got_c, update, peak, probe, new_object, new_probe, stage, store):
    row, col = lax.axis_index("row"), lax.axis_index("col")
    have = inside(row, col)
    scale = 1.0 / peak[0:1, :]

    def keep(i, value):
        return jnp.where(have[i], value.astype(F32), 0.0)

    stores = []
    for k in range(PANELS):
        for p in range(2):
            side = None if k not in (0, PANELS - 1) else (0 if k == 0 else 1)
            for i in range(TILE // HALF):
                rows = slice(i * HALF, (i + 1) * HALF)
                value = canvas[p, k + 1, HALF + i * HALF : 2 * HALF + i * HALF, :]
                if i == 0:
                    value = value + keep(0, got_v[0, p, k])
                if i == TILE // HALF - 1:
                    value = value + keep(1, got_v[1, p, k])
                if side is not None:
                    value = value + keep(2 + side, got_h[side, p, rows, :])
                    if i == 0:
                        value = value + keep(4 + side, got_c[side, p])
                    if i == TILE // HALF - 1:
                        value = value + keep(6 + side, got_c[2 + side, p])
                stage[p, k, rows, :] = held[p, k, rows, :] + value * scale
        copy = pltpu.make_async_copy(stage.at[:, k], new_object.at[:, :, k * LANES : (k + 1) * LANES], store.at[k])
        copy.start()
        stores.append(copy)

    @pl.loop(0, SIZE // 8)
    def _(i):
        rows = pl.ds(pl.multiple_of(i * 8, 8), 8)
        for k in range(2):
            lanes = slice(k * LANES, (k + 1) * LANES)
            first = update[k * 64 + 2 * i].astype(F32)
            second = update[k * 64 + 2 * i + 1].astype(F32)
            for q in range(PLANES):
                value = jnp.concatenate([first[4 * q : 4 * q + 4], second[4 * q : 4 * q + 4]], 0)
                new_probe[q // 2, q % 2, rows, lanes] = probe[q // 2, q % 2, rows, lanes] + value

    for copy in stores:
        copy.wait()


def on_device(object_field, probe_modes, counts, centers, patterns):
    positive, negative = dft_tables()
    dma = pltpu.SemaphoreType.DMA
    probe = pltpu.with_memory_space_constraint(probe_modes, pltpu.VMEM)
    amplitudes = pltpu.with_memory_space_constraint(patterns[0, 0], pltpu.VMEM)
    positive = pltpu.with_memory_space_constraint(jnp.asarray(positive), pltpu.VMEM)
    negative = pltpu.with_memory_space_constraint(jnp.asarray(negative), pltpu.VMEM)
    strips = [
        pltpu.VMEM((2, 2, PANELS, HALF, LANES), BF16),
        pltpu.VMEM((2, 2, TILE, LANES), BF16),
        pltpu.VMEM((4, 2, HALF, LANES), BF16),
    ]

    def inner(*arrays):
        return [pltpu.with_memory_space_constraint(a, pltpu.VMEM) for a in arrays]

    wide, held = pl.pallas_call(
        exchange_object,
        out_shape=[pltpu.VMEM((2, PANELS + 2, EXT, LANES), F32), pltpu.VMEM((2, PANELS, TILE, LANES), F32)],
        in_specs=[ANY],
        out_specs=[VMEM, VMEM],
        scratch_shapes=strips[:2] + strips + [dma((PANELS,)), dma((8,)), dma((8,))],
        compiler_params=pltpu.CompilerParams(collective_id=0, has_side_effects=True, vmem_limit_bytes=LIMIT),
        name="exchange_object",
    )(object_field)
    wide, held = inner(wide, held)
    units, canvas = pl.pallas_call(
        process_slots,
        out_shape=[pltpu.VMEM((UNITS, PLANES + 1, 4, LANES), F32), pltpu.VMEM((2, PANELS + 2, EXT, LANES), F32)],
        in_specs=[SMEM, SMEM, VMEM, VMEM, VMEM, VMEM, VMEM],
        out_specs=[VMEM, VMEM],
        scratch_shapes=[
            pltpu.VMEM((MODES, 2, SIZE, SIZE), F32),
            pltpu.VMEM((PLANES + 1, SIZE, SIZE), F32),
            pltpu.VMEM((2, SIZE, SIZE), F32),
            pltpu.VMEM((MODES, SIZE, 2 * SIZE), BF16),
            pltpu.VMEM((MODES, 2 * SIZE, SIZE), BF16),
            pltpu.VMEM((MODES, SIZE, 2 * SIZE), BF16),
            pltpu.VMEM((MODES, 2 * SIZE, SIZE), BF16),
        ],
        compiler_params=pltpu.CompilerParams(vmem_limit_bytes=LIMIT),
        name="process_slots",
    )(counts, centers[0, 0], wide, probe, amplitudes, positive, negative)
    units, canvas = inner(units, canvas)
    got_v, got_h, got_c, update, peak = pl.pallas_call(
        exchange_sums,
        out_shape=strips + [pltpu.VMEM((UNITS, 16, LANES), BF16), pltpu.VMEM((8, LANES), F32)],
        in_specs=[VMEM] * 3,
        out_specs=[VMEM] * 5,
        scratch_shapes=strips
        + [
            pltpu.VMEM((64, PLANES + 1, 4, LANES), F32),
            pltpu.VMEM((64, PLANES + 1, 4, LANES), F32),
            pltpu.VMEM((3, 16, PLANES + 1, 4, LANES), F32),
            pltpu.VMEM((16, PLANES + 1, 4, LANES), F32),
            pltpu.VMEM((N_COL - 1, PLANES + 1, 4, LANES), F32),
            dma((8,)), dma((8,)), dma((2,)), dma((2,)), dma((6,)), dma((6,)), dma((2 * N_COL - 2,)), dma((2 * N_COL - 2,)),
        ],
        compiler_params=pltpu.CompilerParams(collective_id=1, has_side_effects=True, vmem_limit_bytes=LIMIT),
        name="exchange_sums",
    )(canvas, units, probe)
    new_object, new_probe = pl.pallas_call(
        write_results,
        out_shape=[
            jax.ShapeDtypeStruct(object_field.shape, F32),
            jax.ShapeDtypeStruct(probe_modes.shape, F32),
        ],
        in_specs=[VMEM] * 8,
        out_specs=[ANY, VMEM],
        scratch_shapes=[pltpu.VMEM((2, PANELS, TILE, LANES), F32), dma((PANELS,))],
        compiler_params=pltpu.CompilerParams(vmem_limit_bytes=LIMIT),
        name="write_results",
    )(*inner(canvas, held, got_v, got_h, got_c, update, peak), probe)
    return new_object, new_probe


def solution(mesh):
    placed = (
        P(None, "row", "col"),
        P(),
        P(),
        P("row", "col", None, None),
        P("row", "col", None, None, None),
    )
    return jax.shard_map(
        on_device,
        mesh=mesh,
        in_specs=placed,
        out_specs=(P(None, "row", "col"), P()),
        check_vma=False,
    )
```

```python
import functools
import math

import jax
import jax.numpy as jnp
import ml_dtypes
import numpy as np
from jax import lax
from jax.experimental import pallas as pl
from jax.experimental.pallas import tpu as pltpu
from jax.sharding import PartitionSpec as P

MESH = pl.DeviceIdType.MESH
F32, BF16 = jnp.float32, jnp.bfloat16
SIZE, TILE, HALF, LANES = 256, 768, 128, 128
EXT = TILE + 2 * HALF
PANELS = TILE // LANES
MODES = 2
PLANES = 2 * MODES
N_ROW, N_COL = 8, 16
UNITS = 128
VMEM = pl.BlockSpec(memory_space=pltpu.VMEM)
SMEM = pl.BlockSpec(memory_space=pltpu.SMEM)
HBM = pl.BlockSpec(memory_space=pltpu.HBM)
ANY = pl.BlockSpec(memory_space=pl.ANY)
MIB = 2**20


def dft_tables():
    indices = np.arange(SIZE)
    product = indices[:, None] * indices[None, :] % SIZE
    angles = product.astype(np.float32) * np.float32(2.0 * np.pi / SIZE)
    scale = np.float32(1.0 / math.sqrt(SIZE))
    both = np.stack([np.cos(angles) * scale, np.sin(angles) * scale])
    return both.astype(ml_dtypes.bfloat16).astype(np.float32)


def around(row, col):
    up, down = lax.rem(row + N_ROW - 1, N_ROW), lax.rem(row + 1, N_ROW)
    left, right = lax.rem(col + N_COL - 1, N_COL), lax.rem(col + 1, N_COL)
    return [(up, col), (down, col), (row, left), (row, right), (up, left), (up, right), (down, left), (down, right)]


def greet(targets):
    barrier = pltpu.get_barrier_semaphore()
    for target in targets:
        pl.semaphore_signal(barrier, inc=1, device_id=target, device_id_type=MESH)
    return barrier


def remote(src, dst, send, recv, target):
    return pltpu.make_async_remote_copy(
        src_ref=src, dst_ref=dst, send_sem=send, recv_sem=recv, device_id=target, device_id_type=MESH
    )


def inside(row, col):
    up, down, left, right = row > 0, row < N_ROW - 1, col > 0, col < N_COL - 1
    return [up, down, left, right, up & left, up & right, down & left, down & right]


def rim_copies(out, got, send, recv, row, col):
    opposite = (1, 0, 3, 2, 7, 6, 5, 4)
    return [
        remote(out[i], got[opposite[i]], send.at[i], recv.at[opposite[i]], target)
        for i, target in enumerate(around(row, col))
    ]


def exchange_object(
    obj, patterns, waves, wide, held, amplitudes, tables, canvas,
    low_v, low_h, got_v, got_h, got_c, held_waves, load, send, recv,
):
    row, col = lax.axis_index("row"), lax.axis_index("col")
    order = (0, PANELS - 1) + tuple(range(1, PANELS - 1))
    loads = [
        pltpu.make_async_copy(obj.at[:, :, k * LANES : (k + 1) * LANES], held.at[:, k], load.at[k])
        for k in range(PANELS)
    ]
    for k in order:
        loads[k].start()
    fetches = [
        pltpu.make_async_copy(patterns, amplitudes, load.at[PANELS]),
        pltpu.make_async_copy(waves, held_waves, load.at[PANELS + 1]),
    ]
    for fetch in fetches:
        fetch.start()
    barrier = greet(around(row, col))
    rims = rim_copies(
        [low_v.at[0], low_v.at[1], low_h.at[0], low_h.at[1]]
        + [low_h.at[0, :, 0:HALF], low_h.at[1, :, 0:HALF], low_h.at[0, :, TILE - HALF :], low_h.at[1, :, TILE - HALF :]],
        [got_v.at[0], got_v.at[1], got_h.at[0], got_h.at[1]] + [got_c.at[i] for i in range(4)],
        send,
        recv,
        row,
        col,
    )
    for step, k in enumerate(order):
        loads[k].wait()

        @pl.loop(0, TILE // HALF)
        def _(i, k=k):
            rows = pl.ds(pl.multiple_of(i * HALF, HALF), HALF)
            for p in range(2):
                low = held[p, k, rows, :].astype(BF16)
                wide[p, k + 1, pl.ds(pl.multiple_of(i * HALF + HALF, HALF), HALF), :] = low.astype(F32)
                if k == 0:
                    low_h[0, p, rows, :] = low
                if k == PANELS - 1:
                    low_h[1, p, rows, :] = low

        for p in range(2):
            low_v[0, p, k] = held[p, k, 0:HALF, :].astype(BF16)
            low_v[1, p, k] = held[p, k, TILE - HALF :, :].astype(BF16)
        if step == 1:
            pl.semaphore_wait(barrier, 8)
            for i in (2, 3, 4, 5, 6, 7):
                rims[i].start()
    for i in (0, 1):
        rims[i].start()
    have = inside(row, col)

    def keep(i, value):
        return jnp.where(have[i], value.astype(F32), 0.0)

    @pl.loop(0, EXT // 32)
    def _(i):
        rows = pl.ds(pl.multiple_of(i * 32, 32), 32)
        for p in range(2):
            for k in range(PANELS + 2):
                canvas[p, k, rows, :] = jnp.zeros((32, LANES), F32)

    for fetch in fetches:
        fetch.wait()
    real, imag = slice(0, SIZE), slice(SIZE, 2 * SIZE)
    cosine, sine = held_waves[0].astype(BF16), held_waves[1].astype(BF16)
    minus = (-held_waves[1]).astype(BF16)
    for t in range(2):
        tables[t, real, real] = cosine
        tables[t, imag, imag] = cosine
        tables[t, real, imag] = sine if t else minus
        tables[t, imag, real] = minus if t else sine

    for i in (0, 1, 4, 5, 6, 7, 2, 3):
        rims[i].wait()
    for p in range(2):
        for k in range(PANELS):
            wide[p, k + 1, 0:HALF, :] = keep(0, got_v[0, p, k])
            wide[p, k + 1, EXT - HALF :, :] = keep(1, got_v[1, p, k])
        for corner in range(4):
            rows = slice(0, HALF) if corner < 2 else slice(EXT - HALF, EXT)
            wide[p, (corner % 2) * (PANELS + 1), rows, :] = keep(4 + corner, got_c[corner, p])

    @pl.loop(0, TILE // HALF)
    def _(i):
        rows = pl.ds(pl.multiple_of(i * HALF, HALF), HALF)
        to = pl.ds(pl.multiple_of(i * HALF + HALF, HALF), HALF)
        for p in range(2):
            wide[p, 0, to, :] = keep(2, got_h[0, p, rows, :])
            wide[p, PANELS + 1, to, :] = keep(3, got_h[1, p, rows, :])


def process_slots(counts, centers, wide, probe, patterns, tables, blank, units, canvas, low, sums, patch, wave, half, shift, back):
    row_id, col_id = lax.axis_index("row"), lax.axis_index("col")

    low[...] = probe[...].astype(BF16).astype(F32)
    sums[...] = jnp.zeros_like(sums)
    lane = lax.broadcasted_iota(jnp.int32, (SIZE, LANES), 1)
    real, imag = slice(0, SIZE), slice(SIZE, 2 * SIZE)

    @pl.loop(0, counts[row_id, col_id])
    def _(s):
        row, col = centers[0, s], centers[1, s]
        panel = col // LANES
        turn = col - panel * LANES
        rows = pl.ds(row, SIZE)
        field = []
        for p in range(2):
            parts = [pltpu.roll(wide[p, panel + k, rows, :], lax.rem(LANES - turn, LANES), 1) for k in range(3)]
            whole = jnp.concatenate(
                [jnp.where(lane < LANES - turn, parts[k], parts[k + 1]) for k in range(2)], 1
            )
            patch[p] = whole
            field.append(whole)
        sums[PLANES] += field[0] * field[0] + field[1] * field[1]
        for m in range(MODES):
            wave[m, :, real] = (low[m, 0] * field[0] - low[m, 1] * field[1]).astype(BF16)
            wave[m, :, imag] = (low[m, 0] * field[1] + low[m, 1] * field[0]).astype(BF16)
        for m in range(MODES):
            product = jnp.dot(wave[m], tables[0], preferred_element_type=F32)
            half[m, real, :] = product[:, real].astype(BF16)
            half[m, imag, :] = product[:, imag].astype(BF16)
        spectra = []
        for m in range(MODES):
            spectra.append(
                (
                    jnp.dot(tables[1, real, :], half[m], preferred_element_type=F32),
                    jnp.dot(tables[1, imag, :], half[m], preferred_element_type=F32),
                )
            )
        power = (
            spectra[0][0] * spectra[0][0]
            + spectra[0][1] * spectra[0][1]
            + spectra[1][0] * spectra[1][0]
            + spectra[1][1] * spectra[1][1]
        )
        factor = patterns[s].astype(F32) * lax.rsqrt(jnp.maximum(power, 0.5)) - 1.0
        for m in range(MODES):
            shift[m, :, real] = (factor * spectra[m][0]).astype(BF16)
            shift[m, :, imag] = (factor * spectra[m][1]).astype(BF16)
        for m in range(MODES):
            product = jnp.dot(shift[m], tables[1], preferred_element_type=F32)
            back[m, real, :] = product[:, real].astype(BF16)
            back[m, imag, :] = product[:, imag].astype(BF16)
        terms = [0.0, 0.0]
        for m in range(MODES):
            change_real = jnp.dot(tables[0, real, :], back[m], preferred_element_type=F32)
            change_imag = jnp.dot(tables[0, imag, :], back[m], preferred_element_type=F32)
            terms[0] = terms[0] + low[m, 0] * change_real + low[m, 1] * change_imag
            terms[1] = terms[1] + low[m, 0] * change_imag - low[m, 1] * change_real
            sums[2 * m] += patch[0] * change_real + patch[1] * change_imag
            sums[2 * m + 1] += patch[0] * change_imag - patch[1] * change_real
        for p in range(2):
            term = terms[p].astype(BF16).astype(F32)
            first = pltpu.roll(term[:, :LANES], turn, 1)
            second = pltpu.roll(term[:, LANES:], turn, 1)
            canvas[p, panel, rows, :] += jnp.where(lane < turn, 0.0, first)
            canvas[p, panel + 1, rows, :] += jnp.where(lane < turn, first, second)
            canvas[p, panel + 2, rows, :] += jnp.where(lane < turn, second, 0.0)

    @pl.loop(0, SIZE // 8)
    def _(i):
        for q in range(PLANES + 1):
            for k in range(2):
                value = sums[q, pl.ds(pl.multiple_of(i * 8, 8), 8), k * LANES : (k + 1) * LANES]
                units[k * 64 + 2 * i, q] = value[0:4]
                units[k * 64 + 2 * i + 1, q] = value[4:8]


def exchange_sums(
    canvas, units, probe, got_v, got_h, got_c, update, peak,
    low_v, low_h, low_c, pair, half, from_x, quarter, from_col,
    send, recv, pair_send, pair_recv, x_send, x_recv, col_send, col_recv,
):
    row, col = lax.axis_index("row"), lax.axis_index("col")
    x, core = row // 2, lax.rem(row, 2)
    sibling = (row + 1 - 2 * core, col)
    x_peers = [(lax.rem(row + 2 * j, N_ROW), col) for j in (1, 2, 3)]
    col_peers = [(row, lax.rem(col + j, N_COL)) for j in range(1, N_COL)]
    tiles = around(row, col)
    others = jnp.where(core == 0, tiles[0][0], tiles[1][0])
    barrier = greet([sibling, (others, col)] + tiles[4:] + x_peers + col_peers)
    pl.semaphore_wait(barrier, 2 + 4 + 3 + N_COL - 1)

    mine = core * 64
    to_pair = remote(units.at[pl.ds(64 - mine, 64)], pair, pair_send.at[0], pair_recv.at[0], sibling)
    to_pair.start()

    @pl.loop(0, TILE // HALF)
    def _(i):
        rows = pl.ds(pl.multiple_of(i * HALF, HALF), HALF)
        at = pl.ds(pl.multiple_of(i * HALF + HALF, HALF), HALF)
        for p in range(2):
            low_h[0, p, rows, :] = canvas[p, 0, at, :].astype(BF16)
            low_h[1, p, rows, :] = canvas[p, PANELS + 1, at, :].astype(BF16)

    for p in range(2):
        for corner in range(4):
            at = slice(0, HALF) if corner < 2 else slice(EXT - HALF, EXT)
            low_c[corner, p] = canvas[p, (corner % 2) * (PANELS + 1), at, :].astype(BF16)
        for k in range(PANELS):
            low_v[0, p, k] = canvas[p, k + 1, 0:HALF, :].astype(BF16)
            low_v[1, p, k] = canvas[p, k + 1, EXT - HALF :, :].astype(BF16)
    rims = rim_copies(
        [low_v.at[0], low_v.at[1], low_h.at[0], low_h.at[1]] + [low_c.at[i] for i in range(4)],
        [got_v.at[0], got_v.at[1], got_h.at[0], got_h.at[1]] + [got_c.at[i] for i in range(4)],
        send,
        recv,
        row,
        col,
    )
    for i in (2, 3, 4, 5, 6, 7, 0, 1):
        rims[i].start()
    squares = probe[0, 0] * probe[0, 0] + probe[0, 1] * probe[0, 1]
    squares = squares + probe[1, 0] * probe[1, 0] + probe[1, 1] * probe[1, 1]
    peak[...] = jnp.broadcast_to(jnp.max(squares, keepdims=True) + 1e-06, peak.shape)

    to_pair.wait()

    @pl.loop(0, 64)
    def _(i):
        half[i] = units[mine + i] + pair[i]

    to_x = [
        remote(half.at[pl.ds(16 * (peer[0] // 2), 16)], from_x.at[j], x_send.at[j], x_recv.at[j], peer)
        for j, peer in enumerate(x_peers)
    ]
    for copy in to_x:
        copy.start()
    for copy in to_x:
        copy.wait()

    @pl.loop(0, 16)
    def _(i):
        quarter[i] = half[16 * x + i] + from_x[0, i] + from_x[1, i] + from_x[2, i]

    to_col = [
        remote(quarter.at[peer[1]], from_col.at[j], col_send.at[j], col_recv.at[j], peer)
        for j, peer in enumerate(col_peers)
    ]
    for copy in to_col:
        copy.start()
    for copy in to_col:
        copy.wait()
    total = quarter[col]
    for j in range(N_COL - 1):
        total = total + from_col[j]
    spread = lax.rsqrt(total[PLANES])
    fresh = jnp.concatenate([total[q] * spread for q in range(PLANES)], 0).astype(BF16)
    unit = mine + 16 * x + col
    update[unit] = fresh
    to_col = [
        remote(update.at[unit], update.at[unit], col_send.at[N_COL - 1 + j], col_recv.at[N_COL - 1 + j], peer)
        for j, peer in enumerate(col_peers)
    ]
    for copy in to_col:
        copy.start()
    for copy in to_col:
        copy.wait()
    block = update.at[pl.ds(mine + 16 * x, 16)]
    to_x = [remote(block, block, x_send.at[3 + j], x_recv.at[3 + j], peer) for j, peer in enumerate(x_peers)]
    for copy in to_x:
        copy.start()
    for copy in to_x:
        copy.wait()
    block = update.at[pl.ds(mine, 64)]
    to_pair = remote(block, block, pair_send.at[1], pair_recv.at[1], sibling)
    to_pair.start()
    to_pair.wait()
    for copy in rims:
        copy.wait()


def write_results(canvas, held, got_v, got_h, got_c, update, peak, probe, new_object, new_probe, stage, store):
    row, col = lax.axis_index("row"), lax.axis_index("col")
    have = inside(row, col)
    scale = 1.0 / peak[0:1, :]

    def keep(i, value):
        return jnp.where(have[i], value.astype(F32), 0.0)

    stores = []
    for k in range(PANELS):
        for p in range(2):
            side = None if k not in (0, PANELS - 1) else (0 if k == 0 else 1)
            for i in range(TILE // HALF):
                rows = slice(i * HALF, (i + 1) * HALF)
                value = canvas[p, k + 1, HALF + i * HALF : 2 * HALF + i * HALF, :]
                if i == 0:
                    value = value + keep(0, got_v[0, p, k])
                if i == TILE // HALF - 1:
                    value = value + keep(1, got_v[1, p, k])
                if side is not None:
                    value = value + keep(2 + side, got_h[side, p, rows, :])
                    if i == 0:
                        value = value + keep(4 + side, got_c[side, p])
                    if i == TILE // HALF - 1:
                        value = value + keep(6 + side, got_c[2 + side, p])
                stage[p, k, rows, :] = held[p, k, rows, :] + value * scale
        copy = pltpu.make_async_copy(stage.at[:, k], new_object.at[:, :, k * LANES : (k + 1) * LANES], store.at[k])
        copy.start()
        stores.append(copy)

    @pl.loop(0, SIZE // 8)
    def _(i):
        rows = pl.ds(pl.multiple_of(i * 8, 8), 8)
        for k in range(2):
            lanes = slice(k * LANES, (k + 1) * LANES)
            first = update[k * 64 + 2 * i].astype(F32)
            second = update[k * 64 + 2 * i + 1].astype(F32)
            for q in range(PLANES):
                value = jnp.concatenate([first[4 * q : 4 * q + 4], second[4 * q : 4 * q + 4]], 0)
                new_probe[q // 2, q % 2, rows, lanes] = probe[q // 2, q % 2, rows, lanes] + value

    for copy in stores:
        copy.wait()


def on_device(object_field, probe_modes, counts, centers, patterns):
    waves = pltpu.with_memory_space_constraint(jnp.asarray(dft_tables()), pltpu.HBM)
    dma = pltpu.SemaphoreType.DMA
    probe = pltpu.with_memory_space_constraint(probe_modes, pltpu.VMEM)
    strips = [
        pltpu.VMEM((2, 2, PANELS, HALF, LANES), BF16),
        pltpu.VMEM((2, 2, TILE, LANES), BF16),
        pltpu.VMEM((4, 2, HALF, LANES), BF16),
    ]

    def inner(*arrays):
        return [pltpu.with_memory_space_constraint(a, pltpu.VMEM) for a in arrays]

    extended = pltpu.VMEM((2, PANELS + 2, EXT, LANES), F32)
    wide, held, amplitudes, tables, canvas = pl.pallas_call(
        exchange_object,
        out_shape=[
            extended,
            pltpu.VMEM((2, PANELS, TILE, LANES), F32),
            pltpu.VMEM(patterns.shape[2:], BF16),
            pltpu.VMEM((2, 2 * SIZE, 2 * SIZE), BF16),
            extended,
        ],
        in_specs=[HBM] * 3,
        out_specs=[VMEM] * 5,
        scratch_shapes=strips[:2] + strips + [pltpu.VMEM((2, SIZE, SIZE), F32), dma((PANELS + 2,)), dma((8,)), dma((8,))],
        compiler_params=pltpu.CompilerParams(collective_id=0, has_side_effects=True, vmem_limit_bytes=16 * MIB),
        name="exchange_object",
    )(
        pltpu.with_memory_space_constraint(object_field, pltpu.HBM),
        pltpu.with_memory_space_constraint(patterns[0, 0], pltpu.HBM),
        waves,
    )
    wide, held, amplitudes, tables, canvas = inner(wide, held, amplitudes, tables, canvas)
    units, canvas = pl.pallas_call(
        process_slots,
        out_shape=[pltpu.VMEM((UNITS, PLANES + 1, 4, LANES), F32), extended],
        in_specs=[SMEM, SMEM] + [VMEM] * 5,
        out_specs=[VMEM, VMEM],
        scratch_shapes=[
            pltpu.VMEM((MODES, 2, SIZE, SIZE), F32),
            pltpu.VMEM((PLANES + 1, SIZE, SIZE), F32),
            pltpu.VMEM((2, SIZE, SIZE), F32),
            pltpu.VMEM((MODES, SIZE, 2 * SIZE), BF16),
            pltpu.VMEM((MODES, 2 * SIZE, SIZE), BF16),
            pltpu.VMEM((MODES, SIZE, 2 * SIZE), BF16),
            pltpu.VMEM((MODES, 2 * SIZE, SIZE), BF16),
        ],
        input_output_aliases={6: 1},
        compiler_params=pltpu.CompilerParams(vmem_limit_bytes=24 * MIB),
        name="process_slots",
    )(counts, centers[0, 0], wide, probe, amplitudes, tables, canvas)
    units, canvas = inner(units, canvas)
    got_v, got_h, got_c, update, peak = pl.pallas_call(
        exchange_sums,
        out_shape=strips + [pltpu.VMEM((UNITS, 16, LANES), BF16), pltpu.VMEM((8, LANES), F32)],
        in_specs=[VMEM] * 3,
        out_specs=[VMEM] * 5,
        scratch_shapes=strips
        + [
            pltpu.VMEM((64, PLANES + 1, 4, LANES), F32),
            pltpu.VMEM((64, PLANES + 1, 4, LANES), F32),
            pltpu.VMEM((3, 16, PLANES + 1, 4, LANES), F32),
            pltpu.VMEM((16, PLANES + 1, 4, LANES), F32),
            pltpu.VMEM((N_COL - 1, PLANES + 1, 4, LANES), F32),
            dma((8,)), dma((8,)), dma((2,)), dma((2,)), dma((6,)), dma((6,)), dma((2 * N_COL - 2,)), dma((2 * N_COL - 2,)),
        ],
        compiler_params=pltpu.CompilerParams(collective_id=1, has_side_effects=True, vmem_limit_bytes=16 * MIB),
        name="exchange_sums",
    )(canvas, units, probe)
    new_object, new_probe = pl.pallas_call(
        write_results,
        out_shape=[
            jax.ShapeDtypeStruct(object_field.shape, F32),
            jax.ShapeDtypeStruct(probe_modes.shape, F32),
        ],
        in_specs=[VMEM] * 8,
        out_specs=[ANY, VMEM],
        scratch_shapes=[pltpu.VMEM((2, PANELS, TILE, LANES), F32), dma((PANELS,))],
        compiler_params=pltpu.CompilerParams(vmem_limit_bytes=12 * MIB),
        name="write_results",
    )(*inner(canvas, held, got_v, got_h, got_c, update, peak), probe)
    return new_object, new_probe


def solution(mesh):
    placed = (
        P(None, "row", "col"),
        P(),
        P(),
        P("row", "col", None, None),
        P("row", "col", None, None, None),
    )
    return jax.shard_map(
        on_device,
        mesh=mesh,
        in_specs=placed,
        out_specs=(P(None, "row", "col"), P()),
        check_vma=False,
    )
```

```python
import functools
import math

import jax
import jax.numpy as jnp
import ml_dtypes
import numpy as np
from jax import lax
from jax.experimental import pallas as pl
from jax.experimental.pallas import tpu as pltpu
from jax.sharding import PartitionSpec as P

MESH = pl.DeviceIdType.MESH
F32, BF16 = jnp.float32, jnp.bfloat16
SIZE, TILE, HALF, LANES = 256, 768, 128, 128
EXT = TILE + 2 * HALF
PANELS = TILE // LANES
MODES = 2
PLANES = 2 * MODES
N_ROW, N_COL = 8, 16
UNITS = 128
UNIT_ROWS = 24
BATCH = 2
VMEM = pl.BlockSpec(memory_space=pltpu.VMEM)
SMEM = pl.BlockSpec(memory_space=pltpu.SMEM)
HBM = pl.BlockSpec(memory_space=pltpu.HBM)
ANY = pl.BlockSpec(memory_space=pl.ANY)
MIB = 2**20


def dft_tables():
    indices = np.arange(SIZE)
    product = indices[:, None] * indices[None, :] % SIZE
    angles = product.astype(np.float32) * np.float32(2.0 * np.pi / SIZE)
    scale = np.float32(1.0 / math.sqrt(SIZE))
    both = np.stack([np.cos(angles) * scale, np.sin(angles) * scale])
    return both.astype(ml_dtypes.bfloat16).astype(np.float32)


def around(row, col):
    up, down = lax.rem(row + N_ROW - 1, N_ROW), lax.rem(row + 1, N_ROW)
    left, right = lax.rem(col + N_COL - 1, N_COL), lax.rem(col + 1, N_COL)
    return [(up, col), (down, col), (row, left), (row, right), (up, left), (up, right), (down, left), (down, right)]


def greet(targets):
    barrier = pltpu.get_barrier_semaphore()
    for target in targets:
        pl.semaphore_signal(barrier, inc=1, device_id=target, device_id_type=MESH)
    return barrier


def remote(src, dst, send, recv, target):
    return pltpu.make_async_remote_copy(
        src_ref=src, dst_ref=dst, send_sem=send, recv_sem=recv, device_id=target, device_id_type=MESH
    )


def inside(row, col):
    up, down, left, right = row > 0, row < N_ROW - 1, col > 0, col < N_COL - 1
    return [up, down, left, right, up & left, up & right, down & left, down & right]


def rim_copies(out, got, send, recv, row, col):
    opposite = (1, 0, 3, 2, 7, 6, 5, 4)
    return [
        remote(out[i], got[opposite[i]], send.at[i], recv.at[opposite[i]], target)
        for i, target in enumerate(around(row, col))
    ]


def exchange_object(
    obj, patterns, waves, wide, held, amplitudes, tables, canvas,
    low_v, low_h, got_v, got_h, got_c, held_waves, load, send, recv,
):
    row, col = lax.axis_index("row"), lax.axis_index("col")
    order = (0, PANELS - 1) + tuple(range(1, PANELS - 1))
    loads = [
        pltpu.make_async_copy(obj.at[:, :, k * LANES : (k + 1) * LANES], held.at[:, k], load.at[k])
        for k in range(PANELS)
    ]
    for k in order:
        loads[k].start()
    fetches = [
        pltpu.make_async_copy(patterns, amplitudes, load.at[PANELS]),
        pltpu.make_async_copy(waves, held_waves, load.at[PANELS + 1]),
    ]
    for fetch in fetches:
        fetch.start()
    barrier = greet(around(row, col))
    rims = rim_copies(
        [low_v.at[0], low_v.at[1], low_h.at[0], low_h.at[1]]
        + [low_h.at[0, :, 0:HALF], low_h.at[1, :, 0:HALF], low_h.at[0, :, TILE - HALF :], low_h.at[1, :, TILE - HALF :]],
        [got_v.at[0], got_v.at[1], got_h.at[0], got_h.at[1]] + [got_c.at[i] for i in range(4)],
        send,
        recv,
        row,
        col,
    )
    for step, k in enumerate(order):
        loads[k].wait()

        @pl.loop(0, TILE // HALF)
        def _(i, k=k):
            rows = pl.ds(pl.multiple_of(i * HALF, HALF), HALF)
            for p in range(2):
                low = held[p, k, rows, :].astype(BF16)
                wide[p, k + 1, pl.ds(pl.multiple_of(i * HALF + HALF, HALF), HALF), :] = low.astype(F32)
                if k == 0:
                    low_h[0, p, rows, :] = low
                if k == PANELS - 1:
                    low_h[1, p, rows, :] = low

        for p in range(2):
            low_v[0, p, k] = held[p, k, 0:HALF, :].astype(BF16)
            low_v[1, p, k] = held[p, k, TILE - HALF :, :].astype(BF16)
        if step == 1:
            pl.semaphore_wait(barrier, 8)
            for i in (2, 3, 4, 5, 6, 7):
                rims[i].start()
    for i in (0, 1):
        rims[i].start()
    have = inside(row, col)

    def keep(i, value):
        return jnp.where(have[i], value.astype(F32), 0.0)

    @pl.loop(0, EXT // 32)
    def _(i):
        rows = pl.ds(pl.multiple_of(i * 32, 32), 32)
        for p in range(2):
            for k in range(PANELS + 2):
                canvas[p, k, rows, :] = jnp.zeros((32, LANES), F32)

    for fetch in fetches:
        fetch.wait()
    real, imag = slice(0, SIZE), slice(SIZE, 2 * SIZE)
    cosine, sine = held_waves[0].astype(BF16), held_waves[1].astype(BF16)
    minus = (-held_waves[1]).astype(BF16)
    for t in range(2):
        tables[t, real, real] = cosine
        tables[t, imag, imag] = cosine
        tables[t, real, imag] = sine if t else minus
        tables[t, imag, real] = minus if t else sine

    for i in (0, 1, 4, 5, 6, 7, 2, 3):
        rims[i].wait()
    for p in range(2):
        for k in range(PANELS):
            wide[p, k + 1, 0:HALF, :] = keep(0, got_v[0, p, k])
            wide[p, k + 1, EXT - HALF :, :] = keep(1, got_v[1, p, k])
        for corner in range(4):
            rows = slice(0, HALF) if corner < 2 else slice(EXT - HALF, EXT)
            wide[p, (corner % 2) * (PANELS + 1), rows, :] = keep(4 + corner, got_c[corner, p])

    @pl.loop(0, TILE // HALF)
    def _(i):
        rows = pl.ds(pl.multiple_of(i * HALF, HALF), HALF)
        to = pl.ds(pl.multiple_of(i * HALF + HALF, HALF), HALF)
        for p in range(2):
            wide[p, 0, to, :] = keep(2, got_h[0, p, rows, :])
            wide[p, PANELS + 1, to, :] = keep(3, got_h[1, p, rows, :])


def transform_slots(slots, low, wide, patterns, tables, sums, patch, wave, half, shift, back):
    lane = lax.broadcasted_iota(jnp.int32, (SIZE, LANES), 1)
    real, imag = slice(0, SIZE), slice(SIZE, 2 * SIZE)
    covered = 0.0
    for b, (row, col, s, weight) in enumerate(slots):
        panel = col // LANES
        turn = col - panel * LANES
        rows = pl.ds(row, SIZE)
        field = []
        for p in range(2):
            parts = [pltpu.roll(wide[p, panel + k, rows, :], lax.rem(LANES - turn, LANES), 1) for k in range(3)]
            whole = jnp.concatenate([jnp.where(lane < LANES - turn, parts[k], parts[k + 1]) for k in range(2)], 1)
            patch[b, p] = whole
            field.append(whole)
        covered = covered + weight * (field[0] * field[0] + field[1] * field[1])
        for m in range(MODES):
            wave[b, m, :, real] = (low[m, 0] * field[0] - low[m, 1] * field[1]).astype(BF16)
            wave[b, m, :, imag] = (low[m, 0] * field[1] + low[m, 1] * field[0]).astype(BF16)
    sums[PLANES] += covered
    for b in range(len(slots)):
        for m in range(MODES):
            product = jnp.dot(wave[b, m], tables[0], preferred_element_type=F32)
            half[b, m, real, :] = product[:, real].astype(BF16)
            half[b, m, imag, :] = product[:, imag].astype(BF16)
    for b, (_, _, s, weight) in enumerate(slots):
        spectra = [
            [jnp.dot(tables[1, part, :], half[b, m], preferred_element_type=F32) for part in (real, imag)]
            for m in range(MODES)
        ]
        power = (
            spectra[0][0] * spectra[0][0]
            + spectra[0][1] * spectra[0][1]
            + spectra[1][0] * spectra[1][0]
            + spectra[1][1] * spectra[1][1]
        )
        factor = weight * (patterns[s].astype(F32) * lax.rsqrt(jnp.maximum(power, 0.5)) - 1.0)
        for m in range(MODES):
            shift[b, m, :, real] = (factor * spectra[m][0]).astype(BF16)
            shift[b, m, :, imag] = (factor * spectra[m][1]).astype(BF16)
    for b in range(len(slots)):
        for m in range(MODES):
            product = jnp.dot(shift[b, m], tables[1], preferred_element_type=F32)
            back[b, m, real, :] = product[:, real].astype(BF16)
            back[b, m, imag, :] = product[:, imag].astype(BF16)
    terms = [[0.0, 0.0] for _ in slots]
    for m in range(MODES):
        gained = [0.0, 0.0]
        for b in range(len(slots)):
            change_real = jnp.dot(tables[0, real, :], back[b, m], preferred_element_type=F32)
            change_imag = jnp.dot(tables[0, imag, :], back[b, m], preferred_element_type=F32)
            terms[b][0] = terms[b][0] + low[m, 0] * change_real + low[m, 1] * change_imag
            terms[b][1] = terms[b][1] + low[m, 0] * change_imag - low[m, 1] * change_real
            gained[0] = gained[0] + patch[b, 0] * change_real + patch[b, 1] * change_imag
            gained[1] = gained[1] + patch[b, 0] * change_imag - patch[b, 1] * change_real
        sums[2 * m] += gained[0]
        sums[2 * m + 1] += gained[1]
    return terms


def place_term(canvas, row, col, term):
    lane = lax.broadcasted_iota(jnp.int32, (SIZE, LANES), 1)
    panel = col // LANES
    turn = col - panel * LANES
    rows = pl.ds(row, SIZE)
    for p in range(2):
        rounded = term[p].astype(BF16).astype(F32)
        first = pltpu.roll(rounded[:, :LANES], turn, 1)
        second = pltpu.roll(rounded[:, LANES:], turn, 1)
        canvas[p, panel, rows, :] += jnp.where(lane < turn, 0.0, first)
        canvas[p, panel + 1, rows, :] += jnp.where(lane < turn, first, second)
        canvas[p, panel + 2, rows, :] += jnp.where(lane < turn, second, 0.0)


def process_slots(counts, centers, wide, probe, patterns, tables, blank, units, canvas, low, sums, patch, wave, half, shift, back):
    count = counts[lax.axis_index("row"), lax.axis_index("col")]
    low[...] = probe[...].astype(BF16).astype(F32)
    sums[...] = jnp.zeros_like(sums)

    @pl.loop(0, (count + BATCH - 1) // BATCH)
    def _(i):
        slots = []
        for b in range(BATCH):
            s = jnp.minimum(BATCH * i + b, count - 1)
            weight = jnp.where(BATCH * i + b < count, 1.0, 0.0).astype(F32)
            slots.append((centers[0, s], centers[1, s], s, weight))
        terms = transform_slots(slots, low, wide, patterns, tables, sums, patch, wave, half, shift, back)
        for (row, col, _, _), term in zip(slots, terms):
            place_term(canvas, row, col, term)

    for k in range(2):
        for q in range(PLANES + 1):

            @pl.loop(0, SIZE // 8)
            def _(i, k=k, q=q):
                value = sums[q, pl.ds(pl.multiple_of(i * 8, 8), 8), k * LANES : (k + 1) * LANES]
                units[k * 64 + 2 * i, 4 * q : 4 * q + 4] = value[0:4]
                units[k * 64 + 2 * i + 1, 4 * q : 4 * q + 4] = value[4:8]

    units[:, 4 * PLANES + 4 :, :] = jnp.zeros((UNITS, UNIT_ROWS - 4 * PLANES - 4, LANES), F32)


def exchange_sums(
    canvas, units, probe, got_v, got_h, got_c, update, peak,
    low_v, low_h, low_c, pair, half, from_all,
    send, recv, pair_send, pair_recv, in_send, in_recv, out_send, out_recv,
):
    row, col = lax.axis_index("row"), lax.axis_index("col")
    x, core, z, y = row // 2, lax.rem(row, 2), col // 4, lax.rem(col, 4)
    sibling = (row + 1 - 2 * core, col)
    tiles = around(row, col)
    other = jnp.where(core == 0, tiles[0][0], tiles[1][0])
    along_x = [lax.rem(x + d, 4) for d in range(4)]
    along_z = [4 * lax.rem(z + d, 4) for d in range(4)]
    along_y = [lax.rem(y + d, 4) for d in range(4)]
    cols = [along_z[d // 4] + along_y[d % 4] for d in range(16)]
    peers = [((2 * along_x[j // 16] + core, cols[j % 16]), 16 * along_x[j // 16] + cols[j % 16]) for j in range(64)]
    hops = (0, 1, 2, 1)
    order = sorted(range(1, 64), key=lambda j: -(hops[j // 16] + hops[j // 4 % 4] + hops[j % 4]))
    barrier = greet([sibling, (other, col)] + tiles[4:] + [peers[j][0] for j in order])
    pl.semaphore_wait(barrier, 6 + len(order))

    mine = core * 64
    me = 16 * x + col
    to_pair = remote(units.at[pl.ds(64 - mine, 64)], pair, pair_send.at[0], pair_recv.at[0], sibling)
    to_pair.start()

    @pl.loop(0, TILE // HALF)
    def _(i):
        rows = pl.ds(pl.multiple_of(i * HALF, HALF), HALF)
        at = pl.ds(pl.multiple_of(i * HALF + HALF, HALF), HALF)
        for p in range(2):
            low_h[0, p, rows, :] = canvas[p, 0, at, :].astype(BF16)
            low_h[1, p, rows, :] = canvas[p, PANELS + 1, at, :].astype(BF16)

    for p in range(2):
        for corner in range(4):
            at = slice(0, HALF) if corner < 2 else slice(EXT - HALF, EXT)
            low_c[corner, p] = canvas[p, (corner % 2) * (PANELS + 1), at, :].astype(BF16)
        for k in range(PANELS):
            low_v[0, p, k] = canvas[p, k + 1, 0:HALF, :].astype(BF16)
            low_v[1, p, k] = canvas[p, k + 1, EXT - HALF :, :].astype(BF16)
    rims = rim_copies(
        [low_v.at[0], low_v.at[1], low_h.at[0], low_h.at[1]] + [low_c.at[i] for i in range(4)],
        [got_v.at[0], got_v.at[1], got_h.at[0], got_h.at[1]] + [got_c.at[i] for i in range(4)],
        send,
        recv,
        row,
        col,
    )
    squares = probe[0, 0] * probe[0, 0] + probe[0, 1] * probe[0, 1]
    squares = squares + probe[1, 0] * probe[1, 0] + probe[1, 1] * probe[1, 1]
    peak[...] = jnp.broadcast_to(jnp.max(squares, keepdims=True) + 1e-06, peak.shape)

    to_pair.wait()

    @pl.loop(0, 16)
    def _(i):
        for k in range(4):
            half[4 * i + k] = (units[mine + 4 * i + k] + pair[4 * i + k]).astype(BF16)

    inward = {
        j: remote(half.at[peers[j][1]], from_all.at[j], in_send.at[j], in_recv.at[j], peers[j][0]) for j in order
    }
    for j in order:
        inward[j].start()
    for i in (2, 3, 4, 5, 6, 7, 0, 1):
        rims[i].start()
    from_all[0] = half[me]
    for j in reversed(order):
        inward[j].wait()

    def add(i, total):
        for k in range(8):
            total = total + from_all[8 * i + k].astype(F32)
        return total

    total = lax.fori_loop(0, 8, add, jnp.zeros((UNIT_ROWS, LANES), F32))
    spread = lax.rsqrt(total[4 * PLANES : 4 * PLANES + 4])
    unit = mine + me
    update[unit] = (total[0 : 4 * PLANES] * jnp.concatenate([spread] * PLANES, 0)).astype(BF16)
    outward = {j: remote(update.at[unit], update.at[unit], out_send.at[j], out_recv.at[j], peers[j][0]) for j in order}
    for j in order:
        outward[j].start()
    for j in reversed(order):
        outward[j].wait()
    block = update.at[pl.ds(mine, 64)]
    to_pair = remote(block, block, pair_send.at[1], pair_recv.at[1], sibling)
    to_pair.start()
    to_pair.wait()
    for copy in rims:
        copy.wait()


def write_results(canvas, held, got_v, got_h, got_c, update, peak, probe, new_object, new_probe, stage, store):
    row, col = lax.axis_index("row"), lax.axis_index("col")
    have = inside(row, col)
    scale = 1.0 / peak[0:1, :]

    def keep(i, value):
        return jnp.where(have[i], value.astype(F32), 0.0)

    stores = []
    for k in range(PANELS):
        for p in range(2):
            side = None if k not in (0, PANELS - 1) else (0 if k == 0 else 1)
            for i in range(TILE // HALF):
                rows = slice(i * HALF, (i + 1) * HALF)
                value = canvas[p, k + 1, HALF + i * HALF : 2 * HALF + i * HALF, :]
                if i == 0:
                    value = value + keep(0, got_v[0, p, k])
                if i == TILE // HALF - 1:
                    value = value + keep(1, got_v[1, p, k])
                if side is not None:
                    value = value + keep(2 + side, got_h[side, p, rows, :])
                    if i == 0:
                        value = value + keep(4 + side, got_c[side, p])
                    if i == TILE // HALF - 1:
                        value = value + keep(6 + side, got_c[2 + side, p])
                stage[p, k, rows, :] = held[p, k, rows, :] + value * scale
        copy = pltpu.make_async_copy(stage.at[:, k], new_object.at[:, :, k * LANES : (k + 1) * LANES], store.at[k])
        copy.start()
        stores.append(copy)

    @pl.loop(0, SIZE // 8)
    def _(i):
        rows = pl.ds(pl.multiple_of(i * 8, 8), 8)
        for k in range(2):
            lanes = slice(k * LANES, (k + 1) * LANES)
            first = update[k * 64 + 2 * i].astype(F32)
            second = update[k * 64 + 2 * i + 1].astype(F32)
            for q in range(PLANES):
                value = jnp.concatenate([first[4 * q : 4 * q + 4], second[4 * q : 4 * q + 4]], 0)
                new_probe[q // 2, q % 2, rows, lanes] = probe[q // 2, q % 2, rows, lanes] + value

    for copy in stores:
        copy.wait()


def on_device(object_field, probe_modes, counts, centers, patterns):
    waves = pltpu.with_memory_space_constraint(jnp.asarray(dft_tables()), pltpu.HBM)
    dma = pltpu.SemaphoreType.DMA
    probe = pltpu.with_memory_space_constraint(probe_modes, pltpu.VMEM)
    strips = [
        pltpu.VMEM((2, 2, PANELS, HALF, LANES), BF16),
        pltpu.VMEM((2, 2, TILE, LANES), BF16),
        pltpu.VMEM((4, 2, HALF, LANES), BF16),
    ]

    def inner(*arrays):
        return [pltpu.with_memory_space_constraint(a, pltpu.VMEM) for a in arrays]

    extended = pltpu.VMEM((2, PANELS + 2, EXT, LANES), F32)
    wide, held, amplitudes, tables, canvas = pl.pallas_call(
        exchange_object,
        out_shape=[
            extended,
            pltpu.VMEM((2, PANELS, TILE, LANES), F32),
            pltpu.VMEM(patterns.shape[2:], BF16),
            pltpu.VMEM((2, 2 * SIZE, 2 * SIZE), BF16),
            extended,
        ],
        in_specs=[HBM] * 3,
        out_specs=[VMEM] * 5,
        scratch_shapes=strips[:2] + strips + [pltpu.VMEM((2, SIZE, SIZE), F32), dma((PANELS + 2,)), dma((8,)), dma((8,))],
        compiler_params=pltpu.CompilerParams(collective_id=0, has_side_effects=True, vmem_limit_bytes=16 * MIB),
        name="exchange_object",
    )(
        pltpu.with_memory_space_constraint(object_field, pltpu.HBM),
        pltpu.with_memory_space_constraint(patterns[0, 0], pltpu.HBM),
        waves,
    )
    wide, held, amplitudes, tables, canvas = inner(wide, held, amplitudes, tables, canvas)
    units, canvas = pl.pallas_call(
        process_slots,
        out_shape=[pltpu.VMEM((UNITS, UNIT_ROWS, LANES), F32), extended],
        in_specs=[SMEM, SMEM] + [VMEM] * 5,
        out_specs=[VMEM, VMEM],
        scratch_shapes=[
            pltpu.VMEM((MODES, 2, SIZE, SIZE), F32),
            pltpu.VMEM((PLANES + 1, SIZE, SIZE), F32),
            pltpu.VMEM((BATCH, 2, SIZE, SIZE), F32),
            pltpu.VMEM((BATCH, MODES, SIZE, 2 * SIZE), BF16),
            pltpu.VMEM((BATCH, MODES, 2 * SIZE, SIZE), BF16),
            pltpu.VMEM((BATCH, MODES, SIZE, 2 * SIZE), BF16),
            pltpu.VMEM((BATCH, MODES, 2 * SIZE, SIZE), BF16),
        ],
        input_output_aliases={6: 1},
        compiler_params=pltpu.CompilerParams(vmem_limit_bytes=24 * MIB),
        name="process_slots",
    )(counts, centers[0, 0], wide, probe, amplitudes, tables, canvas)
    units, canvas = inner(units, canvas)
    got_v, got_h, got_c, update, peak = pl.pallas_call(
        exchange_sums,
        out_shape=strips + [pltpu.VMEM((UNITS, 16, LANES), BF16), pltpu.VMEM((8, LANES), F32)],
        in_specs=[VMEM] * 3,
        out_specs=[VMEM] * 5,
        scratch_shapes=strips
        + [
            pltpu.VMEM((64, UNIT_ROWS, LANES), F32),
            pltpu.VMEM((64, UNIT_ROWS, LANES), BF16),
            pltpu.VMEM((64, UNIT_ROWS, LANES), BF16),
            dma((8,)), dma((8,)), dma((2,)), dma((2,)), dma((64,)), dma((64,)), dma((64,)), dma((64,)),
        ],
        compiler_params=pltpu.CompilerParams(collective_id=1, has_side_effects=True, vmem_limit_bytes=16 * MIB),
        name="exchange_sums",
    )(canvas, units, probe)
    new_object, new_probe = pl.pallas_call(
        write_results,
        out_shape=[
            jax.ShapeDtypeStruct(object_field.shape, F32),
            jax.ShapeDtypeStruct(probe_modes.shape, F32),
        ],
        in_specs=[VMEM] * 8,
        out_specs=[ANY, VMEM],
        scratch_shapes=[pltpu.VMEM((2, PANELS, TILE, LANES), F32), dma((PANELS,))],
        compiler_params=pltpu.CompilerParams(vmem_limit_bytes=12 * MIB),
        name="write_results",
    )(*inner(canvas, held, got_v, got_h, got_c, update, peak), probe)
    return new_object, new_probe


def solution(mesh):
    placed = (
        P(None, "row", "col"),
        P(),
        P(),
        P("row", "col", None, None),
        P("row", "col", None, None, None),
    )
    return jax.shard_map(
        on_device,
        mesh=mesh,
        in_specs=placed,
        out_specs=(P(None, "row", "col"), P()),
        check_vma=False,
    )
```

```python
import functools
import math

import jax
import jax.numpy as jnp
import ml_dtypes
import numpy as np
from jax import lax
from jax.experimental import pallas as pl
from jax.experimental.pallas import tpu as pltpu
from jax.sharding import PartitionSpec as P

MESH = pl.DeviceIdType.MESH
F32, BF16 = jnp.float32, jnp.bfloat16
SIZE, TILE, HALF, LANES = 256, 768, 128, 128
EXT = TILE + 2 * HALF
PANELS = TILE // LANES
MODES = 2
PLANES = 2 * MODES
N_ROW, N_COL = 8, 16
UNITS = 128
UNIT_ROWS = 24
BATCH = 2
VMEM = pl.BlockSpec(memory_space=pltpu.VMEM)
SMEM = pl.BlockSpec(memory_space=pltpu.SMEM)
HBM = pl.BlockSpec(memory_space=pltpu.HBM)
ANY = pl.BlockSpec(memory_space=pl.ANY)
MIB = 2**20


def dft_tables():
    indices = np.arange(SIZE)
    product = indices[:, None] * indices[None, :] % SIZE
    angles = product.astype(np.float32) * np.float32(2.0 * np.pi / SIZE)
    scale = np.float32(1.0 / math.sqrt(SIZE))
    both = np.stack([np.cos(angles) * scale, np.sin(angles) * scale])
    return both.astype(ml_dtypes.bfloat16).astype(np.float32)


def around(row, col):
    up, down = lax.rem(row + N_ROW - 1, N_ROW), lax.rem(row + 1, N_ROW)
    left, right = lax.rem(col + N_COL - 1, N_COL), lax.rem(col + 1, N_COL)
    return [(up, col), (down, col), (row, left), (row, right), (up, left), (up, right), (down, left), (down, right)]


def greet(targets):
    barrier = pltpu.get_barrier_semaphore()
    for target in targets:
        pl.semaphore_signal(barrier, inc=1, device_id=target, device_id_type=MESH)
    return barrier


def remote(src, dst, send, recv, target):
    return pltpu.make_async_remote_copy(
        src_ref=src, dst_ref=dst, send_sem=send, recv_sem=recv, device_id=target, device_id_type=MESH
    )


def inside(row, col):
    up, down, left, right = row > 0, row < N_ROW - 1, col > 0, col < N_COL - 1
    return [up, down, left, right, up & left, up & right, down & left, down & right]


def rim_copies(out, got, send, recv, row, col):
    opposite = (1, 0, 3, 2, 7, 6, 5, 4)
    return [
        remote(out[i], got[opposite[i]], send.at[i], recv.at[opposite[i]], target)
        for i, target in enumerate(around(row, col))
    ]


def exchange_object(
    obj, patterns, waves, wide, held, amplitudes, tables, canvas,
    low_v, low_h, got_v, got_h, got_c, held_waves, load, send, recv,
):
    row, col = lax.axis_index("row"), lax.axis_index("col")
    order = (0, PANELS - 1) + tuple(range(1, PANELS - 1))
    loads = [
        pltpu.make_async_copy(obj.at[:, :, k * LANES : (k + 1) * LANES], held.at[:, k], load.at[k])
        for k in range(PANELS)
    ]
    for k in order:
        loads[k].start()
    fetches = [
        pltpu.make_async_copy(patterns, amplitudes, load.at[PANELS]),
        pltpu.make_async_copy(waves, held_waves, load.at[PANELS + 1]),
    ]
    for fetch in fetches:
        fetch.start()
    barrier = greet(around(row, col))
    rims = rim_copies(
        [low_v.at[0], low_v.at[1], low_h.at[0], low_h.at[1]]
        + [low_h.at[0, :, 0:HALF], low_h.at[1, :, 0:HALF], low_h.at[0, :, TILE - HALF :], low_h.at[1, :, TILE - HALF :]],
        [got_v.at[0], got_v.at[1], got_h.at[0], got_h.at[1]] + [got_c.at[i] for i in range(4)],
        send,
        recv,
        row,
        col,
    )
    for step, k in enumerate(order):
        loads[k].wait()

        @pl.loop(0, TILE // HALF)
        def _(i, k=k):
            rows = pl.ds(pl.multiple_of(i * HALF, HALF), HALF)
            for p in range(2):
                low = held[p, k, rows, :].astype(BF16)
                wide[p, k + 1, pl.ds(pl.multiple_of(i * HALF + HALF, HALF), HALF), :] = low.astype(F32)
                if k == 0:
                    low_h[0, p, rows, :] = low
                if k == PANELS - 1:
                    low_h[1, p, rows, :] = low

        for p in range(2):
            low_v[0, p, k] = held[p, k, 0:HALF, :].astype(BF16)
            low_v[1, p, k] = held[p, k, TILE - HALF :, :].astype(BF16)
        if step == 1:
            pl.semaphore_wait(barrier, 8)
            for i in (2, 3, 4, 5, 6, 7):
                rims[i].start()
    for i in (0, 1):
        rims[i].start()
    have = inside(row, col)

    def keep(i, value):
        return jnp.where(have[i], value.astype(F32), 0.0)

    @pl.loop(0, EXT // 32)
    def _(i):
        rows = pl.ds(pl.multiple_of(i * 32, 32), 32)
        for p in range(2):
            for k in range(PANELS + 2):
                canvas[p, k, rows, :] = jnp.zeros((32, LANES), F32)

    for fetch in fetches:
        fetch.wait()
    real, imag = slice(0, SIZE), slice(SIZE, 2 * SIZE)
    cosine, sine = held_waves[0].astype(BF16), held_waves[1].astype(BF16)
    minus = (-held_waves[1]).astype(BF16)
    for t in range(2):
        tables[t, real, real] = cosine
        tables[t, imag, imag] = cosine
        tables[t, real, imag] = sine if t else minus
        tables[t, imag, real] = minus if t else sine

    for i in (0, 1, 4, 5, 6, 7, 2, 3):
        rims[i].wait()
    for p in range(2):
        for k in range(PANELS):
            wide[p, k + 1, 0:HALF, :] = keep(0, got_v[0, p, k])
            wide[p, k + 1, EXT - HALF :, :] = keep(1, got_v[1, p, k])
        for corner in range(4):
            rows = slice(0, HALF) if corner < 2 else slice(EXT - HALF, EXT)
            wide[p, (corner % 2) * (PANELS + 1), rows, :] = keep(4 + corner, got_c[corner, p])

    @pl.loop(0, TILE // HALF)
    def _(i):
        rows = pl.ds(pl.multiple_of(i * HALF, HALF), HALF)
        to = pl.ds(pl.multiple_of(i * HALF + HALF, HALF), HALF)
        for p in range(2):
            wide[p, 0, to, :] = keep(2, got_h[0, p, rows, :])
            wide[p, PANELS + 1, to, :] = keep(3, got_h[1, p, rows, :])


def transform_slots(slots, low, wide, patterns, tables, sums, patch, wave, half, shift, back):
    lane = lax.broadcasted_iota(jnp.int32, (SIZE, LANES), 1)
    real, imag = slice(0, SIZE), slice(SIZE, 2 * SIZE)
    covered = 0.0
    for b, (row, col, s, weight) in enumerate(slots):
        panel = col // LANES
        turn = col - panel * LANES
        rows = pl.ds(row, SIZE)
        field = []
        for p in range(2):
            parts = [pltpu.roll(wide[p, panel + k, rows, :], lax.rem(LANES - turn, LANES), 1) for k in range(3)]
            whole = jnp.concatenate([jnp.where(lane < LANES - turn, parts[k], parts[k + 1]) for k in range(2)], 1)
            patch[b, p] = whole
            field.append(whole)
        covered = covered + weight * (field[0] * field[0] + field[1] * field[1])
        for m in range(MODES):
            wave[b, m, :, real] = (low[m, 0] * field[0] - low[m, 1] * field[1]).astype(BF16)
            wave[b, m, :, imag] = (low[m, 0] * field[1] + low[m, 1] * field[0]).astype(BF16)
    for k in range(2):
        sums[PLANES, k] += covered[:, k * LANES : (k + 1) * LANES]
    for b in range(len(slots)):
        for m in range(MODES):
            product = jnp.dot(wave[b, m], tables[0], preferred_element_type=F32)
            half[b, m, real, :] = product[:, real].astype(BF16)
            half[b, m, imag, :] = product[:, imag].astype(BF16)
    for b, (_, _, s, weight) in enumerate(slots):
        spectra = [
            [jnp.dot(tables[1, part, :], half[b, m], preferred_element_type=F32) for part in (real, imag)]
            for m in range(MODES)
        ]
        power = (
            spectra[0][0] * spectra[0][0]
            + spectra[0][1] * spectra[0][1]
            + spectra[1][0] * spectra[1][0]
            + spectra[1][1] * spectra[1][1]
        )
        factor = weight * (patterns[s].astype(F32) * lax.rsqrt(jnp.maximum(power, 0.5)) - 1.0)
        for m in range(MODES):
            shift[b, m, :, real] = (factor * spectra[m][0]).astype(BF16)
            shift[b, m, :, imag] = (factor * spectra[m][1]).astype(BF16)
    for b in range(len(slots)):
        for m in range(MODES):
            product = jnp.dot(shift[b, m], tables[1], preferred_element_type=F32)
            back[b, m, real, :] = product[:, real].astype(BF16)
            back[b, m, imag, :] = product[:, imag].astype(BF16)
    terms = [[0.0, 0.0] for _ in slots]
    for m in range(MODES):
        gained = [0.0, 0.0]
        for b in range(len(slots)):
            change_real = jnp.dot(tables[0, real, :], back[b, m], preferred_element_type=F32)
            change_imag = jnp.dot(tables[0, imag, :], back[b, m], preferred_element_type=F32)
            terms[b][0] = terms[b][0] + low[m, 0] * change_real + low[m, 1] * change_imag
            terms[b][1] = terms[b][1] + low[m, 0] * change_imag - low[m, 1] * change_real
            gained[0] = gained[0] + patch[b, 0] * change_real + patch[b, 1] * change_imag
            gained[1] = gained[1] + patch[b, 0] * change_imag - patch[b, 1] * change_real
        for part in range(2):
            for k in range(2):
                sums[2 * m + part, k] += gained[part][:, k * LANES : (k + 1) * LANES]
    return terms


def place_term(canvas, row, col, term):
    lane = lax.broadcasted_iota(jnp.int32, (SIZE, LANES), 1)
    panel = col // LANES
    turn = col - panel * LANES
    rows = pl.ds(row, SIZE)
    for p in range(2):
        rounded = term[p].astype(BF16).astype(F32)
        first = pltpu.roll(rounded[:, :LANES], turn, 1)
        second = pltpu.roll(rounded[:, LANES:], turn, 1)
        canvas[p, panel, rows, :] += jnp.where(lane < turn, 0.0, first)
        canvas[p, panel + 1, rows, :] += jnp.where(lane < turn, first, second)
        canvas[p, panel + 2, rows, :] += jnp.where(lane < turn, second, 0.0)


def process_slots(counts, centers, wide, probe, patterns, tables, blank, sums, canvas, low, patch, wave, half, shift, back):
    count = counts[lax.axis_index("row"), lax.axis_index("col")]
    low[...] = probe[...].astype(BF16).astype(F32)
    sums[...] = jnp.zeros_like(sums)

    @pl.loop(0, (count + BATCH - 1) // BATCH)
    def _(i):
        slots = []
        for b in range(BATCH):
            s = jnp.minimum(BATCH * i + b, count - 1)
            weight = jnp.where(BATCH * i + b < count, 1.0, 0.0).astype(F32)
            slots.append((centers[0, s], centers[1, s], s, weight))
        terms = transform_slots(slots, low, wide, patterns, tables, sums, patch, wave, half, shift, back)
        for (row, col, _, _), term in zip(slots, terms):
            place_term(canvas, row, col, term)


def exchange_sums(
    canvas, sums, probe, got_v, got_h, got_c, update, peak,
    low_v, low_h, low_c, pair, half, from_plane, share, from_line,
    send, recv, pair_send, pair_recv, in_send, in_recv, out_send, out_recv,
):
    row, col = lax.axis_index("row"), lax.axis_index("col")
    x, core, z, y = row // 2, lax.rem(row, 2), col // 4, lax.rem(col, 4)
    sibling = (row + 1 - 2 * core, col)
    tiles = around(row, col)
    other = jnp.where(core == 0, tiles[0][0], tiles[1][0])
    along_x = [lax.rem(x + d, 4) for d in range(4)]
    along_z = [4 * lax.rem(z + d, 4) for d in range(4)]
    along_y = [lax.rem(y + d, 4) for d in range(4)]
    cols = [along_z[d // 4] + along_y[d % 4] for d in range(16)]
    plane = [((2 * along_x[j // 4] + core, along_z[j % 4] + y), 16 * along_x[j // 4] + along_z[j % 4]) for j in range(16)]
    line = [((row, 4 * z + along_y[j]), along_y[j]) for j in range(4)]
    hops = (0, 1, 2, 1)
    order = sorted(range(1, 16), key=lambda j: -(hops[j // 4] + hops[j % 4]))
    barrier = greet([sibling, (other, col)] + tiles[2:] + [plane[j][0] for j in order] + [line[j][0] for j in (2, 1, 3)])
    pl.semaphore_wait(barrier, 26)

    mine = core * 64
    me = 16 * x + col
    to_pair = remote(sums.at[:, 1 - core], pair, pair_send.at[0], pair_recv.at[0], sibling)
    to_pair.start()

    @pl.loop(0, TILE // HALF)
    def _(i):
        rows = pl.ds(pl.multiple_of(i * HALF, HALF), HALF)
        at = pl.ds(pl.multiple_of(i * HALF + HALF, HALF), HALF)
        for p in range(2):
            low_h[0, p, rows, :] = canvas[p, 0, at, :].astype(BF16)
            low_h[1, p, rows, :] = canvas[p, PANELS + 1, at, :].astype(BF16)

    for p in range(2):
        for corner in range(4):
            at = slice(0, HALF) if corner < 2 else slice(EXT - HALF, EXT)
            low_c[corner, p] = canvas[p, (corner % 2) * (PANELS + 1), at, :].astype(BF16)
        for k in range(PANELS):
            low_v[0, p, k] = canvas[p, k + 1, 0:HALF, :].astype(BF16)
            low_v[1, p, k] = canvas[p, k + 1, EXT - HALF :, :].astype(BF16)
    rims = rim_copies(
        [low_v.at[0], low_v.at[1], low_h.at[0], low_h.at[1]] + [low_c.at[i] for i in range(4)],
        [got_v.at[0], got_v.at[1], got_h.at[0], got_h.at[1]] + [got_c.at[i] for i in range(4)],
        send,
        recv,
        row,
        col,
    )
    squares = probe[0, 0] * probe[0, 0] + probe[0, 1] * probe[0, 1]
    squares = squares + probe[1, 0] * probe[1, 0] + probe[1, 1] * probe[1, 1]
    peak[...] = jnp.broadcast_to(jnp.max(squares, keepdims=True) + 1e-06, peak.shape)

    to_pair.wait()

    for q in range(PLANES + 1):
        half[q] = (sums[q, core] + pair[q]).astype(BF16)

    def rows_of(block):
        return pl.ds(pl.multiple_of(4 * block, 16), 16)

    inward = [
        remote(half.at[:, rows_of(plane[j][1])], from_plane.at[j - 1], in_send.at[j], in_recv.at[j], plane[j][0])
        for j in order
    ]
    for copy in inward:
        copy.start()
    for i in (2, 3, 4, 5, 6, 7, 0, 1):
        rims[i].start()
    for copy in reversed(inward):
        copy.wait()
    parts = []
    for q in range(PLANES + 1):
        total = half[q, rows_of(16 * x + 4 * z), :].astype(F32)
        for j in range(15):
            total = total + from_plane[j, q].astype(F32)
        parts.append(total)
    blank = jnp.zeros((UNIT_ROWS - 4 * PLANES - 4, LANES), F32)
    for k in range(4):
        share[k] = jnp.concatenate([part[4 * k : 4 * k + 4] for part in parts] + [blank], 0).astype(BF16)
    inward = [
        remote(share.at[line[j][1]], from_line.at[j - 1], in_send.at[15 + j], in_recv.at[15 + j], line[j][0])
        for j in (2, 1, 3)
    ]
    for copy in inward:
        copy.start()
    for copy in inward:
        copy.wait()
    total = share[y].astype(F32)
    for j in range(3):
        total = total + from_line[j].astype(F32)
    spread = lax.rsqrt(total[4 * PLANES : 4 * PLANES + 4])
    unit = mine + me
    update[unit] = (total[0 : 4 * PLANES] * jnp.concatenate([spread] * PLANES, 0)).astype(BF16)
    outward = [
        remote(update.at[unit], update.at[unit], out_send.at[15 + j], out_recv.at[15 + j], line[j][0]) for j in (2, 1, 3)
    ]
    for copy in outward:
        copy.start()
    for copy in outward:
        copy.wait()
    block = update.at[pl.ds(mine + 16 * x + 4 * z, 4)]
    outward = {j: remote(block, block, out_send.at[j], out_recv.at[j], plane[j][0]) for j in order}
    for j in order:
        outward[j].start()
    over = []
    for j in [0] + order[::-1]:
        came = 4 * ((4 - j // 4) % 4) + (4 - j % 4) % 4
        block = update.at[pl.ds(mine + plane[came][1], 4)]
        if j:
            outward[j].wait()
        over.append(remote(block, block, pair_send.at[1 + j], pair_recv.at[1 + j], sibling))
        over[-1].start()
    for copy in over:
        copy.wait()
    for copy in rims:
        copy.wait()


def write_results(canvas, held, got_v, got_h, got_c, update, peak, probe, new_object, new_probe, stage, store):
    row, col = lax.axis_index("row"), lax.axis_index("col")
    have = inside(row, col)
    scale = 1.0 / peak[0:1, :]

    def keep(i, value):
        return jnp.where(have[i], value.astype(F32), 0.0)

    stores = []
    for k in range(PANELS):
        for p in range(2):
            side = None if k not in (0, PANELS - 1) else (0 if k == 0 else 1)
            for i in range(TILE // HALF):
                rows = slice(i * HALF, (i + 1) * HALF)
                value = canvas[p, k + 1, HALF + i * HALF : 2 * HALF + i * HALF, :]
                if i == 0:
                    value = value + keep(0, got_v[0, p, k])
                if i == TILE // HALF - 1:
                    value = value + keep(1, got_v[1, p, k])
                if side is not None:
                    value = value + keep(2 + side, got_h[side, p, rows, :])
                    if i == 0:
                        value = value + keep(4 + side, got_c[side, p])
                    if i == TILE // HALF - 1:
                        value = value + keep(6 + side, got_c[2 + side, p])
                stage[p, k, rows, :] = held[p, k, rows, :] + value * scale
        copy = pltpu.make_async_copy(stage.at[:, k], new_object.at[:, :, k * LANES : (k + 1) * LANES], store.at[k])
        copy.start()
        stores.append(copy)

    @pl.loop(0, SIZE // 8)
    def _(i):
        rows = pl.ds(pl.multiple_of(i * 8, 8), 8)
        for k in range(2):
            lanes = slice(k * LANES, (k + 1) * LANES)
            first = update[k * 64 + 2 * i].astype(F32)
            second = update[k * 64 + 2 * i + 1].astype(F32)
            for q in range(PLANES):
                value = jnp.concatenate([first[4 * q : 4 * q + 4], second[4 * q : 4 * q + 4]], 0)
                new_probe[q // 2, q % 2, rows, lanes] = probe[q // 2, q % 2, rows, lanes] + value

    for copy in stores:
        copy.wait()


def on_device(object_field, probe_modes, counts, centers, patterns):
    waves = pltpu.with_memory_space_constraint(jnp.asarray(dft_tables()), pltpu.HBM)
    dma = pltpu.SemaphoreType.DMA
    probe = pltpu.with_memory_space_constraint(probe_modes, pltpu.VMEM)
    strips = [
        pltpu.VMEM((2, 2, PANELS, HALF, LANES), BF16),
        pltpu.VMEM((2, 2, TILE, LANES), BF16),
        pltpu.VMEM((4, 2, HALF, LANES), BF16),
    ]

    def inner(*arrays):
        return [pltpu.with_memory_space_constraint(a, pltpu.VMEM) for a in arrays]

    extended = pltpu.VMEM((2, PANELS + 2, EXT, LANES), F32)
    wide, held, amplitudes, tables, canvas = pl.pallas_call(
        exchange_object,
        out_shape=[
            extended,
            pltpu.VMEM((2, PANELS, TILE, LANES), F32),
            pltpu.VMEM(patterns.shape[2:], BF16),
            pltpu.VMEM((2, 2 * SIZE, 2 * SIZE), BF16),
            extended,
        ],
        in_specs=[HBM] * 3,
        out_specs=[VMEM] * 5,
        scratch_shapes=strips[:2] + strips + [pltpu.VMEM((2, SIZE, SIZE), F32), dma((PANELS + 2,)), dma((8,)), dma((8,))],
        compiler_params=pltpu.CompilerParams(collective_id=0, has_side_effects=True, vmem_limit_bytes=16 * MIB),
        name="exchange_object",
    )(
        pltpu.with_memory_space_constraint(object_field, pltpu.HBM),
        pltpu.with_memory_space_constraint(patterns[0, 0], pltpu.HBM),
        waves,
    )
    wide, held, amplitudes, tables, canvas = inner(wide, held, amplitudes, tables, canvas)
    sums, canvas = pl.pallas_call(
        process_slots,
        out_shape=[pltpu.VMEM((PLANES + 1, 2, SIZE, LANES), F32), extended],
        in_specs=[SMEM, SMEM] + [VMEM] * 5,
        out_specs=[VMEM, VMEM],
        scratch_shapes=[
            pltpu.VMEM((MODES, 2, SIZE, SIZE), F32),
            pltpu.VMEM((BATCH, 2, SIZE, SIZE), F32),
            pltpu.VMEM((BATCH, MODES, SIZE, 2 * SIZE), BF16),
            pltpu.VMEM((BATCH, MODES, 2 * SIZE, SIZE), BF16),
            pltpu.VMEM((BATCH, MODES, SIZE, 2 * SIZE), BF16),
            pltpu.VMEM((BATCH, MODES, 2 * SIZE, SIZE), BF16),
        ],
        input_output_aliases={6: 1},
        compiler_params=pltpu.CompilerParams(vmem_limit_bytes=24 * MIB),
        name="process_slots",
    )(counts, centers[0, 0], wide, probe, amplitudes, tables, canvas)
    sums, canvas = inner(sums, canvas)
    got_v, got_h, got_c, update, peak = pl.pallas_call(
        exchange_sums,
        out_shape=strips + [pltpu.VMEM((UNITS, 16, LANES), BF16), pltpu.VMEM((8, LANES), F32)],
        in_specs=[VMEM] * 3,
        out_specs=[VMEM] * 5,
        scratch_shapes=strips
        + [
            pltpu.VMEM((PLANES + 1, SIZE, LANES), F32),
            pltpu.VMEM((PLANES + 1, SIZE, LANES), BF16),
            pltpu.VMEM((15, PLANES + 1, 16, LANES), BF16),
            pltpu.VMEM((4, UNIT_ROWS, LANES), BF16),
            pltpu.VMEM((3, UNIT_ROWS, LANES), BF16),
            dma((8,)), dma((8,)), dma((17,)), dma((17,)), dma((19,)), dma((19,)), dma((19,)), dma((19,)),
        ],
        compiler_params=pltpu.CompilerParams(collective_id=1, has_side_effects=True, vmem_limit_bytes=16 * MIB),
        name="exchange_sums",
    )(canvas, sums, probe)
    new_object, new_probe = pl.pallas_call(
        write_results,
        out_shape=[
            jax.ShapeDtypeStruct(object_field.shape, F32),
            jax.ShapeDtypeStruct(probe_modes.shape, F32),
        ],
        in_specs=[VMEM] * 8,
        out_specs=[ANY, VMEM],
        scratch_shapes=[pltpu.VMEM((2, PANELS, TILE, LANES), F32), dma((PANELS,))],
        compiler_params=pltpu.CompilerParams(vmem_limit_bytes=12 * MIB),
        name="write_results",
    )(*inner(canvas, held, got_v, got_h, got_c, update, peak), probe)
    return new_object, new_probe


def solution(mesh):
    placed = (
        P(None, "row", "col"),
        P(),
        P(),
        P("row", "col", None, None),
        P("row", "col", None, None, None),
    )
    return jax.shard_map(
        on_device,
        mesh=mesh,
        in_specs=placed,
        out_specs=(P(None, "row", "col"), P()),
        check_vma=False,
    )
```

```python
import functools
import math

import jax
import jax.numpy as jnp
import ml_dtypes
import numpy as np
from jax import lax
from jax.experimental import pallas as pl
from jax.experimental.pallas import tpu as pltpu
from jax.sharding import PartitionSpec as P

MESH = pl.DeviceIdType.MESH
F32, BF16 = jnp.float32, jnp.bfloat16
SIZE, TILE, HALF, LANES = 256, 768, 128, 128
EXT = TILE + 2 * HALF
PANELS = TILE // LANES
MODES = 2
PLANES = 2 * MODES
N_ROW, N_COL = 8, 16
UNITS = 128
UNIT_ROWS = 24
BATCH = 2
VMEM = pl.BlockSpec(memory_space=pltpu.VMEM)
SMEM = pl.BlockSpec(memory_space=pltpu.SMEM)
HBM = pl.BlockSpec(memory_space=pltpu.HBM)
ANY = pl.BlockSpec(memory_space=pl.ANY)
MIB = 2**20


def dft_tables():
    indices = np.arange(SIZE)
    product = indices[:, None] * indices[None, :] % SIZE
    angles = product.astype(np.float32) * np.float32(2.0 * np.pi / SIZE)
    scale = np.float32(1.0 / math.sqrt(SIZE))
    both = np.stack([np.cos(angles) * scale, np.sin(angles) * scale])
    return both.astype(ml_dtypes.bfloat16).astype(np.float32)


def around(row, col):
    up, down = lax.rem(row + N_ROW - 1, N_ROW), lax.rem(row + 1, N_ROW)
    left, right = lax.rem(col + N_COL - 1, N_COL), lax.rem(col + 1, N_COL)
    return [(up, col), (down, col), (row, left), (row, right), (up, left), (up, right), (down, left), (down, right)]


def greet(targets):
    barrier = pltpu.get_barrier_semaphore()
    for target in targets:
        pl.semaphore_signal(barrier, inc=1, device_id=target, device_id_type=MESH)
    return barrier


def remote(src, dst, send, recv, target):
    return pltpu.make_async_remote_copy(
        src_ref=src, dst_ref=dst, send_sem=send, recv_sem=recv, device_id=target, device_id_type=MESH
    )


def inside(row, col):
    up, down, left, right = row > 0, row < N_ROW - 1, col > 0, col < N_COL - 1
    return [up, down, left, right, up & left, up & right, down & left, down & right]


def rim_copies(out, got, send, recv, row, col):
    opposite = (1, 0, 3, 2, 7, 6, 5, 4)
    return [
        remote(out[i], got[opposite[i]], send.at[i], recv.at[opposite[i]], target)
        for i, target in enumerate(around(row, col))
    ]


def exchange_object(
    obj, patterns, waves, wide, held, amplitudes, tables, canvas,
    low_v, low_h, got_v, got_h, got_c, held_waves, load, send, recv,
):
    row, col = lax.axis_index("row"), lax.axis_index("col")
    order = (0, PANELS - 1) + tuple(range(1, PANELS - 1))
    loads = [
        pltpu.make_async_copy(obj.at[:, :, k * LANES : (k + 1) * LANES], held.at[:, k], load.at[k])
        for k in range(PANELS)
    ]
    for k in order:
        loads[k].start()
    fetches = [
        pltpu.make_async_copy(patterns, amplitudes, load.at[PANELS]),
        pltpu.make_async_copy(waves, held_waves, load.at[PANELS + 1]),
    ]
    for fetch in fetches:
        fetch.start()
    barrier = greet(around(row, col))
    rims = rim_copies(
        [low_v.at[0], low_v.at[1], low_h.at[0], low_h.at[1]]
        + [low_h.at[0, :, 0:HALF], low_h.at[1, :, 0:HALF], low_h.at[0, :, TILE - HALF :], low_h.at[1, :, TILE - HALF :]],
        [got_v.at[0], got_v.at[1], got_h.at[0], got_h.at[1]] + [got_c.at[i] for i in range(4)],
        send,
        recv,
        row,
        col,
    )
    for step, k in enumerate(order):
        loads[k].wait()

        @pl.loop(0, TILE // HALF)
        def _(i, k=k):
            rows = pl.ds(pl.multiple_of(i * HALF, HALF), HALF)
            for p in range(2):
                low = held[p, k, rows, :].astype(BF16)
                wide[p, k + 1, pl.ds(pl.multiple_of(i * HALF + HALF, HALF), HALF), :] = low.astype(F32)
                if k == 0:
                    low_h[0, p, rows, :] = low
                if k == PANELS - 1:
                    low_h[1, p, rows, :] = low

        for p in range(2):
            low_v[0, p, k] = held[p, k, 0:HALF, :].astype(BF16)
            low_v[1, p, k] = held[p, k, TILE - HALF :, :].astype(BF16)
        if step == 1:
            pl.semaphore_wait(barrier, 8)
            for i in (2, 3, 4, 5, 6, 7):
                rims[i].start()
    for i in (0, 1):
        rims[i].start()
    have = inside(row, col)

    def keep(i, value):
        return jnp.where(have[i], value.astype(F32), 0.0)

    @pl.loop(0, EXT // 32)
    def _(i):
        rows = pl.ds(pl.multiple_of(i * 32, 32), 32)
        for p in range(2):
            for k in range(PANELS + 2):
                canvas[p, k, rows, :] = jnp.zeros((32, LANES), F32)

    for fetch in fetches:
        fetch.wait()
    real, imag = slice(0, SIZE), slice(SIZE, 2 * SIZE)
    cosine, sine = held_waves[0].astype(BF16), held_waves[1].astype(BF16)
    minus = (-held_waves[1]).astype(BF16)
    for t in range(2):
        tables[t, real, real] = cosine
        tables[t, imag, imag] = cosine
        tables[t, real, imag] = sine if t else minus
        tables[t, imag, real] = minus if t else sine

    for i in (0, 1, 4, 5, 6, 7, 2, 3):
        rims[i].wait()
    for p in range(2):
        for k in range(PANELS):
            wide[p, k + 1, 0:HALF, :] = keep(0, got_v[0, p, k])
            wide[p, k + 1, EXT - HALF :, :] = keep(1, got_v[1, p, k])
        for corner in range(4):
            rows = slice(0, HALF) if corner < 2 else slice(EXT - HALF, EXT)
            wide[p, (corner % 2) * (PANELS + 1), rows, :] = keep(4 + corner, got_c[corner, p])

    @pl.loop(0, TILE // HALF)
    def _(i):
        rows = pl.ds(pl.multiple_of(i * HALF, HALF), HALF)
        to = pl.ds(pl.multiple_of(i * HALF + HALF, HALF), HALF)
        for p in range(2):
            wide[p, 0, to, :] = keep(2, got_h[0, p, rows, :])
            wide[p, PANELS + 1, to, :] = keep(3, got_h[1, p, rows, :])


def transform_slots(slots, low, wide, patterns, tables, sums, patch, wave, half, shift, back):
    lane = lax.broadcasted_iota(jnp.int32, (SIZE, LANES), 1)
    real, imag = slice(0, SIZE), slice(SIZE, 2 * SIZE)
    covered = 0.0
    for b, (row, col, s, weight) in enumerate(slots):
        panel = col // LANES
        turn = col - panel * LANES
        rows = pl.ds(row, SIZE)
        field = []
        for p in range(2):
            parts = [pltpu.roll(wide[p, panel + k, rows, :], lax.rem(LANES - turn, LANES), 1) for k in range(3)]
            whole = jnp.concatenate([jnp.where(lane < LANES - turn, parts[k], parts[k + 1]) for k in range(2)], 1)
            patch[b, p] = whole
            field.append(whole)
        covered = covered + weight * (field[0] * field[0] + field[1] * field[1])
        for m in range(MODES):
            wave[b, m, :, real] = (low[m, 0] * field[0] - low[m, 1] * field[1]).astype(BF16)
            wave[b, m, :, imag] = (low[m, 0] * field[1] + low[m, 1] * field[0]).astype(BF16)
    for k in range(2):
        sums[PLANES, k] += covered[:, k * LANES : (k + 1) * LANES]
    for b in range(len(slots)):
        for m in range(MODES):
            product = jnp.dot(wave[b, m], tables[0], preferred_element_type=F32)
            half[b, m, real, :] = product[:, real].astype(BF16)
            half[b, m, imag, :] = product[:, imag].astype(BF16)
    for b, (_, _, s, weight) in enumerate(slots):
        spectra = [
            [jnp.dot(tables[1, part, :], half[b, m], preferred_element_type=F32) for part in (real, imag)]
            for m in range(MODES)
        ]
        power = (
            spectra[0][0] * spectra[0][0]
            + spectra[0][1] * spectra[0][1]
            + spectra[1][0] * spectra[1][0]
            + spectra[1][1] * spectra[1][1]
        )
        factor = weight * (patterns[s].astype(F32) * lax.rsqrt(jnp.maximum(power, 0.5)) - 1.0)
        for m in range(MODES):
            shift[b, m, :, real] = (factor * spectra[m][0]).astype(BF16)
            shift[b, m, :, imag] = (factor * spectra[m][1]).astype(BF16)
    for b in range(len(slots)):
        for m in range(MODES):
            product = jnp.dot(shift[b, m], tables[1], preferred_element_type=F32)
            back[b, m, real, :] = product[:, real].astype(BF16)
            back[b, m, imag, :] = product[:, imag].astype(BF16)
    terms = [[0.0, 0.0] for _ in slots]
    for m in range(MODES):
        gained = [0.0, 0.0]
        for b in range(len(slots)):
            change_real = jnp.dot(tables[0, real, :], back[b, m], preferred_element_type=F32)
            change_imag = jnp.dot(tables[0, imag, :], back[b, m], preferred_element_type=F32)
            terms[b][0] = terms[b][0] + low[m, 0] * change_real + low[m, 1] * change_imag
            terms[b][1] = terms[b][1] + low[m, 0] * change_imag - low[m, 1] * change_real
            gained[0] = gained[0] + patch[b, 0] * change_real + patch[b, 1] * change_imag
            gained[1] = gained[1] + patch[b, 0] * change_imag - patch[b, 1] * change_real
        for part in range(2):
            for k in range(2):
                sums[2 * m + part, k] += gained[part][:, k * LANES : (k + 1) * LANES]
    return terms


def place_term(canvas, row, col, term):
    lane = lax.broadcasted_iota(jnp.int32, (SIZE, LANES), 1)
    panel = col // LANES
    turn = col - panel * LANES
    rows = pl.ds(row, SIZE)
    for p in range(2):
        rounded = term[p].astype(BF16).astype(F32)
        first = pltpu.roll(rounded[:, :LANES], turn, 1)
        second = pltpu.roll(rounded[:, LANES:], turn, 1)
        canvas[p, panel, rows, :] += jnp.where(lane < turn, 0.0, first)
        canvas[p, panel + 1, rows, :] += jnp.where(lane < turn, first, second)
        canvas[p, panel + 2, rows, :] += jnp.where(lane < turn, second, 0.0)


def process_slots(counts, centers, wide, probe, patterns, tables, blank, sums, canvas, low, patch, wave, half, shift, back):
    count = counts[lax.axis_index("row"), lax.axis_index("col")]
    low[...] = probe[...].astype(BF16).astype(F32)
    sums[...] = jnp.zeros_like(sums)

    @pl.loop(0, (count + BATCH - 1) // BATCH)
    def _(i):
        slots = []
        for b in range(BATCH):
            s = jnp.minimum(BATCH * i + b, count - 1)
            weight = jnp.where(BATCH * i + b < count, 1.0, 0.0).astype(F32)
            slots.append((centers[0, s], centers[1, s], s, weight))
        terms = transform_slots(slots, low, wide, patterns, tables, sums, patch, wave, half, shift, back)
        for (row, col, _, _), term in zip(slots, terms):
            place_term(canvas, row, col, term)


def exchange_sums(
    canvas, sums, probe, got_v, got_h, got_c, update, peak,
    low_v, low_h, low_c, pair, half, from_plane, share, from_line,
    send, recv, pair_send, pair_recv, in_send, in_recv, out_send, out_recv,
):
    row, col = lax.axis_index("row"), lax.axis_index("col")
    x, core, z, y = row // 2, lax.rem(row, 2), col // 4, lax.rem(col, 4)
    sibling = (row + 1 - 2 * core, col)
    tiles = around(row, col)
    other = jnp.where(core == 0, tiles[0][0], tiles[1][0])
    along_x = [lax.rem(x + d, 4) for d in range(4)]
    along_z = [4 * lax.rem(z + d, 4) for d in range(4)]
    along_y = [lax.rem(y + d, 4) for d in range(4)]
    cols = [along_z[d // 4] + along_y[d % 4] for d in range(16)]
    plane = [((2 * along_x[j // 4] + core, along_z[j % 4] + y), 16 * along_x[j // 4] + along_z[j % 4]) for j in range(16)]
    line = [((row, 4 * z + along_y[j]), along_y[j]) for j in range(4)]
    hops = (0, 1, 2, 1)
    order = sorted(range(1, 16), key=lambda j: -(hops[j // 4] + hops[j % 4]))
    barrier = greet([sibling, (other, col)] + tiles[2:] + [plane[j][0] for j in order] + [line[j][0] for j in (2, 1, 3)])
    pl.semaphore_wait(barrier, 26)

    mine = core * 64
    me = 16 * x + col
    to_pair = remote(sums.at[:, 1 - core], pair, pair_send.at[0], pair_recv.at[0], sibling)
    to_pair.start()

    @pl.loop(0, TILE // HALF)
    def _(i):
        rows = pl.ds(pl.multiple_of(i * HALF, HALF), HALF)
        at = pl.ds(pl.multiple_of(i * HALF + HALF, HALF), HALF)
        for p in range(2):
            low_h[0, p, rows, :] = canvas[p, 0, at, :].astype(BF16)
            low_h[1, p, rows, :] = canvas[p, PANELS + 1, at, :].astype(BF16)

    for p in range(2):
        for corner in range(4):
            at = slice(0, HALF) if corner < 2 else slice(EXT - HALF, EXT)
            low_c[corner, p] = canvas[p, (corner % 2) * (PANELS + 1), at, :].astype(BF16)
        for k in range(PANELS):
            low_v[0, p, k] = canvas[p, k + 1, 0:HALF, :].astype(BF16)
            low_v[1, p, k] = canvas[p, k + 1, EXT - HALF :, :].astype(BF16)
    opposite = (1, 0, 3, 2, 7, 6, 5, 4)
    third, pairs = TILE // 3, PANELS // 3
    parts = {}
    for part in range(3):
        some, few = slice(part * third, (part + 1) * third), slice(part * pairs, (part + 1) * pairs)
        for i in range(2):
            parts[i, part] = low_v.at[i, :, few], got_v.at[1 - i, :, few]
            parts[2 + i, part] = low_h.at[i, :, some], got_h.at[1 - i, :, some]
    for i in range(4):
        parts[4 + i, 0] = low_c.at[i], got_c.at[3 - i]
    places = sorted(parts)
    rims = []

    def send_rims(*chosen):
        for i, part in chosen:
            source, target = parts[i, part]
            arrival = recv.at[places.index((opposite[i], part))]
            rims.append(remote(source, target, send.at[places.index((i, part))], arrival, tiles[i]))
            rims[-1].start()

    squares = probe[0, 0] * probe[0, 0] + probe[0, 1] * probe[0, 1]
    squares = squares + probe[1, 0] * probe[1, 0] + probe[1, 1] * probe[1, 1]
    peak[...] = jnp.broadcast_to(jnp.max(squares, keepdims=True) + 1e-06, peak.shape)

    send_rims((2, 0), (3, 0), (0, 0), (1, 0))
    to_pair.wait()

    for q in range(PLANES + 1):
        half[q] = (sums[q, core] + pair[q]).astype(BF16)

    def rows_of(block):
        return pl.ds(pl.multiple_of(4 * block, 16), 16)

    inward = [
        remote(half.at[:, rows_of(plane[j][1])], from_plane.at[j - 1], in_send.at[j], in_recv.at[j], plane[j][0])
        for j in order
    ]
    for copy in inward:
        copy.start()
    send_rims((2, 1), (3, 1), (0, 1), (1, 1))
    for copy in reversed(inward):
        copy.wait()
    pieces = []
    for q in range(PLANES + 1):
        total = half[q, rows_of(16 * x + 4 * z), :].astype(F32)
        for j in range(15):
            total = total + from_plane[j, q].astype(F32)
        pieces.append(total)
    blank = jnp.zeros((UNIT_ROWS - 4 * PLANES - 4, LANES), F32)
    for k in range(4):
        share[k] = jnp.concatenate([piece[4 * k : 4 * k + 4] for piece in pieces] + [blank], 0).astype(BF16)
    inward = [
        remote(share.at[line[j][1]], from_line.at[j - 1], in_send.at[15 + j], in_recv.at[15 + j], line[j][0])
        for j in (2, 1, 3)
    ]
    for copy in inward:
        copy.start()
    send_rims((0, 2), (1, 2), (4, 0), (5, 0))
    for copy in inward:
        copy.wait()
    total = share[y].astype(F32)
    for j in range(3):
        total = total + from_line[j].astype(F32)
    spread = lax.rsqrt(total[4 * PLANES : 4 * PLANES + 4])
    unit = mine + me
    update[unit] = (total[0 : 4 * PLANES] * jnp.concatenate([spread] * PLANES, 0)).astype(BF16)
    outward = [
        remote(update.at[unit], update.at[unit], out_send.at[15 + j], out_recv.at[15 + j], line[j][0]) for j in (2, 1, 3)
    ]
    for copy in outward:
        copy.start()
    send_rims((6, 0), (7, 0))
    for copy in outward:
        copy.wait()
    block = update.at[pl.ds(mine + 16 * x + 4 * z, 4)]
    outward = {j: remote(block, block, out_send.at[j], out_recv.at[j], plane[j][0]) for j in order}
    for j in order:
        outward[j].start()
    send_rims((2, 2), (3, 2))
    over = []
    for j in [0] + order[::-1]:
        came = 4 * ((4 - j // 4) % 4) + (4 - j % 4) % 4
        block = update.at[pl.ds(mine + plane[came][1], 4)]
        if j:
            outward[j].wait()
        over.append(remote(block, block, pair_send.at[1 + j], pair_recv.at[1 + j], sibling))
        over[-1].start()
    for copy in over:
        copy.wait()
    for copy in rims:
        copy.wait()


def write_results(canvas, held, got_v, got_h, got_c, update, peak, probe, new_object, new_probe, stage, store):
    row, col = lax.axis_index("row"), lax.axis_index("col")
    have = inside(row, col)
    scale = 1.0 / peak[0:1, :]

    def keep(i, value):
        return jnp.where(have[i], value.astype(F32), 0.0)

    stores = []
    for k in range(PANELS):
        for p in range(2):
            side = None if k not in (0, PANELS - 1) else (0 if k == 0 else 1)
            for i in range(TILE // HALF):
                rows = slice(i * HALF, (i + 1) * HALF)
                value = canvas[p, k + 1, HALF + i * HALF : 2 * HALF + i * HALF, :]
                if i == 0:
                    value = value + keep(0, got_v[0, p, k])
                if i == TILE // HALF - 1:
                    value = value + keep(1, got_v[1, p, k])
                if side is not None:
                    value = value + keep(2 + side, got_h[side, p, rows, :])
                    if i == 0:
                        value = value + keep(4 + side, got_c[side, p])
                    if i == TILE // HALF - 1:
                        value = value + keep(6 + side, got_c[2 + side, p])
                stage[p, k, rows, :] = held[p, k, rows, :] + value * scale
        copy = pltpu.make_async_copy(stage.at[:, k], new_object.at[:, :, k * LANES : (k + 1) * LANES], store.at[k])
        copy.start()
        stores.append(copy)

    @pl.loop(0, SIZE // 8)
    def _(i):
        rows = pl.ds(pl.multiple_of(i * 8, 8), 8)
        for k in range(2):
            lanes = slice(k * LANES, (k + 1) * LANES)
            first = update[k * 64 + 2 * i].astype(F32)
            second = update[k * 64 + 2 * i + 1].astype(F32)
            for q in range(PLANES):
                value = jnp.concatenate([first[4 * q : 4 * q + 4], second[4 * q : 4 * q + 4]], 0)
                new_probe[q // 2, q % 2, rows, lanes] = probe[q // 2, q % 2, rows, lanes] + value

    for copy in stores:
        copy.wait()


def on_device(object_field, probe_modes, counts, centers, patterns):
    waves = pltpu.with_memory_space_constraint(jnp.asarray(dft_tables()), pltpu.HBM)
    dma = pltpu.SemaphoreType.DMA
    probe = pltpu.with_memory_space_constraint(probe_modes, pltpu.VMEM)
    strips = [
        pltpu.VMEM((2, 2, PANELS, HALF, LANES), BF16),
        pltpu.VMEM((2, 2, TILE, LANES), BF16),
        pltpu.VMEM((4, 2, HALF, LANES), BF16),
    ]

    def inner(*arrays):
        return [pltpu.with_memory_space_constraint(a, pltpu.VMEM) for a in arrays]

    extended = pltpu.VMEM((2, PANELS + 2, EXT, LANES), F32)
    wide, held, amplitudes, tables, canvas = pl.pallas_call(
        exchange_object,
        out_shape=[
            extended,
            pltpu.VMEM((2, PANELS, TILE, LANES), F32),
            pltpu.VMEM(patterns.shape[2:], BF16),
            pltpu.VMEM((2, 2 * SIZE, 2 * SIZE), BF16),
            extended,
        ],
        in_specs=[HBM] * 3,
        out_specs=[VMEM] * 5,
        scratch_shapes=strips[:2] + strips + [pltpu.VMEM((2, SIZE, SIZE), F32), dma((PANELS + 2,)), dma((8,)), dma((8,))],
        compiler_params=pltpu.CompilerParams(collective_id=0, has_side_effects=True, vmem_limit_bytes=16 * MIB),
        name="exchange_object",
    )(
        pltpu.with_memory_space_constraint(object_field, pltpu.HBM),
        pltpu.with_memory_space_constraint(patterns[0, 0], pltpu.HBM),
        waves,
    )
    wide, held, amplitudes, tables, canvas = inner(wide, held, amplitudes, tables, canvas)
    sums, canvas = pl.pallas_call(
        process_slots,
        out_shape=[pltpu.VMEM((PLANES + 1, 2, SIZE, LANES), F32), extended],
        in_specs=[SMEM, SMEM] + [VMEM] * 5,
        out_specs=[VMEM, VMEM],
        scratch_shapes=[
            pltpu.VMEM((MODES, 2, SIZE, SIZE), F32),
            pltpu.VMEM((BATCH, 2, SIZE, SIZE), F32),
            pltpu.VMEM((BATCH, MODES, SIZE, 2 * SIZE), BF16),
            pltpu.VMEM((BATCH, MODES, 2 * SIZE, SIZE), BF16),
            pltpu.VMEM((BATCH, MODES, SIZE, 2 * SIZE), BF16),
            pltpu.VMEM((BATCH, MODES, 2 * SIZE, SIZE), BF16),
        ],
        input_output_aliases={6: 1},
        compiler_params=pltpu.CompilerParams(vmem_limit_bytes=24 * MIB),
        name="process_slots",
    )(counts, centers[0, 0], wide, probe, amplitudes, tables, canvas)
    sums, canvas = inner(sums, canvas)
    got_v, got_h, got_c, update, peak = pl.pallas_call(
        exchange_sums,
        out_shape=strips + [pltpu.VMEM((UNITS, 16, LANES), BF16), pltpu.VMEM((8, LANES), F32)],
        in_specs=[VMEM] * 3,
        out_specs=[VMEM] * 5,
        scratch_shapes=strips
        + [
            pltpu.VMEM((PLANES + 1, SIZE, LANES), F32),
            pltpu.VMEM((PLANES + 1, SIZE, LANES), BF16),
            pltpu.VMEM((15, PLANES + 1, 16, LANES), BF16),
            pltpu.VMEM((4, UNIT_ROWS, LANES), BF16),
            pltpu.VMEM((3, UNIT_ROWS, LANES), BF16),
            dma((16,)), dma((16,)), dma((17,)), dma((17,)), dma((19,)), dma((19,)), dma((19,)), dma((19,)),
        ],
        compiler_params=pltpu.CompilerParams(collective_id=1, has_side_effects=True, vmem_limit_bytes=16 * MIB),
        name="exchange_sums",
    )(canvas, sums, probe)
    new_object, new_probe = pl.pallas_call(
        write_results,
        out_shape=[
            jax.ShapeDtypeStruct(object_field.shape, F32),
            jax.ShapeDtypeStruct(probe_modes.shape, F32),
        ],
        in_specs=[VMEM] * 8,
        out_specs=[ANY, VMEM],
        scratch_shapes=[pltpu.VMEM((2, PANELS, TILE, LANES), F32), dma((PANELS,))],
        compiler_params=pltpu.CompilerParams(vmem_limit_bytes=12 * MIB),
        name="write_results",
    )(*inner(canvas, held, got_v, got_h, got_c, update, peak), probe)
    return new_object, new_probe


def solution(mesh):
    placed = (
        P(None, "row", "col"),
        P(),
        P(),
        P("row", "col", None, None),
        P("row", "col", None, None, None),
    )
    return jax.shard_map(
        on_device,
        mesh=mesh,
        in_specs=placed,
        out_specs=(P(None, "row", "col"), P()),
        check_vma=False,
    )
```

```python
import functools
import math

import jax
import jax.numpy as jnp
import ml_dtypes
import numpy as np
from jax import lax
from jax.experimental import pallas as pl
from jax.experimental.pallas import tpu as pltpu
from jax.sharding import PartitionSpec as P

MESH = pl.DeviceIdType.MESH
F32, BF16 = jnp.float32, jnp.bfloat16
SIZE, TILE, HALF, LANES = 256, 768, 128, 128
EXT = TILE + 2 * HALF
PANELS = TILE // LANES
MODES = 2
PLANES = 2 * MODES
N_ROW, N_COL = 8, 16
SLOTS = 12
UNITS = 128
UNIT_ROWS = 24
BATCH = 2
VMEM = pl.BlockSpec(memory_space=pltpu.VMEM)
SMEM = pl.BlockSpec(memory_space=pltpu.SMEM)
HBM = pl.BlockSpec(memory_space=pltpu.HBM)
ANY = pl.BlockSpec(memory_space=pl.ANY)
MIB = 2**20


def dft_tables():
    indices = np.arange(SIZE)
    product = indices[:, None] * indices[None, :] % SIZE
    angles = product.astype(np.float32) * np.float32(2.0 * np.pi / SIZE)
    scale = np.float32(1.0 / math.sqrt(SIZE))
    both = np.stack([np.cos(angles) * scale, np.sin(angles) * scale])
    return both.astype(ml_dtypes.bfloat16).astype(np.float32)


def around(row, col):
    up, down = lax.rem(row + N_ROW - 1, N_ROW), lax.rem(row + 1, N_ROW)
    left, right = lax.rem(col + N_COL - 1, N_COL), lax.rem(col + 1, N_COL)
    return [(up, col), (down, col), (row, left), (row, right), (up, left), (up, right), (down, left), (down, right)]


def greet(targets):
    barrier = pltpu.get_barrier_semaphore()
    for target in targets:
        pl.semaphore_signal(barrier, inc=1, device_id=target, device_id_type=MESH)
    return barrier


def remote(src, dst, send, recv, target):
    return pltpu.make_async_remote_copy(
        src_ref=src, dst_ref=dst, send_sem=send, recv_sem=recv, device_id=target, device_id_type=MESH
    )


def inside(row, col):
    up, down, left, right = row > 0, row < N_ROW - 1, col > 0, col < N_COL - 1
    return [up, down, left, right, up & left, up & right, down & left, down & right]


def rim_copies(out, got, send, recv, row, col):
    opposite = (1, 0, 3, 2, 7, 6, 5, 4)
    return [
        remote(out[i], got[opposite[i]], send.at[i], recv.at[opposite[i]], target)
        for i, target in enumerate(around(row, col))
    ]


def choose_slots(counts, centers):
    count = counts[lax.axis_index("row"), lax.axis_index("col")]
    picks, found, taken = [0] * 4, [0] * 4, []
    inner_seen, calm_seen = 0, 0
    for s in range(SLOTS):
        row, col = centers[0, s], centers[1, s]
        live = jnp.where(s < count, 1, 0)
        calm = live * jnp.where(col >= HALF, 1, 0) * jnp.where(col <= TILE - HALF, 1, 0)
        inner = calm * jnp.where(row >= HALF, 1, 0) * jnp.where(row <= TILE - HALF, 1, 0)
        first = inner * jnp.where(inner_seen < 2, 1, 0)
        second = (calm - first) * jnp.where(calm_seen < 2, 1, 0)
        for i in range(2):
            here = first * jnp.where(inner_seen == i, 1, 0)
            picks[i], found[i] = picks[i] + s * here, found[i] + here
            here = second * jnp.where(calm_seen == i, 1, 0)
            picks[2 + i], found[2 + i] = picks[2 + i] + s * here, found[2 + i] + here
        inner_seen, calm_seen = inner_seen + first, calm_seen + second
        taken.append((live, first + second))
    slots = []
    for s, flag in zip(picks, found):
        row = jnp.where(flag == 1, centers[0, s], HALF)
        col = jnp.where(flag == 1, centers[1, s], HALF)
        slots.append((row, col, s, jnp.where(flag == 1, 1.0, 0.0).astype(F32)))
    return slots, taken


def exchange_object(
    all_counts, all_centers, obj, patterns, waves, probe, wide, held, amplitudes, tables, canvas, low, sums, terms,
    low_v, low_h, got_v, got_h, got_c, held_waves, held_probe, counts, centers, patch, wave, half, shift, back,
    load, send, recv,
):
    row, col = lax.axis_index("row"), lax.axis_index("col")
    order = (0, PANELS - 1) + tuple(range(1, PANELS - 1))
    loads = [
        pltpu.make_async_copy(obj.at[:, :, k * LANES : (k + 1) * LANES], held.at[:, k], load.at[k])
        for k in range(PANELS)
    ]
    for k in order:
        loads[k].start()
    fetches = [
        pltpu.make_async_copy(waves, held_waves, load.at[PANELS]),
        pltpu.make_async_copy(probe, held_probe, load.at[PANELS + 1]),
        pltpu.make_async_copy(patterns, amplitudes, load.at[PANELS + 2]),
        pltpu.make_async_copy(all_counts, counts, load.at[PANELS + 3]),
        pltpu.make_async_copy(all_centers, centers, load.at[PANELS + 4]),
    ]
    for fetch in fetches:
        fetch.start()
    barrier = greet(around(row, col))
    rims = rim_copies(
        [low_v.at[0], low_v.at[1], low_h.at[0], low_h.at[1]]
        + [low_h.at[0, :, 0:HALF], low_h.at[1, :, 0:HALF], low_h.at[0, :, TILE - HALF :], low_h.at[1, :, TILE - HALF :]],
        [got_v.at[0], got_v.at[1], got_h.at[0], got_h.at[1]] + [got_c.at[i] for i in range(4)],
        send,
        recv,
        row,
        col,
    )
    for step, k in enumerate(order):
        loads[k].wait()

        @pl.loop(0, TILE // HALF)
        def _(i, k=k):
            rows = pl.ds(pl.multiple_of(i * HALF, HALF), HALF)
            for p in range(2):
                rounded = held[p, k, rows, :].astype(BF16)
                wide[p, k + 1, pl.ds(pl.multiple_of(i * HALF + HALF, HALF), HALF), :] = rounded.astype(F32)
                if k == 0:
                    low_h[0, p, rows, :] = rounded
                if k == PANELS - 1:
                    low_h[1, p, rows, :] = rounded

        for p in range(2):
            low_v[0, p, k] = held[p, k, 0:HALF, :].astype(BF16)
            low_v[1, p, k] = held[p, k, TILE - HALF :, :].astype(BF16)
        if step == 1:
            pl.semaphore_wait(barrier, 8)
            for i in (2, 3, 4, 5, 6, 7):
                rims[i].start()
    for i in (0, 1):
        rims[i].start()
    have = inside(row, col)

    def keep(i, value):
        return jnp.where(have[i], value.astype(F32), 0.0)

    for fetch in fetches:
        fetch.wait()
    real, imag = slice(0, SIZE), slice(SIZE, 2 * SIZE)
    cosine, sine = held_waves[0].astype(BF16), held_waves[1].astype(BF16)
    minus = (-held_waves[1]).astype(BF16)
    for t in range(2):
        tables[t, real, real] = cosine
        tables[t, imag, imag] = cosine
        tables[t, real, imag] = sine if t else minus
        tables[t, imag, real] = minus if t else sine
    low[...] = held_probe[...].astype(BF16).astype(F32)
    sums[...] = jnp.zeros_like(sums)
    slots, _ = choose_slots(counts, centers)

    def run(i):
        made = transform_slots(
            slots[i : i + 2], low, wide, amplitudes, tables, sums, patch, wave, half, shift, back
        )
        for b in range(2):
            for p in range(2):
                terms[i + b, p] = made[b][p].astype(BF16).astype(F32)

    run(0)
    for i in (0, 1):
        rims[i].wait()
    for p in range(2):
        for k in range(PANELS):
            wide[p, k + 1, 0:HALF, :] = keep(0, got_v[0, p, k])
            wide[p, k + 1, EXT - HALF :, :] = keep(1, got_v[1, p, k])
    run(2)

    @pl.loop(0, EXT // 32)
    def _(i):
        rows = pl.ds(pl.multiple_of(i * 32, 32), 32)
        for p in range(2):
            for k in range(PANELS + 2):
                canvas[p, k, rows, :] = jnp.zeros((32, LANES), F32)

    for i in (4, 5, 6, 7, 2, 3):
        rims[i].wait()
    for p in range(2):
        for corner in range(4):
            rows = slice(0, HALF) if corner < 2 else slice(EXT - HALF, EXT)
            wide[p, (corner % 2) * (PANELS + 1), rows, :] = keep(4 + corner, got_c[corner, p])

    @pl.loop(0, TILE // HALF)
    def _(i):
        rows = pl.ds(pl.multiple_of(i * HALF, HALF), HALF)
        to = pl.ds(pl.multiple_of(i * HALF + HALF, HALF), HALF)
        for p in range(2):
            wide[p, 0, to, :] = keep(2, got_h[0, p, rows, :])
            wide[p, PANELS + 1, to, :] = keep(3, got_h[1, p, rows, :])


def transform_slots(slots, low, wide, patterns, tables, sums, patch, wave, half, shift, back):
    lane = lax.broadcasted_iota(jnp.int32, (SIZE, LANES), 1)
    real, imag = slice(0, SIZE), slice(SIZE, 2 * SIZE)
    covered = 0.0
    for b, (row, col, s, weight) in enumerate(slots):
        panel = col // LANES
        turn = col - panel * LANES
        rows = pl.ds(row, SIZE)
        field = []
        for p in range(2):
            parts = [pltpu.roll(wide[p, panel + k, rows, :], lax.rem(LANES - turn, LANES), 1) for k in range(3)]
            whole = jnp.concatenate([jnp.where(lane < LANES - turn, parts[k], parts[k + 1]) for k in range(2)], 1)
            patch[b, p] = whole
            field.append(whole)
        covered = covered + weight * (field[0] * field[0] + field[1] * field[1])
        for m in range(MODES):
            wave[b, m, :, real] = (low[m, 0] * field[0] - low[m, 1] * field[1]).astype(BF16)
            wave[b, m, :, imag] = (low[m, 0] * field[1] + low[m, 1] * field[0]).astype(BF16)
    for k in range(2):
        sums[PLANES, k] += covered[:, k * LANES : (k + 1) * LANES]
    for b in range(len(slots)):
        for m in range(MODES):
            product = jnp.dot(wave[b, m], tables[0], preferred_element_type=F32)
            half[b, m, real, :] = product[:, real].astype(BF16)
            half[b, m, imag, :] = product[:, imag].astype(BF16)
    for b, (_, _, s, weight) in enumerate(slots):
        spectra = [
            [jnp.dot(tables[1, part, :], half[b, m], preferred_element_type=F32) for part in (real, imag)]
            for m in range(MODES)
        ]
        power = (
            spectra[0][0] * spectra[0][0]
            + spectra[0][1] * spectra[0][1]
            + spectra[1][0] * spectra[1][0]
            + spectra[1][1] * spectra[1][1]
        )
        factor = weight * (patterns[s].astype(F32) * lax.rsqrt(jnp.maximum(power, 0.5)) - 1.0)
        for m in range(MODES):
            shift[b, m, :, real] = (factor * spectra[m][0]).astype(BF16)
            shift[b, m, :, imag] = (factor * spectra[m][1]).astype(BF16)
    for b in range(len(slots)):
        for m in range(MODES):
            product = jnp.dot(shift[b, m], tables[1], preferred_element_type=F32)
            back[b, m, real, :] = product[:, real].astype(BF16)
            back[b, m, imag, :] = product[:, imag].astype(BF16)
    terms = [[0.0, 0.0] for _ in slots]
    for m in range(MODES):
        gained = [0.0, 0.0]
        for b in range(len(slots)):
            change_real = jnp.dot(tables[0, real, :], back[b, m], preferred_element_type=F32)
            change_imag = jnp.dot(tables[0, imag, :], back[b, m], preferred_element_type=F32)
            terms[b][0] = terms[b][0] + low[m, 0] * change_real + low[m, 1] * change_imag
            terms[b][1] = terms[b][1] + low[m, 0] * change_imag - low[m, 1] * change_real
            gained[0] = gained[0] + patch[b, 0] * change_real + patch[b, 1] * change_imag
            gained[1] = gained[1] + patch[b, 0] * change_imag - patch[b, 1] * change_real
        for part in range(2):
            for k in range(2):
                sums[2 * m + part, k] += gained[part][:, k * LANES : (k + 1) * LANES]
    return terms


def place_term(canvas, row, col, term):
    lane = lax.broadcasted_iota(jnp.int32, (SIZE, LANES), 1)
    panel = col // LANES
    turn = col - panel * LANES
    rows = pl.ds(row, SIZE)
    for p in range(2):
        rounded = term[p].astype(BF16).astype(F32)
        first = pltpu.roll(rounded[:, :LANES], turn, 1)
        second = pltpu.roll(rounded[:, LANES:], turn, 1)
        canvas[p, panel, rows, :] += jnp.where(lane < turn, 0.0, first)
        canvas[p, panel + 1, rows, :] += jnp.where(lane < turn, first, second)
        canvas[p, panel + 2, rows, :] += jnp.where(lane < turn, second, 0.0)


def process_slots(
    counts, centers, wide, low, patterns, tables, terms, blank, begun, sums, canvas, left, patch, wave, half, shift, back
):
    slots, taken = choose_slots(counts, centers)
    for i, (row, col, _, _) in enumerate(slots):
        place_term(canvas, row, col, terms[i])
    count = 0
    for s, (live, done) in enumerate(taken):
        left[count] = s
        count = count + live - done

    @pl.loop(0, (count + BATCH - 1) // BATCH)
    def _(i):
        slots = []
        for b in range(BATCH):
            s = left[jnp.minimum(BATCH * i + b, count - 1)]
            weight = jnp.where(BATCH * i + b < count, 1.0, 0.0).astype(F32)
            slots.append((centers[0, s], centers[1, s], s, weight))
        made = transform_slots(slots, low, wide, patterns, tables, sums, patch, wave, half, shift, back)
        for (row, col, _, _), term in zip(slots, made):
            place_term(canvas, row, col, term)


def exchange_sums(
    canvas, sums, probe, got_v, got_h, got_c, update, peak,
    low_v, low_h, low_c, pair, half, from_plane, share, from_line,
    send, recv, pair_send, pair_recv, in_send, in_recv, out_send, out_recv,
):
    row, col = lax.axis_index("row"), lax.axis_index("col")
    x, core, z, y = row // 2, lax.rem(row, 2), col // 4, lax.rem(col, 4)
    sibling = (row + 1 - 2 * core, col)
    tiles = around(row, col)
    other = jnp.where(core == 0, tiles[0][0], tiles[1][0])
    along_x = [lax.rem(x + d, 4) for d in range(4)]
    along_z = [4 * lax.rem(z + d, 4) for d in range(4)]
    along_y = [lax.rem(y + d, 4) for d in range(4)]
    cols = [along_z[d // 4] + along_y[d % 4] for d in range(16)]
    plane = [((2 * along_x[j // 4] + core, along_z[j % 4] + y), 16 * along_x[j // 4] + along_z[j % 4]) for j in range(16)]
    line = [((row, 4 * z + along_y[j]), along_y[j]) for j in range(4)]
    hops = (0, 1, 2, 1)
    order = sorted(range(1, 16), key=lambda j: -(hops[j // 4] + hops[j % 4]))
    barrier = greet([sibling, (other, col)] + tiles[2:] + [plane[j][0] for j in order] + [line[j][0] for j in (2, 1, 3)])
    pl.semaphore_wait(barrier, 26)

    mine = core * 64
    me = 16 * x + col
    to_pair = remote(sums.at[:, 1 - core], pair, pair_send.at[0], pair_recv.at[0], sibling)
    to_pair.start()

    @pl.loop(0, TILE // HALF)
    def _(i):
        rows = pl.ds(pl.multiple_of(i * HALF, HALF), HALF)
        at = pl.ds(pl.multiple_of(i * HALF + HALF, HALF), HALF)
        for p in range(2):
            low_h[0, p, rows, :] = canvas[p, 0, at, :].astype(BF16)
            low_h[1, p, rows, :] = canvas[p, PANELS + 1, at, :].astype(BF16)

    for p in range(2):
        for corner in range(4):
            at = slice(0, HALF) if corner < 2 else slice(EXT - HALF, EXT)
            low_c[corner, p] = canvas[p, (corner % 2) * (PANELS + 1), at, :].astype(BF16)
        for k in range(PANELS):
            low_v[0, p, k] = canvas[p, k + 1, 0:HALF, :].astype(BF16)
            low_v[1, p, k] = canvas[p, k + 1, EXT - HALF :, :].astype(BF16)
    opposite = (1, 0, 3, 2, 7, 6, 5, 4)
    third, pairs = TILE // 3, PANELS // 3
    parts = {}
    for part in range(3):
        some, few = slice(part * third, (part + 1) * third), slice(part * pairs, (part + 1) * pairs)
        for i in range(2):
            parts[i, part] = low_v.at[i, :, few], got_v.at[1 - i, :, few]
            parts[2 + i, part] = low_h.at[i, :, some], got_h.at[1 - i, :, some]
    for i in range(4):
        parts[4 + i, 0] = low_c.at[i], got_c.at[3 - i]
    places = sorted(parts)
    rims = []

    def send_rims(*chosen):
        for i, part in chosen:
            source, target = parts[i, part]
            arrival = recv.at[places.index((opposite[i], part))]
            rims.append(remote(source, target, send.at[places.index((i, part))], arrival, tiles[i]))
            rims[-1].start()

    squares = probe[0, 0] * probe[0, 0] + probe[0, 1] * probe[0, 1]
    squares = squares + probe[1, 0] * probe[1, 0] + probe[1, 1] * probe[1, 1]
    peak[...] = jnp.broadcast_to(jnp.max(squares, keepdims=True) + 1e-06, peak.shape)

    send_rims((2, 0), (3, 0), (0, 0), (1, 0))
    to_pair.wait()

    for q in range(PLANES + 1):
        half[q] = (sums[q, core] + pair[q]).astype(BF16)

    def rows_of(block):
        return pl.ds(pl.multiple_of(4 * block, 16), 16)

    inward = [
        remote(half.at[:, rows_of(plane[j][1])], from_plane.at[j - 1], in_send.at[j], in_recv.at[j], plane[j][0])
        for j in order
    ]
    for copy in inward:
        copy.start()
    send_rims((2, 1), (3, 1), (0, 1), (1, 1))
    for copy in reversed(inward):
        copy.wait()
    pieces = []
    for q in range(PLANES + 1):
        total = half[q, rows_of(16 * x + 4 * z), :].astype(F32)
        for j in range(15):
            total = total + from_plane[j, q].astype(F32)
        pieces.append(total)
    blank = jnp.zeros((UNIT_ROWS - 4 * PLANES - 4, LANES), F32)
    for k in range(4):
        share[k] = jnp.concatenate([piece[4 * k : 4 * k + 4] for piece in pieces] + [blank], 0).astype(BF16)
    inward = [
        remote(share.at[line[j][1]], from_line.at[j - 1], in_send.at[15 + j], in_recv.at[15 + j], line[j][0])
        for j in (2, 1, 3)
    ]
    for copy in inward:
        copy.start()
    send_rims((0, 2), (1, 2), (4, 0), (5, 0))
    for copy in inward:
        copy.wait()
    total = share[y].astype(F32)
    for j in range(3):
        total = total + from_line[j].astype(F32)
    spread = lax.rsqrt(total[4 * PLANES : 4 * PLANES + 4])
    unit = mine + me
    update[unit] = (total[0 : 4 * PLANES] * jnp.concatenate([spread] * PLANES, 0)).astype(BF16)
    outward = [
        remote(update.at[unit], update.at[unit], out_send.at[15 + j], out_recv.at[15 + j], line[j][0]) for j in (2, 1, 3)
    ]
    for copy in outward:
        copy.start()
    send_rims((6, 0), (7, 0))
    for copy in outward:
        copy.wait()
    block = update.at[pl.ds(mine + 16 * x + 4 * z, 4)]
    outward = {j: remote(block, block, out_send.at[j], out_recv.at[j], plane[j][0]) for j in order}
    for j in order:
        outward[j].start()
    send_rims((2, 2), (3, 2))
    over = []
    for j in [0] + order[::-1]:
        came = 4 * ((4 - j // 4) % 4) + (4 - j % 4) % 4
        block = update.at[pl.ds(mine + plane[came][1], 4)]
        if j:
            outward[j].wait()
        over.append(remote(block, block, pair_send.at[1 + j], pair_recv.at[1 + j], sibling))
        over[-1].start()
    for copy in over:
        copy.wait()
    for copy in rims:
        copy.wait()


def write_results(canvas, held, got_v, got_h, got_c, update, peak, probe, new_object, new_probe, stage, store):
    row, col = lax.axis_index("row"), lax.axis_index("col")
    have = inside(row, col)
    scale = 1.0 / peak[0:1, :]

    def keep(i, value):
        return jnp.where(have[i], value.astype(F32), 0.0)

    stores = []
    for k in range(PANELS):
        for p in range(2):
            side = None if k not in (0, PANELS - 1) else (0 if k == 0 else 1)
            for i in range(TILE // HALF):
                rows = slice(i * HALF, (i + 1) * HALF)
                value = canvas[p, k + 1, HALF + i * HALF : 2 * HALF + i * HALF, :]
                if i == 0:
                    value = value + keep(0, got_v[0, p, k])
                if i == TILE // HALF - 1:
                    value = value + keep(1, got_v[1, p, k])
                if side is not None:
                    value = value + keep(2 + side, got_h[side, p, rows, :])
                    if i == 0:
                        value = value + keep(4 + side, got_c[side, p])
                    if i == TILE // HALF - 1:
                        value = value + keep(6 + side, got_c[2 + side, p])
                stage[p, k, rows, :] = held[p, k, rows, :] + value * scale
        copy = pltpu.make_async_copy(stage.at[:, k], new_object.at[:, :, k * LANES : (k + 1) * LANES], store.at[k])
        copy.start()
        stores.append(copy)

    @pl.loop(0, SIZE // 8)
    def _(i):
        rows = pl.ds(pl.multiple_of(i * 8, 8), 8)
        for k in range(2):
            lanes = slice(k * LANES, (k + 1) * LANES)
            first = update[k * 64 + 2 * i].astype(F32)
            second = update[k * 64 + 2 * i + 1].astype(F32)
            for q in range(PLANES):
                value = jnp.concatenate([first[4 * q : 4 * q + 4], second[4 * q : 4 * q + 4]], 0)
                new_probe[q // 2, q % 2, rows, lanes] = probe[q // 2, q % 2, rows, lanes] + value

    for copy in stores:
        copy.wait()


def on_device(object_field, probe_modes, counts, centers, patterns):
    waves = pltpu.with_memory_space_constraint(jnp.asarray(dft_tables()), pltpu.HBM)
    dma = pltpu.SemaphoreType.DMA
    probe = pltpu.with_memory_space_constraint(probe_modes, pltpu.VMEM)
    strips = [
        pltpu.VMEM((2, 2, PANELS, HALF, LANES), BF16),
        pltpu.VMEM((2, 2, TILE, LANES), BF16),
        pltpu.VMEM((4, 2, HALF, LANES), BF16),
    ]

    def inner(*arrays):
        return [pltpu.with_memory_space_constraint(a, pltpu.VMEM) for a in arrays]

    extended = pltpu.VMEM((2, PANELS + 2, EXT, LANES), F32)
    summed = pltpu.VMEM((PLANES + 1, 2, SIZE, LANES), F32)
    work = [
        pltpu.VMEM((BATCH, 2, SIZE, SIZE), F32),
        pltpu.VMEM((BATCH, MODES, SIZE, 2 * SIZE), BF16),
        pltpu.VMEM((BATCH, MODES, 2 * SIZE, SIZE), BF16),
        pltpu.VMEM((BATCH, MODES, SIZE, 2 * SIZE), BF16),
        pltpu.VMEM((BATCH, MODES, 2 * SIZE, SIZE), BF16),
    ]
    spots = centers[0, 0]
    wide, held, amplitudes, tables, canvas, low, sums, terms = pl.pallas_call(
        exchange_object,
        out_shape=[
            extended,
            pltpu.VMEM((2, PANELS, TILE, LANES), F32),
            pltpu.VMEM(patterns.shape[2:], BF16),
            pltpu.VMEM((2, 2 * SIZE, 2 * SIZE), BF16),
            extended,
            pltpu.VMEM(probe_modes.shape, F32),
            summed,
            pltpu.VMEM((4, 2, SIZE, SIZE), F32),
        ],
        in_specs=[HBM] * 6,
        out_specs=[VMEM] * 8,
        scratch_shapes=strips[:2]
        + strips
        + [pltpu.VMEM((2, SIZE, SIZE), F32), pltpu.VMEM(probe_modes.shape, F32)]
        + [pltpu.SMEM(counts.shape, jnp.int32), pltpu.SMEM(spots.shape, jnp.int32)]
        + work
        + [dma((PANELS + 5,)), dma((8,)), dma((8,))],
        compiler_params=pltpu.CompilerParams(collective_id=0, has_side_effects=True, vmem_limit_bytes=14 * MIB),
        name="exchange_object",
    )(
        pltpu.with_memory_space_constraint(counts, pltpu.HBM),
        pltpu.with_memory_space_constraint(spots, pltpu.HBM),
        pltpu.with_memory_space_constraint(object_field, pltpu.HBM),
        pltpu.with_memory_space_constraint(patterns[0, 0], pltpu.HBM),
        waves,
        pltpu.with_memory_space_constraint(probe_modes, pltpu.HBM),
    )
    wide, held, amplitudes, tables, canvas, low, sums, terms = inner(
        wide, held, amplitudes, tables, canvas, low, sums, terms
    )
    sums, canvas = pl.pallas_call(
        process_slots,
        out_shape=[summed, extended],
        in_specs=[SMEM, SMEM] + [VMEM] * 7,
        out_specs=[VMEM, VMEM],
        scratch_shapes=[pltpu.SMEM((SLOTS + 1,), jnp.int32)] + work,
        input_output_aliases={7: 1, 8: 0},
        compiler_params=pltpu.CompilerParams(vmem_limit_bytes=10 * MIB),
        name="process_slots",
    )(counts, spots, wide, low, amplitudes, tables, terms, canvas, sums)
    sums, canvas = inner(sums, canvas)
    got_v, got_h, got_c, update, peak = pl.pallas_call(
        exchange_sums,
        out_shape=strips + [pltpu.VMEM((UNITS, 16, LANES), BF16), pltpu.VMEM((8, LANES), F32)],
        in_specs=[VMEM] * 3,
        out_specs=[VMEM] * 5,
        scratch_shapes=strips
        + [
            pltpu.VMEM((PLANES + 1, SIZE, LANES), F32),
            pltpu.VMEM((PLANES + 1, SIZE, LANES), BF16),
            pltpu.VMEM((15, PLANES + 1, 16, LANES), BF16),
            pltpu.VMEM((4, UNIT_ROWS, LANES), BF16),
            pltpu.VMEM((3, UNIT_ROWS, LANES), BF16),
            dma((16,)), dma((16,)), dma((17,)), dma((17,)), dma((19,)), dma((19,)), dma((19,)), dma((19,)),
        ],
        compiler_params=pltpu.CompilerParams(collective_id=1, has_side_effects=True, vmem_limit_bytes=9 * MIB),
        name="exchange_sums",
    )(canvas, sums, probe)
    new_object, new_probe = pl.pallas_call(
        write_results,
        out_shape=[
            jax.ShapeDtypeStruct(object_field.shape, F32),
            jax.ShapeDtypeStruct(probe_modes.shape, F32),
        ],
        in_specs=[VMEM] * 8,
        out_specs=[ANY, VMEM],
        scratch_shapes=[pltpu.VMEM((2, PANELS, TILE, LANES), F32), dma((PANELS,))],
        compiler_params=pltpu.CompilerParams(vmem_limit_bytes=8 * MIB),
        name="write_results",
    )(*inner(canvas, held, got_v, got_h, got_c, update, peak), probe)
    return new_object, new_probe


def solution(mesh):
    placed = (
        P(None, "row", "col"),
        P(),
        P(),
        P("row", "col", None, None),
        P("row", "col", None, None, None),
    )
    return jax.shard_map(
        on_device,
        mesh=mesh,
        in_specs=placed,
        out_specs=(P(None, "row", "col"), P()),
        check_vma=False,
    )
```

```python
import functools
import math

import jax
import jax.numpy as jnp
import ml_dtypes
import numpy as np
from jax import lax
from jax.experimental import pallas as pl
from jax.experimental.pallas import tpu as pltpu
from jax.sharding import PartitionSpec as P

MESH = pl.DeviceIdType.MESH
F32, BF16 = jnp.float32, jnp.bfloat16
SIZE, TILE, HALF, LANES = 256, 768, 128, 128
EXT = TILE + 2 * HALF
PANELS = TILE // LANES
MODES = 2
PLANES = 2 * MODES
N_ROW, N_COL = 8, 16
SLOTS = 12
BLOCKS = 32
BATCH = 2
VMEM = pl.BlockSpec(memory_space=pltpu.VMEM)
SMEM = pl.BlockSpec(memory_space=pltpu.SMEM)
HBM = pl.BlockSpec(memory_space=pltpu.HBM)
ANY = pl.BlockSpec(memory_space=pl.ANY)
MIB = 2**20


def dft_tables():
    indices = np.arange(SIZE)
    product = indices[:, None] * indices[None, :] % SIZE
    angles = product.astype(np.float32) * np.float32(2.0 * np.pi / SIZE)
    scale = np.float32(1.0 / math.sqrt(SIZE))
    both = np.stack([np.cos(angles) * scale, np.sin(angles) * scale])
    return both.astype(ml_dtypes.bfloat16).astype(np.float32)


def around(row, col):
    up, down = lax.rem(row + N_ROW - 1, N_ROW), lax.rem(row + 1, N_ROW)
    left, right = lax.rem(col + N_COL - 1, N_COL), lax.rem(col + 1, N_COL)
    return [(up, col), (down, col), (row, left), (row, right), (up, left), (up, right), (down, left), (down, right)]


def greet(targets):
    barrier = pltpu.get_barrier_semaphore()
    for target in targets:
        pl.semaphore_signal(barrier, inc=1, device_id=target, device_id_type=MESH)
    return barrier


def remote(src, dst, send, recv, target):
    return pltpu.make_async_remote_copy(
        src_ref=src, dst_ref=dst, send_sem=send, recv_sem=recv, device_id=target, device_id_type=MESH
    )


def inside(row, col):
    up, down, left, right = row > 0, row < N_ROW - 1, col > 0, col < N_COL - 1
    return [up, down, left, right, up & left, up & right, down & left, down & right]


def choose_slots(counts, centers):
    count = counts[lax.axis_index("row"), lax.axis_index("col")]
    picks, found, taken = [0] * 4, [0] * 4, []
    inner_seen, calm_seen = 0, 0
    for s in range(SLOTS):
        row, col = centers[0, s], centers[1, s]
        live = jnp.where(s < count, 1, 0)
        calm = live * jnp.where(col >= HALF, 1, 0) * jnp.where(col <= TILE - HALF, 1, 0)
        inner = calm * jnp.where(row >= HALF, 1, 0) * jnp.where(row <= TILE - HALF, 1, 0)
        first = inner * jnp.where(inner_seen < 2, 1, 0)
        second = (calm - first) * jnp.where(calm_seen < 2, 1, 0)
        for i in range(2):
            here = first * jnp.where(inner_seen == i, 1, 0)
            picks[i], found[i] = picks[i] + s * here, found[i] + here
            here = second * jnp.where(calm_seen == i, 1, 0)
            picks[2 + i], found[2 + i] = picks[2 + i] + s * here, found[2 + i] + here
        inner_seen, calm_seen = inner_seen + first, calm_seen + second
        taken.append((live, first + second))
    slots = []
    for s, flag in zip(picks, found):
        row = jnp.where(flag == 1, centers[0, s], HALF)
        col = jnp.where(flag == 1, centers[1, s], HALF)
        slots.append((row, col, s, jnp.where(flag == 1, 1.0, 0.0).astype(F32)))
    return slots, taken


def exchange_object(
    all_counts, all_centers, obj, patterns, waves, probe, wide, held, amplitudes, tables, canvas, low, sums, terms,
    low_v, low_h, got_v, got_h, got_c, held_waves, held_probe, counts, centers, patch, wave, half, shift, back,
    load, send, recv,
):
    row, col = lax.axis_index("row"), lax.axis_index("col")
    order = (0, PANELS - 1) + tuple(range(1, PANELS - 1))
    loads = [
        pltpu.make_async_copy(obj.at[:, :, k * LANES : (k + 1) * LANES], held.at[:, k], load.at[k])
        for k in range(PANELS)
    ]
    for k in order:
        loads[k].start()
    fetches = [
        pltpu.make_async_copy(waves, held_waves, load.at[PANELS]),
        pltpu.make_async_copy(probe, held_probe, load.at[PANELS + 1]),
        pltpu.make_async_copy(patterns, amplitudes, load.at[PANELS + 2]),
        pltpu.make_async_copy(all_counts, counts, load.at[PANELS + 3]),
        pltpu.make_async_copy(all_centers, centers, load.at[PANELS + 4]),
    ]
    for fetch in fetches:
        fetch.start()
    tiles = around(row, col)
    barrier = greet(tiles[:4])
    ends = (slice(0, HALF), slice(TILE - HALF, TILE), slice(HALF, TILE - HALF))
    upright = [
        remote(low_v.at[i], got_v.at[1 - i], send.at[i], recv.at[1 - i], tiles[i]) for i in range(2)
    ]
    sides = [
        remote(
            low_h.at[i, :, ends[part]], got_h.at[1 - i, :, ends[part]],
            send.at[2 + 3 * i + part], recv.at[5 - 3 * i + part], tiles[2 + i],
        )
        for part in range(3)
        for i in range(2)
    ]
    corners = [
        remote(got_h.at[c % 2, :, ends[1 - c // 2]], got_c.at[c], send.at[8 + c], recv.at[8 + c], tiles[1 - c // 2])
        for c in range(4)
    ]
    for step, k in enumerate(order):
        loads[k].wait()

        @pl.loop(0, TILE // HALF)
        def _(i, k=k):
            rows = pl.ds(pl.multiple_of(i * HALF, HALF), HALF)
            for p in range(2):
                rounded = held[p, k, rows, :].astype(BF16)
                wide[p, k + 1, pl.ds(pl.multiple_of(i * HALF + HALF, HALF), HALF), :] = rounded.astype(F32)
                if k == 0:
                    low_h[0, p, rows, :] = rounded
                if k == PANELS - 1:
                    low_h[1, p, rows, :] = rounded

        for p in range(2):
            low_v[0, p, k] = held[p, k, 0:HALF, :].astype(BF16)
            low_v[1, p, k] = held[p, k, TILE - HALF :, :].astype(BF16)
        if step == 1:
            pl.semaphore_wait(barrier, 4)
            for copy in sides:
                copy.start()
    for copy in upright:
        copy.start()
    have = inside(row, col)

    def keep(i, value):
        return jnp.where(have[i], value.astype(F32), 0.0)

    for fetch in fetches:
        fetch.wait()
    real, imag = slice(0, SIZE), slice(SIZE, 2 * SIZE)
    cosine, sine = held_waves[0].astype(BF16), held_waves[1].astype(BF16)
    minus = (-held_waves[1]).astype(BF16)
    for t in range(2):
        tables[t, real, real] = cosine
        tables[t, imag, imag] = cosine
        tables[t, real, imag] = sine if t else minus
        tables[t, imag, real] = minus if t else sine
    low[...] = held_probe[...].astype(BF16).astype(F32)
    sums[...] = jnp.zeros_like(sums)
    slots, _ = choose_slots(counts, centers)

    def run(i):
        made = transform_slots(
            slots[i : i + 2], low, wide, amplitudes, tables, sums, patch, wave, half, shift, back
        )
        for b in range(2):
            for p in range(2):
                terms[i + b, p] = made[b][p].astype(BF16).astype(F32)

    run(0)
    for copy in sides[:4]:
        copy.wait()
    for copy in corners:
        copy.start()
    for copy in upright:
        copy.wait()
    for p in range(2):
        for k in range(PANELS):
            wide[p, k + 1, 0:HALF, :] = keep(0, got_v[0, p, k])
            wide[p, k + 1, EXT - HALF :, :] = keep(1, got_v[1, p, k])
    run(2)

    @pl.loop(0, EXT // 32)
    def _(i):
        rows = pl.ds(pl.multiple_of(i * 32, 32), 32)
        for p in range(2):
            for k in range(PANELS + 2):
                canvas[p, k, rows, :] = jnp.zeros((32, LANES), F32)

    for copy in corners + sides[4:]:
        copy.wait()
    for p in range(2):
        for corner in range(4):
            rows = slice(0, HALF) if corner < 2 else slice(EXT - HALF, EXT)
            wide[p, (corner % 2) * (PANELS + 1), rows, :] = keep(4 + corner, got_c[corner, p])

    @pl.loop(0, TILE // HALF)
    def _(i):
        rows = pl.ds(pl.multiple_of(i * HALF, HALF), HALF)
        to = pl.ds(pl.multiple_of(i * HALF + HALF, HALF), HALF)
        for p in range(2):
            wide[p, 0, to, :] = keep(2, got_h[0, p, rows, :])
            wide[p, PANELS + 1, to, :] = keep(3, got_h[1, p, rows, :])


def transform_slots(slots, low, wide, patterns, tables, sums, patch, wave, half, shift, back):
    lane = lax.broadcasted_iota(jnp.int32, (SIZE, LANES), 1)
    real, imag = slice(0, SIZE), slice(SIZE, 2 * SIZE)
    covered = 0.0
    for b, (row, col, s, weight) in enumerate(slots):
        panel = col // LANES
        turn = col - panel * LANES
        rows = pl.ds(row, SIZE)
        field = []
        for p in range(2):
            parts = [pltpu.roll(wide[p, panel + k, rows, :], lax.rem(LANES - turn, LANES), 1) for k in range(3)]
            whole = jnp.concatenate([jnp.where(lane < LANES - turn, parts[k], parts[k + 1]) for k in range(2)], 1)
            patch[b, p] = whole
            field.append(whole)
        covered = covered + weight * (field[0] * field[0] + field[1] * field[1])
        for m in range(MODES):
            wave[b, m, :, real] = (low[m, 0] * field[0] - low[m, 1] * field[1]).astype(BF16)
            wave[b, m, :, imag] = (low[m, 0] * field[1] + low[m, 1] * field[0]).astype(BF16)
    for k in range(2):
        sums[PLANES, k] += covered[:, k * LANES : (k + 1) * LANES]
    for b in range(len(slots)):
        for m in range(MODES):
            product = jnp.dot(wave[b, m], tables[0], preferred_element_type=F32)
            half[b, m, real, :] = product[:, real].astype(BF16)
            half[b, m, imag, :] = product[:, imag].astype(BF16)
    for b, (_, _, s, weight) in enumerate(slots):
        spectra = [
            [jnp.dot(tables[1, part, :], half[b, m], preferred_element_type=F32) for part in (real, imag)]
            for m in range(MODES)
        ]
        power = (
            spectra[0][0] * spectra[0][0]
            + spectra[0][1] * spectra[0][1]
            + spectra[1][0] * spectra[1][0]
            + spectra[1][1] * spectra[1][1]
        )
        factor = weight * (patterns[s].astype(F32) * lax.rsqrt(jnp.maximum(power, 0.5)) - 1.0)
        for m in range(MODES):
            shift[b, m, :, real] = (factor * spectra[m][0]).astype(BF16)
            shift[b, m, :, imag] = (factor * spectra[m][1]).astype(BF16)
    for b in range(len(slots)):
        for m in range(MODES):
            product = jnp.dot(shift[b, m], tables[1], preferred_element_type=F32)
            back[b, m, real, :] = product[:, real].astype(BF16)
            back[b, m, imag, :] = product[:, imag].astype(BF16)
    terms = [[0.0, 0.0] for _ in slots]
    for m in range(MODES):
        gained = [0.0, 0.0]
        for b in range(len(slots)):
            change_real = jnp.dot(tables[0, real, :], back[b, m], preferred_element_type=F32)
            change_imag = jnp.dot(tables[0, imag, :], back[b, m], preferred_element_type=F32)
            terms[b][0] = terms[b][0] + low[m, 0] * change_real + low[m, 1] * change_imag
            terms[b][1] = terms[b][1] + low[m, 0] * change_imag - low[m, 1] * change_real
            gained[0] = gained[0] + patch[b, 0] * change_real + patch[b, 1] * change_imag
            gained[1] = gained[1] + patch[b, 0] * change_imag - patch[b, 1] * change_real
        for part in range(2):
            for k in range(2):
                sums[2 * m + part, k] += gained[part][:, k * LANES : (k + 1) * LANES]
    return terms


def place_term(canvas, row, col, term):
    lane = lax.broadcasted_iota(jnp.int32, (SIZE, LANES), 1)
    panel = col // LANES
    turn = col - panel * LANES
    rows = pl.ds(row, SIZE)
    for p in range(2):
        rounded = term[p].astype(BF16).astype(F32)
        first = pltpu.roll(rounded[:, :LANES], turn, 1)
        second = pltpu.roll(rounded[:, LANES:], turn, 1)
        canvas[p, panel, rows, :] += jnp.where(lane < turn, 0.0, first)
        canvas[p, panel + 1, rows, :] += jnp.where(lane < turn, first, second)
        canvas[p, panel + 2, rows, :] += jnp.where(lane < turn, second, 0.0)


def process_slots(
    counts, centers, wide, low, patterns, tables, terms, blank, begun, sums, canvas, left, patch, wave, half, shift, back
):
    slots, taken = choose_slots(counts, centers)
    for i, (row, col, _, _) in enumerate(slots):
        place_term(canvas, row, col, terms[i])
    count = 0
    for s, (live, done) in enumerate(taken):
        left[count] = s
        count = count + live - done

    @pl.loop(0, (count + BATCH - 1) // BATCH)
    def _(i):
        slots = []
        for b in range(BATCH):
            s = left[jnp.minimum(BATCH * i + b, count - 1)]
            weight = jnp.where(BATCH * i + b < count, 1.0, 0.0).astype(F32)
            slots.append((centers[0, s], centers[1, s], s, weight))
        made = transform_slots(slots, low, wide, patterns, tables, sums, patch, wave, half, shift, back)
        for (row, col, _, _), term in zip(slots, made):
            place_term(canvas, row, col, term)


def exchange_sums(
    canvas, sums, probe, got_v, got_h, got_c, update, peak,
    low_v, low_h, low_c, pair, half, from_plane, lines,
    send, recv, pair_send, pair_recv, in_send, in_recv, out_send, out_recv,
):
    row, col = lax.axis_index("row"), lax.axis_index("col")
    x, core, z, y = row // 2, lax.rem(row, 2), col // 4, lax.rem(col, 4)
    sibling = (row + 1 - 2 * core, col)
    tiles = around(row, col)
    other = jnp.where(core == 0, tiles[0][0], tiles[1][0])
    along_x = [lax.rem(x + d, 4) for d in range(4)]
    along_z = [4 * lax.rem(z + d, 4) for d in range(4)]
    along_y = [lax.rem(y + d, 4) for d in range(4)]
    cols = [along_z[d // 4] + along_y[d % 4] for d in range(16)]
    plane = [((2 * along_x[j // 4] + core, along_z[j % 4] + y), 4 * along_x[j // 4] + along_z[j % 4] // 4) for j in range(16)]
    line = [(row, 4 * z + along_y[j]) for j in range(4)]
    hops = (0, 1, 2, 1)
    order = sorted(range(1, 16), key=lambda j: -(hops[j // 4] + hops[j % 4]))
    barrier = greet([sibling, (other, col)] + tiles[2:] + [plane[j][0] for j in order] + [line[j] for j in (2, 1, 3)])
    pl.semaphore_wait(barrier, 26)

    mine = 16 * core + 4 * x + z
    to_pair = remote(sums.at[:, 1 - core], pair, pair_send.at[0], pair_recv.at[0], sibling)
    to_pair.start()

    @pl.loop(0, TILE // HALF)
    def _(i):
        rows = pl.ds(pl.multiple_of(i * HALF, HALF), HALF)
        at = pl.ds(pl.multiple_of(i * HALF + HALF, HALF), HALF)
        for p in range(2):
            low_h[0, p, rows, :] = canvas[p, 0, at, :].astype(BF16)
            low_h[1, p, rows, :] = canvas[p, PANELS + 1, at, :].astype(BF16)

    for p in range(2):
        for corner in range(4):
            at = slice(0, HALF) if corner < 2 else slice(EXT - HALF, EXT)
            low_c[corner, p] = canvas[p, (corner % 2) * (PANELS + 1), at, :].astype(BF16)
        for k in range(PANELS):
            low_v[0, p, k] = canvas[p, k + 1, 0:HALF, :].astype(BF16)
            low_v[1, p, k] = canvas[p, k + 1, EXT - HALF :, :].astype(BF16)
    opposite = (1, 0, 3, 2, 7, 6, 5, 4)
    third, pairs = TILE // 3, PANELS // 3
    parts = {}
    for part in range(3):
        some, few = slice(part * third, (part + 1) * third), slice(part * pairs, (part + 1) * pairs)
        for i in range(2):
            parts[i, part] = low_v.at[i, :, few], got_v.at[1 - i, :, few]
            parts[2 + i, part] = low_h.at[i, :, some], got_h.at[1 - i, :, some]
    for i in range(4):
        parts[4 + i, 0] = low_c.at[i], got_c.at[3 - i]
    places = sorted(parts)
    rims = []

    def send_rims(*chosen):
        for i, part in chosen:
            source, target = parts[i, part]
            arrival = recv.at[places.index((opposite[i], part))]
            rims.append(remote(source, target, send.at[places.index((i, part))], arrival, tiles[i]))
            rims[-1].start()

    squares = probe[0, 0] * probe[0, 0] + probe[0, 1] * probe[0, 1]
    squares = squares + probe[1, 0] * probe[1, 0] + probe[1, 1] * probe[1, 1]
    peak[...] = jnp.broadcast_to(jnp.max(squares, keepdims=True) + 1e-06, peak.shape)

    send_rims((2, 0), (3, 0), (0, 0), (1, 0))
    to_pair.wait()

    for q in range(PLANES + 1):
        half[q] = (sums[q, core] + pair[q]).astype(BF16)

    def rows_of(block):
        return pl.ds(pl.multiple_of(16 * block, 16), 16)

    inward = [
        remote(half.at[:, rows_of(plane[j][1])], from_plane.at[j - 1], in_send.at[j], in_recv.at[j], plane[j][0])
        for j in order
    ]
    for copy in inward:
        copy.start()
    send_rims((2, 1), (3, 1), (0, 1), (1, 1))
    for copy in reversed(inward):
        copy.wait()
    for q in range(PLANES + 1):
        total = half[q, rows_of(4 * x + z), :].astype(F32)
        for j in range(15):
            total = total + from_plane[j, q].astype(F32)
        lines[y, q] = total.astype(BF16)
    across = [
        remote(lines.at[y], lines.at[y], in_send.at[15 + j], in_recv.at[15 + j], line[j]) for j in (2, 1, 3)
    ]
    for copy in across:
        copy.start()
    send_rims((0, 2), (1, 2), (4, 0), (5, 0))
    for copy in across:
        copy.wait()
    sums_here = []
    for q in range(PLANES + 1):
        total = lines[0, q].astype(F32)
        for j in range(1, 4):
            total = total + lines[j, q].astype(F32)
        sums_here.append(total)
    spread = lax.rsqrt(sums_here[PLANES])
    for q in range(PLANES):
        update[mine, q] = (sums_here[q] * spread).astype(BF16)
    block = update.at[mine]
    outward = {j: remote(block, block, out_send.at[j], out_recv.at[j], plane[j][0]) for j in order}
    for j in order:
        outward[j].start()
    send_rims((6, 0), (7, 0), (2, 2), (3, 2))
    over = []
    for j in [0] + order[::-1]:
        came = 4 * ((4 - j // 4) % 4) + (4 - j % 4) % 4
        block = update.at[16 * core + plane[came][1]]
        if j:
            outward[j].wait()
        over.append(remote(block, block, pair_send.at[1 + j], pair_recv.at[1 + j], sibling))
        over[-1].start()
    for copy in over:
        copy.wait()
    for copy in rims:
        copy.wait()


def write_results(canvas, held, got_v, got_h, got_c, update, peak, probe, new_object, new_probe, stage, store):
    row, col = lax.axis_index("row"), lax.axis_index("col")
    have = inside(row, col)
    scale = 1.0 / peak[0:1, :]

    def keep(i, value):
        return jnp.where(have[i], value.astype(F32), 0.0)

    stores = []
    for k in range(PANELS):
        for p in range(2):
            side = None if k not in (0, PANELS - 1) else (0 if k == 0 else 1)
            for i in range(TILE // HALF):
                rows = slice(i * HALF, (i + 1) * HALF)
                value = canvas[p, k + 1, HALF + i * HALF : 2 * HALF + i * HALF, :]
                if i == 0:
                    value = value + keep(0, got_v[0, p, k])
                if i == TILE // HALF - 1:
                    value = value + keep(1, got_v[1, p, k])
                if side is not None:
                    value = value + keep(2 + side, got_h[side, p, rows, :])
                    if i == 0:
                        value = value + keep(4 + side, got_c[side, p])
                    if i == TILE // HALF - 1:
                        value = value + keep(6 + side, got_c[2 + side, p])
                stage[p, k, rows, :] = held[p, k, rows, :] + value * scale
        copy = pltpu.make_async_copy(stage.at[:, k], new_object.at[:, :, k * LANES : (k + 1) * LANES], store.at[k])
        copy.start()
        stores.append(copy)

    @pl.loop(0, SIZE // 16)
    def _(i):
        rows = pl.ds(pl.multiple_of(i * 16, 16), 16)
        for k in range(2):
            lanes = slice(k * LANES, (k + 1) * LANES)
            for q in range(PLANES):
                gained = update[k * 16 + i, q].astype(F32)
                new_probe[q // 2, q % 2, rows, lanes] = probe[q // 2, q % 2, rows, lanes] + gained

    for copy in stores:
        copy.wait()


def on_device(object_field, probe_modes, counts, centers, patterns):
    waves = pltpu.with_memory_space_constraint(jnp.asarray(dft_tables()), pltpu.HBM)
    dma = pltpu.SemaphoreType.DMA
    probe = pltpu.with_memory_space_constraint(probe_modes, pltpu.VMEM)
    strips = [
        pltpu.VMEM((2, 2, PANELS, HALF, LANES), BF16),
        pltpu.VMEM((2, 2, TILE, LANES), BF16),
        pltpu.VMEM((4, 2, HALF, LANES), BF16),
    ]

    def inner(*arrays):
        return [pltpu.with_memory_space_constraint(a, pltpu.VMEM) for a in arrays]

    extended = pltpu.VMEM((2, PANELS + 2, EXT, LANES), F32)
    summed = pltpu.VMEM((PLANES + 1, 2, SIZE, LANES), F32)
    work = [
        pltpu.VMEM((BATCH, 2, SIZE, SIZE), F32),
        pltpu.VMEM((BATCH, MODES, SIZE, 2 * SIZE), BF16),
        pltpu.VMEM((BATCH, MODES, 2 * SIZE, SIZE), BF16),
        pltpu.VMEM((BATCH, MODES, SIZE, 2 * SIZE), BF16),
        pltpu.VMEM((BATCH, MODES, 2 * SIZE, SIZE), BF16),
    ]
    spots = centers[0, 0]
    wide, held, amplitudes, tables, canvas, low, sums, terms = pl.pallas_call(
        exchange_object,
        out_shape=[
            extended,
            pltpu.VMEM((2, PANELS, TILE, LANES), F32),
            pltpu.VMEM(patterns.shape[2:], BF16),
            pltpu.VMEM((2, 2 * SIZE, 2 * SIZE), BF16),
            extended,
            pltpu.VMEM(probe_modes.shape, F32),
            summed,
            pltpu.VMEM((4, 2, SIZE, SIZE), F32),
        ],
        in_specs=[HBM] * 6,
        out_specs=[VMEM] * 8,
        scratch_shapes=strips[:2]
        + strips
        + [pltpu.VMEM((2, SIZE, SIZE), F32), pltpu.VMEM(probe_modes.shape, F32)]
        + [pltpu.SMEM(counts.shape, jnp.int32), pltpu.SMEM(spots.shape, jnp.int32)]
        + work
        + [dma((PANELS + 5,)), dma((12,)), dma((12,))],
        compiler_params=pltpu.CompilerParams(collective_id=0, has_side_effects=True, vmem_limit_bytes=14 * MIB),
        name="exchange_object",
    )(
        pltpu.with_memory_space_constraint(counts, pltpu.HBM),
        pltpu.with_memory_space_constraint(spots, pltpu.HBM),
        pltpu.with_memory_space_constraint(object_field, pltpu.HBM),
        pltpu.with_memory_space_constraint(patterns[0, 0], pltpu.HBM),
        waves,
        pltpu.with_memory_space_constraint(probe_modes, pltpu.HBM),
    )
    wide, held, amplitudes, tables, canvas, low, sums, terms = inner(
        wide, held, amplitudes, tables, canvas, low, sums, terms
    )
    sums, canvas = pl.pallas_call(
        process_slots,
        out_shape=[summed, extended],
        in_specs=[SMEM, SMEM] + [VMEM] * 7,
        out_specs=[VMEM, VMEM],
        scratch_shapes=[pltpu.SMEM((SLOTS + 1,), jnp.int32)] + work,
        input_output_aliases={7: 1, 8: 0},
        compiler_params=pltpu.CompilerParams(vmem_limit_bytes=10 * MIB),
        name="process_slots",
    )(counts, spots, wide, low, amplitudes, tables, terms, canvas, sums)
    sums, canvas = inner(sums, canvas)
    got_v, got_h, got_c, update, peak = pl.pallas_call(
        exchange_sums,
        out_shape=strips + [pltpu.VMEM((BLOCKS, PLANES, 16, LANES), BF16), pltpu.VMEM((8, LANES), F32)],
        in_specs=[VMEM] * 3,
        out_specs=[VMEM] * 5,
        scratch_shapes=strips
        + [
            pltpu.VMEM((PLANES + 1, SIZE, LANES), F32),
            pltpu.VMEM((PLANES + 1, SIZE, LANES), BF16),
            pltpu.VMEM((15, PLANES + 1, 16, LANES), BF16),
            pltpu.VMEM((4, PLANES + 1, 16, LANES), BF16),
            dma((16,)), dma((16,)), dma((17,)), dma((17,)), dma((19,)), dma((19,)), dma((16,)), dma((16,)),
        ],
        compiler_params=pltpu.CompilerParams(collective_id=1, has_side_effects=True, vmem_limit_bytes=9 * MIB),
        name="exchange_sums",
    )(canvas, sums, probe)
    new_object, new_probe = pl.pallas_call(
        write_results,
        out_shape=[
            jax.ShapeDtypeStruct(object_field.shape, F32),
            jax.ShapeDtypeStruct(probe_modes.shape, F32),
        ],
        in_specs=[VMEM] * 8,
        out_specs=[ANY, VMEM],
        scratch_shapes=[pltpu.VMEM((2, PANELS, TILE, LANES), F32), dma((PANELS,))],
        compiler_params=pltpu.CompilerParams(vmem_limit_bytes=8 * MIB),
        name="write_results",
    )(*inner(canvas, held, got_v, got_h, got_c, update, peak), probe)
    return new_object, new_probe


def solution(mesh):
    placed = (
        P(None, "row", "col"),
        P(),
        P(),
        P("row", "col", None, None),
        P("row", "col", None, None, None),
    )
    return jax.shard_map(
        on_device,
        mesh=mesh,
        in_specs=placed,
        out_specs=(P(None, "row", "col"), P()),
        check_vma=False,
    )
```

```python
import functools
import math

import jax
import jax.numpy as jnp
import ml_dtypes
import numpy as np
from jax import lax
from jax.experimental import pallas as pl
from jax.experimental.pallas import tpu as pltpu
from jax.sharding import PartitionSpec as P

MESH = pl.DeviceIdType.MESH
F32, BF16 = jnp.float32, jnp.bfloat16
SIZE, TILE, HALF, LANES = 256, 768, 128, 128
EXT = TILE + 2 * HALF
PANELS = TILE // LANES
MODES = 2
PLANES = 2 * MODES
N_ROW, N_COL = 8, 16
SLOTS = 12
BLOCKS = 32
BATCH = 2
VMEM = pl.BlockSpec(memory_space=pltpu.VMEM)
SMEM = pl.BlockSpec(memory_space=pltpu.SMEM)
HBM = pl.BlockSpec(memory_space=pltpu.HBM)
MIB = 2**20


def dft_tables():
    indices = np.arange(SIZE)
    product = indices[:, None] * indices[None, :] % SIZE
    angles = product.astype(np.float32) * np.float32(2.0 * np.pi / SIZE)
    scale = np.float32(1.0 / math.sqrt(SIZE))
    both = np.stack([np.cos(angles) * scale, np.sin(angles) * scale])
    return both.astype(ml_dtypes.bfloat16).astype(np.float32)


def around(row, col):
    up, down = lax.rem(row + N_ROW - 1, N_ROW), lax.rem(row + 1, N_ROW)
    left, right = lax.rem(col + N_COL - 1, N_COL), lax.rem(col + 1, N_COL)
    return [(up, col), (down, col), (row, left), (row, right), (up, left), (up, right), (down, left), (down, right)]


def greet(targets):
    barrier = pltpu.get_barrier_semaphore()
    for target in targets:
        pl.semaphore_signal(barrier, inc=1, device_id=target, device_id_type=MESH)
    return barrier


def remote(src, dst, send, recv, target):
    return pltpu.make_async_remote_copy(
        src_ref=src, dst_ref=dst, send_sem=send, recv_sem=recv, device_id=target, device_id_type=MESH
    )


def inside(row, col):
    up, down, left, right = row > 0, row < N_ROW - 1, col > 0, col < N_COL - 1
    return [up, down, left, right, up & left, up & right, down & left, down & right]


def choose_slots(counts, centers):
    count = counts[lax.axis_index("row"), lax.axis_index("col")]
    picks, found, taken = [0] * 4, [0] * 4, []
    inner_seen, calm_seen = 0, 0
    for s in range(SLOTS):
        row, col = centers[0, s], centers[1, s]
        live = jnp.where(s < count, 1, 0)
        calm = live * jnp.where(col >= HALF, 1, 0) * jnp.where(col <= TILE - HALF, 1, 0)
        inner = calm * jnp.where(row >= HALF, 1, 0) * jnp.where(row <= TILE - HALF, 1, 0)
        first = inner * jnp.where(inner_seen < 2, 1, 0)
        second = (calm - first) * jnp.where(calm_seen < 2, 1, 0)
        for i in range(2):
            here = first * jnp.where(inner_seen == i, 1, 0)
            picks[i], found[i] = picks[i] + s * here, found[i] + here
            here = second * jnp.where(calm_seen == i, 1, 0)
            picks[2 + i], found[2 + i] = picks[2 + i] + s * here, found[2 + i] + here
        inner_seen, calm_seen = inner_seen + first, calm_seen + second
        taken.append((live, first + second))
    slots = []
    for s, flag in zip(picks, found):
        row = jnp.where(flag == 1, centers[0, s], HALF)
        col = jnp.where(flag == 1, centers[1, s], HALF)
        slots.append((row, col, s, jnp.where(flag == 1, 1.0, 0.0).astype(F32)))
    return slots, taken


def exchange_object(
    all_counts, all_centers, obj, patterns, waves, probe, wide, held, amplitudes, tables, canvas, low, sums, terms,
    low_v, low_h, got_v, got_h, got_c, held_waves, held_probe, counts, centers, patch, wave, half, shift, back,
    load, send, recv,
):
    row, col = lax.axis_index("row"), lax.axis_index("col")
    order = (0, PANELS - 1) + tuple(range(1, PANELS - 1))
    loads = [
        pltpu.make_async_copy(obj.at[:, :, k * LANES : (k + 1) * LANES], held.at[:, k], load.at[k])
        for k in range(PANELS)
    ]
    for k in order:
        loads[k].start()
    fetches = [
        pltpu.make_async_copy(waves, held_waves, load.at[PANELS]),
        pltpu.make_async_copy(probe, held_probe, load.at[PANELS + 1]),
        pltpu.make_async_copy(patterns, amplitudes, load.at[PANELS + 2]),
        pltpu.make_async_copy(all_counts, counts, load.at[PANELS + 3]),
        pltpu.make_async_copy(all_centers, centers, load.at[PANELS + 4]),
    ]
    for fetch in fetches:
        fetch.start()
    tiles = around(row, col)
    barrier = greet(tiles[:4])
    ends = (slice(0, HALF), slice(TILE - HALF, TILE), slice(HALF, TILE - HALF))
    upright = [
        remote(low_v.at[i], got_v.at[1 - i], send.at[i], recv.at[1 - i], tiles[i]) for i in range(2)
    ]
    sides = [
        remote(
            low_h.at[i, :, ends[part]], got_h.at[1 - i, :, ends[part]],
            send.at[2 + 3 * i + part], recv.at[5 - 3 * i + part], tiles[2 + i],
        )
        for part in range(3)
        for i in range(2)
    ]
    corners = [
        remote(got_h.at[c % 2, :, ends[1 - c // 2]], got_c.at[c], send.at[8 + c], recv.at[8 + c], tiles[1 - c // 2])
        for c in range(4)
    ]
    for step, k in enumerate(order):
        loads[k].wait()

        @pl.loop(0, TILE // HALF)
        def _(i, k=k):
            rows = pl.ds(pl.multiple_of(i * HALF, HALF), HALF)
            for p in range(2):
                rounded = held[p, k, rows, :].astype(BF16)
                wide[p, k + 1, pl.ds(pl.multiple_of(i * HALF + HALF, HALF), HALF), :] = rounded.astype(F32)
                if k == 0:
                    low_h[0, p, rows, :] = rounded
                if k == PANELS - 1:
                    low_h[1, p, rows, :] = rounded

        for p in range(2):
            low_v[0, p, k] = held[p, k, 0:HALF, :].astype(BF16)
            low_v[1, p, k] = held[p, k, TILE - HALF :, :].astype(BF16)
        if step == 1:
            pl.semaphore_wait(barrier, 4)
            for copy in sides:
                copy.start()
    for copy in upright:
        copy.start()
    have = inside(row, col)

    def keep(i, value):
        return jnp.where(have[i], value.astype(F32), 0.0)

    for fetch in fetches:
        fetch.wait()
    real, imag = slice(0, SIZE), slice(SIZE, 2 * SIZE)
    cosine, sine = held_waves[0].astype(BF16), held_waves[1].astype(BF16)
    minus = (-held_waves[1]).astype(BF16)
    for t in range(2):
        tables[t, real, real] = cosine
        tables[t, imag, imag] = cosine
        tables[t, real, imag] = sine if t else minus
        tables[t, imag, real] = minus if t else sine
    low[...] = held_probe[...].astype(BF16).astype(F32)
    sums[...] = jnp.zeros_like(sums)
    slots, _ = choose_slots(counts, centers)

    def run(i):
        made = transform_slots(
            slots[i : i + 2], low, wide, amplitudes, tables, sums, patch, wave, half, shift, back
        )
        for b in range(2):
            for p in range(2):
                terms[i + b, p] = made[b][p].astype(BF16).astype(F32)

    run(0)
    for copy in sides[:4]:
        copy.wait()
    for copy in corners:
        copy.start()
    for copy in upright:
        copy.wait()
    for p in range(2):
        for k in range(PANELS):
            wide[p, k + 1, 0:HALF, :] = keep(0, got_v[0, p, k])
            wide[p, k + 1, EXT - HALF :, :] = keep(1, got_v[1, p, k])
    run(2)

    @pl.loop(0, EXT // 32)
    def _(i):
        rows = pl.ds(pl.multiple_of(i * 32, 32), 32)
        for p in range(2):
            for k in range(PANELS + 2):
                canvas[p, k, rows, :] = jnp.zeros((32, LANES), F32)

    for copy in corners + sides[4:]:
        copy.wait()
    for p in range(2):
        for corner in range(4):
            rows = slice(0, HALF) if corner < 2 else slice(EXT - HALF, EXT)
            wide[p, (corner % 2) * (PANELS + 1), rows, :] = keep(4 + corner, got_c[corner, p])

    @pl.loop(0, TILE // HALF)
    def _(i):
        rows = pl.ds(pl.multiple_of(i * HALF, HALF), HALF)
        to = pl.ds(pl.multiple_of(i * HALF + HALF, HALF), HALF)
        for p in range(2):
            wide[p, 0, to, :] = keep(2, got_h[0, p, rows, :])
            wide[p, PANELS + 1, to, :] = keep(3, got_h[1, p, rows, :])


def transform_slots(slots, low, wide, patterns, tables, sums, patch, wave, half, shift, back):
    lane = lax.broadcasted_iota(jnp.int32, (SIZE, LANES), 1)
    real, imag = slice(0, SIZE), slice(SIZE, 2 * SIZE)
    covered = 0.0
    for b, (row, col, s, weight) in enumerate(slots):
        panel = col // LANES
        turn = col - panel * LANES
        rows = pl.ds(row, SIZE)
        field = []
        for p in range(2):
            parts = [pltpu.roll(wide[p, panel + k, rows, :], lax.rem(LANES - turn, LANES), 1) for k in range(3)]
            whole = jnp.concatenate([jnp.where(lane < LANES - turn, parts[k], parts[k + 1]) for k in range(2)], 1)
            patch[b, p] = whole
            field.append(whole)
        covered = covered + weight * (field[0] * field[0] + field[1] * field[1])
        for m in range(MODES):
            wave[b, m, :, real] = (low[m, 0] * field[0] - low[m, 1] * field[1]).astype(BF16)
            wave[b, m, :, imag] = (low[m, 0] * field[1] + low[m, 1] * field[0]).astype(BF16)
    for k in range(2):
        sums[PLANES, k] += covered[:, k * LANES : (k + 1) * LANES]
    for b in range(len(slots)):
        for m in range(MODES):
            product = jnp.dot(wave[b, m], tables[0], preferred_element_type=F32)
            half[b, m, real, :] = product[:, real].astype(BF16)
            half[b, m, imag, :] = product[:, imag].astype(BF16)
    for b, (_, _, s, weight) in enumerate(slots):
        spectra = [
            [jnp.dot(tables[1, part, :], half[b, m], preferred_element_type=F32) for part in (real, imag)]
            for m in range(MODES)
        ]
        power = (
            spectra[0][0] * spectra[0][0]
            + spectra[0][1] * spectra[0][1]
            + spectra[1][0] * spectra[1][0]
            + spectra[1][1] * spectra[1][1]
        )
        factor = weight * (patterns[s].astype(F32) * lax.rsqrt(jnp.maximum(power, 0.5)) - 1.0)
        for m in range(MODES):
            shift[b, m, :, real] = (factor * spectra[m][0]).astype(BF16)
            shift[b, m, :, imag] = (factor * spectra[m][1]).astype(BF16)
    for b in range(len(slots)):
        for m in range(MODES):
            product = jnp.dot(shift[b, m], tables[1], preferred_element_type=F32)
            back[b, m, real, :] = product[:, real].astype(BF16)
            back[b, m, imag, :] = product[:, imag].astype(BF16)
    terms = [[0.0, 0.0] for _ in slots]
    for m in range(MODES):
        gained = [0.0, 0.0]
        for b in range(len(slots)):
            change_real = jnp.dot(tables[0, real, :], back[b, m], preferred_element_type=F32)
            change_imag = jnp.dot(tables[0, imag, :], back[b, m], preferred_element_type=F32)
            terms[b][0] = terms[b][0] + low[m, 0] * change_real + low[m, 1] * change_imag
            terms[b][1] = terms[b][1] + low[m, 0] * change_imag - low[m, 1] * change_real
            gained[0] = gained[0] + patch[b, 0] * change_real + patch[b, 1] * change_imag
            gained[1] = gained[1] + patch[b, 0] * change_imag - patch[b, 1] * change_real
        for part in range(2):
            for k in range(2):
                sums[2 * m + part, k] += gained[part][:, k * LANES : (k + 1) * LANES]
    return terms


def place_term(canvas, row, col, term):
    lane = lax.broadcasted_iota(jnp.int32, (SIZE, LANES), 1)
    panel = col // LANES
    turn = col - panel * LANES
    rows = pl.ds(row, SIZE)
    for p in range(2):
        rounded = term[p].astype(BF16).astype(F32)
        first = pltpu.roll(rounded[:, :LANES], turn, 1)
        second = pltpu.roll(rounded[:, LANES:], turn, 1)
        canvas[p, panel, rows, :] += jnp.where(lane < turn, 0.0, first)
        canvas[p, panel + 1, rows, :] += jnp.where(lane < turn, first, second)
        canvas[p, panel + 2, rows, :] += jnp.where(lane < turn, second, 0.0)


def process_slots(
    counts, centers, wide, low, patterns, tables, terms, blank, begun, sums, canvas, left, patch, wave, half, shift, back
):
    slots, taken = choose_slots(counts, centers)
    for i, (row, col, _, _) in enumerate(slots):
        place_term(canvas, row, col, terms[i])
    count = 0
    for s, (live, done) in enumerate(taken):
        left[count] = s
        count = count + live - done

    @pl.loop(0, (count + BATCH - 1) // BATCH)
    def _(i):
        slots = []
        for b in range(BATCH):
            s = left[jnp.minimum(BATCH * i + b, count - 1)]
            weight = jnp.where(BATCH * i + b < count, 1.0, 0.0).astype(F32)
            slots.append((centers[0, s], centers[1, s], s, weight))
        made = transform_slots(slots, low, wide, patterns, tables, sums, patch, wave, half, shift, back)
        for (row, col, _, _), term in zip(slots, made):
            place_term(canvas, row, col, term)


def exchange_sums(
    canvas, sums, probe, held, got_v, got_h, update, peak, ahead,
    low_v, low_h, low_c, got_c, pair, half, from_plane, lines,
    send, recv, pair_send, pair_recv, in_send, in_recv, out_send, out_recv,
):
    row, col = lax.axis_index("row"), lax.axis_index("col")
    x, core, z, y = row // 2, lax.rem(row, 2), col // 4, lax.rem(col, 4)
    sibling = (row + 1 - 2 * core, col)
    tiles = around(row, col)
    other = jnp.where(core == 0, tiles[0][0], tiles[1][0])
    along_x = [lax.rem(x + d, 4) for d in range(4)]
    along_z = [4 * lax.rem(z + d, 4) for d in range(4)]
    along_y = [lax.rem(y + d, 4) for d in range(4)]
    cols = [along_z[d // 4] + along_y[d % 4] for d in range(16)]
    plane = [((2 * along_x[j // 4] + core, along_z[j % 4] + y), 4 * along_x[j // 4] + along_z[j % 4] // 4) for j in range(16)]
    line = [(row, 4 * z + along_y[j]) for j in range(4)]
    hops = (0, 1, 2, 1)
    order = sorted(range(1, 16), key=lambda j: -(hops[j // 4] + hops[j % 4]))
    barrier = greet([sibling, (other, col)] + tiles[2:4] + [plane[j][0] for j in order] + [line[j] for j in (2, 1, 3)])
    pl.semaphore_wait(barrier, 22)

    mine = 16 * core + 4 * x + z
    quarters = [pl.ds(pl.multiple_of(64 * along_x[d], 64), 64) for d in (2, 1, 3, 0)]
    to_pair = [
        remote(sums.at[:, 1 - core, rows], pair.at[:, rows], pair_send.at[16 + i], pair_recv.at[16 + i], sibling)
        for i, rows in enumerate(quarters)
    ]
    for copy in to_pair:
        copy.start()

    @pl.loop(0, TILE // HALF)
    def _(i):
        rows = pl.ds(pl.multiple_of(i * HALF, HALF), HALF)
        at = pl.ds(pl.multiple_of(i * HALF + HALF, HALF), HALF)
        for p in range(2):
            low_h[0, p, rows, :] = canvas[p, 0, at, :].astype(BF16)
            low_h[1, p, rows, :] = canvas[p, PANELS + 1, at, :].astype(BF16)

    for p in range(2):
        for corner in range(4):
            at = slice(0, HALF) if corner < 2 else slice(EXT - HALF, EXT)
            low_c[corner, p] = canvas[p, (corner % 2) * (PANELS + 1), at, :].astype(BF16)
        for k in range(PANELS):
            low_v[0, p, k] = canvas[p, k + 1, 0:HALF, :].astype(BF16)
            low_v[1, p, k] = canvas[p, k + 1, EXT - HALF :, :].astype(BF16)
    opposite = (1, 0, 3, 2, 7, 6, 5, 4)
    third, pairs = TILE // 3, PANELS // 3
    parts = {}
    for part in range(3):
        some, few = slice(part * third, (part + 1) * third), slice(part * pairs, (part + 1) * pairs)
        for i in range(2):
            parts[i, part] = low_v.at[i, :, few], got_v.at[1 - i, :, few]
            parts[2 + i, part] = low_h.at[i, :, some], got_h.at[1 - i, :, some]
    for i in range(4):
        parts[i // 2, 3 + i % 2] = low_c.at[i], got_c.at[i]
    places = sorted(parts)
    rims = []

    def send_rims(*chosen):
        for i, part in chosen:
            source, target = parts[i, part]
            arrival = recv.at[places.index((1 - i if part > 2 else opposite[i], part))]
            rims.append(remote(source, target, send.at[places.index((i, part))], arrival, tiles[i]))
            rims[-1].start()

    squares = probe[0, 0] * probe[0, 0] + probe[0, 1] * probe[0, 1]
    squares = squares + probe[1, 0] * probe[1, 0] + probe[1, 1] * probe[1, 1]
    most = jnp.max(squares, keepdims=True) + 1e-06
    peak[...] = jnp.broadcast_to(most, peak.shape)

    send_rims((0, 3), (0, 4), (1, 3), (1, 4), (2, 1), (3, 1), (0, 0), (1, 0))

    def rows_of(block):
        return pl.ds(pl.multiple_of(16 * block, 16), 16)

    inward = []
    for i, d in enumerate((2, 1, 3, 0)):
        to_pair[i].wait()
        for q in range(PLANES + 1):
            half[q, quarters[i], :] = (sums[q, core, quarters[i], :] + pair[q, quarters[i], :]).astype(BF16)
        for e in (2, 1, 3, 0):
            j = 4 * d + e
            if j:
                block = half.at[:, rows_of(plane[j][1])]
                copy = remote(block, from_plane.at[j - 1], in_send.at[j], in_recv.at[j], plane[j][0])
                copy.start()
                inward.append(copy)
    for copy in rims[:4]:
        copy.wait()
    have = inside(row, col)
    for p in range(2):
        for side in range(2):
            k = side * (PANELS + 1)
            above = jnp.where(have[0], got_c[2 + side, p].astype(F32), 0.0)
            below = jnp.where(have[1], got_c[side, p].astype(F32), 0.0)
            low_h[side, p, 0:HALF, :] = (canvas[p, k, HALF : 2 * HALF, :] + above).astype(BF16)
            low_h[side, p, TILE - HALF :, :] = (canvas[p, k, TILE : TILE + HALF, :] + below).astype(BF16)
    send_rims((2, 0), (3, 0), (0, 1), (1, 1))
    scale = jnp.broadcast_to(1.0 / most, (1, LANES))

    @pl.loop(0, TILE // HALF)
    def _(i):
        rows = pl.ds(pl.multiple_of(i * HALF, HALF), HALF)
        at = pl.ds(pl.multiple_of(i * HALF + HALF, HALF), HALF)
        for p in range(2):
            for k in range(PANELS):
                ahead[p, k, rows, :] = held[p, k, rows, :] + canvas[p, k + 1, at, :] * scale

    for copy in reversed(inward):
        copy.wait()
    for q in range(PLANES + 1):
        total = half[q, rows_of(4 * x + z), :].astype(F32)
        for j in range(15):
            total = total + from_plane[j, q].astype(F32)
        lines[y, q] = total.astype(BF16)
    across = [
        remote(lines.at[y], lines.at[y], in_send.at[15 + j], in_recv.at[15 + j], line[j]) for j in (2, 1, 3)
    ]
    for copy in across:
        copy.start()
    send_rims((0, 2), (1, 2))
    for copy in across:
        copy.wait()
    sums_here = []
    for q in range(PLANES + 1):
        total = lines[0, q].astype(F32)
        for j in range(1, 4):
            total = total + lines[j, q].astype(F32)
        sums_here.append(total)
    spread = lax.rsqrt(sums_here[PLANES])
    for q in range(PLANES):
        update[mine, q] = (sums_here[q] * spread).astype(BF16)
    block = update.at[mine]
    outward = {j: remote(block, block, out_send.at[j], out_recv.at[j], plane[j][0]) for j in order}
    for j in order:
        outward[j].start()
    send_rims((2, 2), (3, 2))
    over = []
    for j in [0] + order[::-1]:
        came = 4 * ((4 - j // 4) % 4) + (4 - j % 4) % 4
        block = update.at[16 * core + plane[came][1]]
        if j:
            outward[j].wait()
        over.append(remote(block, block, pair_send.at[j], pair_recv.at[j], sibling))
        over[-1].start()
    for copy in over:
        copy.wait()
    for copy in rims[4:]:
        copy.wait()


def write_results(ahead, got_v, got_h, update, peak, probe, new_object, new_probe, rows_out, sides_out, probe_out, store):
    row, col = lax.axis_index("row"), lax.axis_index("col")
    have = inside(row, col)
    scale = 1.0 / peak[0:1, :]
    low_edge, high_edge = HALF, TILE - HALF
    stores = []

    def write(source, target):
        copy = pltpu.make_async_copy(source, target, store.at[len(stores)])
        copy.start()
        stores.append(copy)

    def lanes_of(k):
        return slice(k * LANES, (k + 1) * LANES)

    def keep(i, value):
        return jnp.where(have[i], value.astype(F32), 0.0) * scale

    for k in range(1, PANELS - 1):
        write(ahead.at[:, k, low_edge:high_edge], new_object.at[:, low_edge:high_edge, lanes_of(k)])
    for side, k in ((0, 0), (1, PANELS - 1)):
        for p in range(2):
            sides_out[side, p] = ahead[p, k, low_edge:high_edge, :] + keep(2 + side, got_h[side, p, low_edge:high_edge, :])
        write(sides_out.at[side], new_object.at[:, low_edge:high_edge, lanes_of(k)])
    for end, rows in ((0, slice(0, HALF)), (1, slice(high_edge, TILE))):
        for k in range(PANELS):
            for p in range(2):
                value = ahead[p, k, rows, :] + keep(end, got_v[end, p, k])
                if k == 0:
                    value = value + keep(2, got_h[0, p, rows, :])
                if k == PANELS - 1:
                    value = value + keep(3, got_h[1, p, rows, :])
                rows_out[end, p, k] = value
            write(rows_out.at[end, :, k], new_object.at[:, rows, lanes_of(k)])

    @pl.loop(0, SIZE // 16)
    def _(i):
        rows = pl.ds(pl.multiple_of(i * 16, 16), 16)
        for k in range(2):
            for q in range(PLANES):
                gained = update[k * 16 + i, q].astype(F32)
                probe_out[q // 2, q % 2, rows, lanes_of(k)] = probe[q // 2, q % 2, rows, lanes_of(k)] + gained

    write(probe_out, new_probe)
    for copy in stores:
        copy.wait()


def on_device(object_field, probe_modes, counts, centers, patterns):
    waves = pltpu.with_memory_space_constraint(jnp.asarray(dft_tables()), pltpu.HBM)
    dma = pltpu.SemaphoreType.DMA
    probe = pltpu.with_memory_space_constraint(probe_modes, pltpu.VMEM)
    strips = [
        pltpu.VMEM((2, 2, PANELS, HALF, LANES), BF16),
        pltpu.VMEM((2, 2, TILE, LANES), BF16),
        pltpu.VMEM((4, 2, HALF, LANES), BF16),
    ]

    def inner(*arrays):
        return [pltpu.with_memory_space_constraint(a, pltpu.VMEM) for a in arrays]

    extended = pltpu.VMEM((2, PANELS + 2, EXT, LANES), F32)
    summed = pltpu.VMEM((PLANES + 1, 2, SIZE, LANES), F32)
    work = [
        pltpu.VMEM((BATCH, 2, SIZE, SIZE), F32),
        pltpu.VMEM((BATCH, MODES, SIZE, 2 * SIZE), BF16),
        pltpu.VMEM((BATCH, MODES, 2 * SIZE, SIZE), BF16),
        pltpu.VMEM((BATCH, MODES, SIZE, 2 * SIZE), BF16),
        pltpu.VMEM((BATCH, MODES, 2 * SIZE, SIZE), BF16),
    ]
    spots = centers[0, 0]
    wide, held, amplitudes, tables, canvas, low, sums, terms = pl.pallas_call(
        exchange_object,
        out_shape=[
            extended,
            pltpu.VMEM((2, PANELS, TILE, LANES), F32),
            pltpu.VMEM(patterns.shape[2:], BF16),
            pltpu.VMEM((2, 2 * SIZE, 2 * SIZE), BF16),
            extended,
            pltpu.VMEM(probe_modes.shape, F32),
            summed,
            pltpu.VMEM((4, 2, SIZE, SIZE), F32),
        ],
        in_specs=[HBM] * 6,
        out_specs=[VMEM] * 8,
        scratch_shapes=strips[:2]
        + strips
        + [pltpu.VMEM((2, SIZE, SIZE), F32), pltpu.VMEM(probe_modes.shape, F32)]
        + [pltpu.SMEM(counts.shape, jnp.int32), pltpu.SMEM(spots.shape, jnp.int32)]
        + work
        + [dma((PANELS + 5,)), dma((12,)), dma((12,))],
        compiler_params=pltpu.CompilerParams(collective_id=0, has_side_effects=True, vmem_limit_bytes=14 * MIB),
        name="exchange_object",
    )(
        pltpu.with_memory_space_constraint(counts, pltpu.HBM),
        pltpu.with_memory_space_constraint(spots, pltpu.HBM),
        pltpu.with_memory_space_constraint(object_field, pltpu.HBM),
        pltpu.with_memory_space_constraint(patterns[0, 0], pltpu.HBM),
        waves,
        pltpu.with_memory_space_constraint(probe_modes, pltpu.HBM),
    )
    wide, held, amplitudes, tables, canvas, low, sums, terms = inner(
        wide, held, amplitudes, tables, canvas, low, sums, terms
    )
    sums, canvas = pl.pallas_call(
        process_slots,
        out_shape=[summed, extended],
        in_specs=[SMEM, SMEM] + [VMEM] * 7,
        out_specs=[VMEM, VMEM],
        scratch_shapes=[pltpu.SMEM((SLOTS + 1,), jnp.int32)] + work,
        input_output_aliases={7: 1, 8: 0},
        compiler_params=pltpu.CompilerParams(vmem_limit_bytes=10 * MIB),
        name="process_slots",
    )(counts, spots, wide, low, amplitudes, tables, terms, canvas, sums)
    sums, canvas = inner(sums, canvas)
    got_v, got_h, update, peak, ahead = pl.pallas_call(
        exchange_sums,
        out_shape=strips[:2]
        + [
            pltpu.VMEM((BLOCKS, PLANES, 16, LANES), BF16),
            pltpu.VMEM((8, LANES), F32),
            pltpu.VMEM((2, PANELS, TILE, LANES), F32),
        ],
        in_specs=[VMEM] * 4,
        out_specs=[VMEM] * 5,
        scratch_shapes=strips
        + [
            strips[2],
            pltpu.VMEM((PLANES + 1, SIZE, LANES), F32),
            pltpu.VMEM((PLANES + 1, SIZE, LANES), BF16),
            pltpu.VMEM((15, PLANES + 1, 16, LANES), BF16),
            pltpu.VMEM((4, PLANES + 1, 16, LANES), BF16),
            dma((16,)), dma((16,)), dma((20,)), dma((20,)), dma((19,)), dma((19,)), dma((16,)), dma((16,)),
        ],
        compiler_params=pltpu.CompilerParams(collective_id=1, has_side_effects=True, vmem_limit_bytes=9 * MIB),
        name="exchange_sums",
    )(canvas, sums, probe, held)
    new_object, new_probe = pl.pallas_call(
        write_results,
        out_shape=[
            jax.ShapeDtypeStruct(object_field.shape, F32),
            jax.ShapeDtypeStruct(probe_modes.shape, F32),
        ],
        in_specs=[VMEM] * 6,
        out_specs=[HBM, HBM],
        scratch_shapes=[
            pltpu.VMEM((2, 2, PANELS, HALF, LANES), F32),
            pltpu.VMEM((2, 2, TILE - 2 * HALF, LANES), F32),
            pltpu.VMEM(probe_modes.shape, F32),
            dma((3 * PANELS + 1,)),
        ],
        compiler_params=pltpu.CompilerParams(vmem_limit_bytes=8 * MIB),
        name="write_results",
    )(*inner(ahead, got_v, got_h, update, peak), probe)
    return new_object, new_probe


def solution(mesh):
    placed = (
        P(None, "row", "col"),
        P(),
        P(),
        P("row", "col", None, None),
        P("row", "col", None, None, None),
    )
    return jax.shard_map(
        on_device,
        mesh=mesh,
        in_specs=placed,
        out_specs=(P(None, "row", "col"), P()),
        check_vma=False,
    )
```

```python
import functools
import math

import jax
import jax.numpy as jnp
import ml_dtypes
import numpy as np
from jax import lax
from jax.experimental import pallas as pl
from jax.experimental.pallas import tpu as pltpu
from jax.sharding import PartitionSpec as P

MESH = pl.DeviceIdType.MESH
F32, BF16 = jnp.float32, jnp.bfloat16
SIZE, TILE, HALF, LANES = 256, 768, 128, 128
EXT = TILE + 2 * HALF
PANELS = TILE // LANES
MODES = 2
PLANES = 2 * MODES
N_ROW, N_COL = 8, 16
SLOTS = 12
BLOCKS = 32
BATCH = 2
VMEM = pl.BlockSpec(memory_space=pltpu.VMEM)
SMEM = pl.BlockSpec(memory_space=pltpu.SMEM)
HBM = pl.BlockSpec(memory_space=pltpu.HBM)
MIB = 2**20


def dft_tables():
    indices = np.arange(SIZE)
    product = indices[:, None] * indices[None, :] % SIZE
    angles = product.astype(np.float32) * np.float32(2.0 * np.pi / SIZE)
    scale = np.float32(1.0 / math.sqrt(SIZE))
    both = np.stack([np.cos(angles) * scale, np.sin(angles) * scale])
    return both.astype(ml_dtypes.bfloat16).astype(np.float32)


def around(row, col):
    up, down = lax.rem(row + N_ROW - 1, N_ROW), lax.rem(row + 1, N_ROW)
    left, right = lax.rem(col + N_COL - 1, N_COL), lax.rem(col + 1, N_COL)
    return [(up, col), (down, col), (row, left), (row, right), (up, left), (up, right), (down, left), (down, right)]


def greet(targets):
    barrier = pltpu.get_barrier_semaphore()
    for target in targets:
        pl.semaphore_signal(barrier, inc=1, device_id=target, device_id_type=MESH)
    return barrier


def remote(src, dst, send, recv, target):
    return pltpu.make_async_remote_copy(
        src_ref=src, dst_ref=dst, send_sem=send, recv_sem=recv, device_id=target, device_id_type=MESH
    )


def inside(row, col):
    up, down, left, right = row > 0, row < N_ROW - 1, col > 0, col < N_COL - 1
    return [up, down, left, right, up & left, up & right, down & left, down & right]


def choose_slots(counts, centers):
    count = counts[lax.axis_index("row"), lax.axis_index("col")]
    picks, found, taken = [0] * 4, [0] * 4, []
    inner_seen, calm_seen = 0, 0
    for s in range(SLOTS):
        row, col = centers[0, s], centers[1, s]
        live = jnp.where(s < count, 1, 0)
        calm = live * jnp.where(col >= HALF, 1, 0) * jnp.where(col <= TILE - HALF, 1, 0)
        inner = calm * jnp.where(row >= HALF, 1, 0) * jnp.where(row <= TILE - HALF, 1, 0)
        first = inner * jnp.where(inner_seen < 2, 1, 0)
        second = (calm - first) * jnp.where(calm_seen < 2, 1, 0)
        for i in range(2):
            here = first * jnp.where(inner_seen == i, 1, 0)
            picks[i], found[i] = picks[i] + s * here, found[i] + here
            here = second * jnp.where(calm_seen == i, 1, 0)
            picks[2 + i], found[2 + i] = picks[2 + i] + s * here, found[2 + i] + here
        inner_seen, calm_seen = inner_seen + first, calm_seen + second
        taken.append((live, first + second))
    slots = []
    for s, flag in zip(picks, found):
        row = jnp.where(flag == 1, centers[0, s], HALF)
        col = jnp.where(flag == 1, centers[1, s], HALF)
        slots.append((row, col, s, jnp.where(flag == 1, 1.0, 0.0).astype(F32)))
    return slots, taken


def exchange_object(
    all_counts, all_centers, obj, patterns, waves, probe, wide, held, amplitudes, tables, canvas, low, sums, terms,
    low_v, low_h, got_v, got_h, got_c, held_waves, held_probe, counts, centers, patch, wave, half, shift, back,
    load, send, recv,
):
    row, col = lax.axis_index("row"), lax.axis_index("col")
    order = (0, PANELS - 1) + tuple(range(1, PANELS - 1))
    loads = [
        pltpu.make_async_copy(obj.at[:, :, k * LANES : (k + 1) * LANES], held.at[:, k], load.at[k])
        for k in range(PANELS)
    ]
    for k in order:
        loads[k].start()
    fetches = [
        pltpu.make_async_copy(waves, held_waves, load.at[PANELS]),
        pltpu.make_async_copy(probe, held_probe, load.at[PANELS + 1]),
        pltpu.make_async_copy(patterns, amplitudes, load.at[PANELS + 2]),
        pltpu.make_async_copy(all_counts, counts, load.at[PANELS + 3]),
        pltpu.make_async_copy(all_centers, centers, load.at[PANELS + 4]),
    ]
    for fetch in fetches:
        fetch.start()
    tiles = around(row, col)
    barrier = greet(tiles[:4])
    ends = (slice(0, HALF), slice(TILE - HALF, TILE), slice(HALF, TILE - HALF))
    upright = [
        remote(low_v.at[i], got_v.at[1 - i], send.at[i], recv.at[1 - i], tiles[i]) for i in range(2)
    ]
    sides = [
        remote(
            low_h.at[i, :, ends[part]], got_h.at[1 - i, :, ends[part]],
            send.at[2 + 3 * i + part], recv.at[5 - 3 * i + part], tiles[2 + i],
        )
        for part in range(3)
        for i in range(2)
    ]
    corners = [
        remote(got_h.at[c % 2, :, ends[1 - c // 2]], got_c.at[c], send.at[8 + c], recv.at[8 + c], tiles[1 - c // 2])
        for c in range(4)
    ]
    @pl.loop(0, EXT // 32)
    def _(i):
        rows = pl.ds(pl.multiple_of(i * 32, 32), 32)
        for p in range(2):
            for k in range(PANELS + 2):
                canvas[p, k, rows, :] = jnp.zeros((32, LANES), F32)

    sums[...] = jnp.zeros_like(sums)
    for step, k in enumerate(order):
        loads[k].wait()

        @pl.loop(0, TILE // HALF)
        def _(i, k=k):
            rows = pl.ds(pl.multiple_of(i * HALF, HALF), HALF)
            for p in range(2):
                rounded = held[p, k, rows, :].astype(BF16)
                wide[p, k + 1, pl.ds(pl.multiple_of(i * HALF + HALF, HALF), HALF), :] = rounded.astype(F32)
                if k == 0:
                    low_h[0, p, rows, :] = rounded
                if k == PANELS - 1:
                    low_h[1, p, rows, :] = rounded

        for p in range(2):
            low_v[0, p, k] = held[p, k, 0:HALF, :].astype(BF16)
            low_v[1, p, k] = held[p, k, TILE - HALF :, :].astype(BF16)
        if step == 1:
            pl.semaphore_wait(barrier, 4)
            for copy in sides:
                copy.start()
    for copy in upright:
        copy.start()
    have = inside(row, col)

    def keep(i, value):
        return jnp.where(have[i], value.astype(F32), 0.0)

    for fetch in fetches:
        fetch.wait()
    real, imag = slice(0, SIZE), slice(SIZE, 2 * SIZE)
    cosine, sine = held_waves[0].astype(BF16), held_waves[1].astype(BF16)
    minus = (-held_waves[1]).astype(BF16)
    for t in range(2):
        tables[t, real, real] = cosine
        tables[t, imag, imag] = cosine
        tables[t, real, imag] = sine if t else minus
        tables[t, imag, real] = minus if t else sine
    low[...] = held_probe[...].astype(BF16).astype(F32)
    slots, _ = choose_slots(counts, centers)

    def run(i):
        made = transform_slots(
            slots[i : i + 2], low, wide, amplitudes, tables, sums, patch, wave, half, shift, back
        )
        for b in range(2):
            for p in range(2):
                terms[i + b, p] = made[b][p].astype(BF16).astype(F32)

    run(0)
    for copy in sides[:4]:
        copy.wait()
    for copy in corners:
        copy.start()
    for copy in upright:
        copy.wait()
    for p in range(2):
        for k in range(PANELS):
            wide[p, k + 1, 0:HALF, :] = keep(0, got_v[0, p, k])
            wide[p, k + 1, EXT - HALF :, :] = keep(1, got_v[1, p, k])
    run(2)

    for copy in corners + sides[4:]:
        copy.wait()
    for p in range(2):
        for corner in range(4):
            rows = slice(0, HALF) if corner < 2 else slice(EXT - HALF, EXT)
            wide[p, (corner % 2) * (PANELS + 1), rows, :] = keep(4 + corner, got_c[corner, p])

    @pl.loop(0, TILE // HALF)
    def _(i):
        rows = pl.ds(pl.multiple_of(i * HALF, HALF), HALF)
        to = pl.ds(pl.multiple_of(i * HALF + HALF, HALF), HALF)
        for p in range(2):
            wide[p, 0, to, :] = keep(2, got_h[0, p, rows, :])
            wide[p, PANELS + 1, to, :] = keep(3, got_h[1, p, rows, :])


def transform_slots(slots, low, wide, patterns, tables, sums, patch, wave, half, shift, back):
    lane = lax.broadcasted_iota(jnp.int32, (SIZE, LANES), 1)
    real, imag = slice(0, SIZE), slice(SIZE, 2 * SIZE)
    covered = 0.0
    for b, (row, col, s, weight) in enumerate(slots):
        panel = col // LANES
        turn = col - panel * LANES
        rows = pl.ds(row, SIZE)
        field = []
        for p in range(2):
            parts = [pltpu.roll(wide[p, panel + k, rows, :], lax.rem(LANES - turn, LANES), 1) for k in range(3)]
            whole = jnp.concatenate([jnp.where(lane < LANES - turn, parts[k], parts[k + 1]) for k in range(2)], 1)
            patch[b, p] = whole
            field.append(whole)
        covered = covered + weight * (field[0] * field[0] + field[1] * field[1])
        for m in range(MODES):
            wave[b, m, :, real] = (low[m, 0] * field[0] - low[m, 1] * field[1]).astype(BF16)
            wave[b, m, :, imag] = (low[m, 0] * field[1] + low[m, 1] * field[0]).astype(BF16)
    for k in range(2):
        sums[PLANES, k] += covered[:, k * LANES : (k + 1) * LANES]
    for b in range(len(slots)):
        for m in range(MODES):
            product = jnp.dot(wave[b, m], tables[0], preferred_element_type=F32)
            half[b, m, real, :] = product[:, real].astype(BF16)
            half[b, m, imag, :] = product[:, imag].astype(BF16)
    for b, (_, _, s, weight) in enumerate(slots):
        spectra = [
            [jnp.dot(tables[1, part, :], half[b, m], preferred_element_type=F32) for part in (real, imag)]
            for m in range(MODES)
        ]
        power = (
            spectra[0][0] * spectra[0][0]
            + spectra[0][1] * spectra[0][1]
            + spectra[1][0] * spectra[1][0]
            + spectra[1][1] * spectra[1][1]
        )
        factor = weight * (patterns[s].astype(F32) * lax.rsqrt(jnp.maximum(power, 0.5)) - 1.0)
        for m in range(MODES):
            shift[b, m, :, real] = (factor * spectra[m][0]).astype(BF16)
            shift[b, m, :, imag] = (factor * spectra[m][1]).astype(BF16)
    for b in range(len(slots)):
        for m in range(MODES):
            product = jnp.dot(shift[b, m], tables[1], preferred_element_type=F32)
            back[b, m, real, :] = product[:, real].astype(BF16)
            back[b, m, imag, :] = product[:, imag].astype(BF16)
    terms = [[0.0, 0.0] for _ in slots]
    for m in range(MODES):
        gained = [0.0, 0.0]
        for b in range(len(slots)):
            change_real = jnp.dot(tables[0, real, :], back[b, m], preferred_element_type=F32)
            change_imag = jnp.dot(tables[0, imag, :], back[b, m], preferred_element_type=F32)
            terms[b][0] = terms[b][0] + low[m, 0] * change_real + low[m, 1] * change_imag
            terms[b][1] = terms[b][1] + low[m, 0] * change_imag - low[m, 1] * change_real
            gained[0] = gained[0] + patch[b, 0] * change_real + patch[b, 1] * change_imag
            gained[1] = gained[1] + patch[b, 0] * change_imag - patch[b, 1] * change_real
        for part in range(2):
            for k in range(2):
                sums[2 * m + part, k] += gained[part][:, k * LANES : (k + 1) * LANES]
    return terms


def place_term(canvas, row, col, term):
    lane = lax.broadcasted_iota(jnp.int32, (SIZE, LANES), 1)
    panel = col // LANES
    turn = col - panel * LANES
    rows = pl.ds(row, SIZE)
    for p in range(2):
        rounded = term[p].astype(BF16).astype(F32)
        first = pltpu.roll(rounded[:, :LANES], turn, 1)
        second = pltpu.roll(rounded[:, LANES:], turn, 1)
        canvas[p, panel, rows, :] += jnp.where(lane < turn, 0.0, first)
        canvas[p, panel + 1, rows, :] += jnp.where(lane < turn, first, second)
        canvas[p, panel + 2, rows, :] += jnp.where(lane < turn, second, 0.0)


def process_slots(
    counts, centers, wide, low, patterns, tables, terms, blank, begun, sums, canvas, left, patch, wave, half, shift, back
):
    slots, taken = choose_slots(counts, centers)
    for i, (row, col, _, _) in enumerate(slots):
        place_term(canvas, row, col, terms[i])
    count = 0
    for s, (live, done) in enumerate(taken):
        left[count] = s
        count = count + live - done

    @pl.loop(0, (count + BATCH - 1) // BATCH)
    def _(i):
        slots = []
        for b in range(BATCH):
            s = left[jnp.minimum(BATCH * i + b, count - 1)]
            weight = jnp.where(BATCH * i + b < count, 1.0, 0.0).astype(F32)
            slots.append((centers[0, s], centers[1, s], s, weight))
        made = transform_slots(slots, low, wide, patterns, tables, sums, patch, wave, half, shift, back)
        for (row, col, _, _), term in zip(slots, made):
            place_term(canvas, row, col, term)


def exchange_sums(
    canvas, sums, probe, held, got_v, got_h, update, peak, ahead,
    low_v, low_h, low_c, got_c, pair, half, from_plane, lines,
    send, recv, pair_send, pair_recv, in_send, in_recv, out_send, out_recv,
):
    row, col = lax.axis_index("row"), lax.axis_index("col")
    x, core, z, y = row // 2, lax.rem(row, 2), col // 4, lax.rem(col, 4)
    sibling = (row + 1 - 2 * core, col)
    tiles = around(row, col)
    other = jnp.where(core == 0, tiles[0][0], tiles[1][0])
    along_x = [lax.rem(x + d, 4) for d in range(4)]
    along_z = [4 * lax.rem(z + d, 4) for d in range(4)]
    along_y = [lax.rem(y + d, 4) for d in range(4)]
    cols = [along_z[d // 4] + along_y[d % 4] for d in range(16)]
    plane = [((2 * along_x[j // 4] + core, along_z[j % 4] + y), 4 * along_x[j // 4] + along_z[j % 4] // 4) for j in range(16)]
    line = [(row, 4 * z + along_y[j]) for j in range(4)]
    hops = (0, 1, 2, 1)
    order = sorted(range(1, 16), key=lambda j: -(hops[j // 4] + hops[j % 4]))
    barrier = greet([sibling, (other, col)] + tiles[2:4] + [plane[j][0] for j in order] + [line[j] for j in (2, 1, 3)])
    pl.semaphore_wait(barrier, 22)

    mine = 16 * core + 4 * x + z
    quarters = [pl.ds(pl.multiple_of(64 * along_x[d], 64), 64) for d in (2, 1, 3, 0)]
    to_pair = [
        remote(sums.at[:, 1 - core, rows], pair.at[:, rows], pair_send.at[16 + i], pair_recv.at[16 + i], sibling)
        for i, rows in enumerate(quarters)
    ]
    for copy in to_pair:
        copy.start()

    @pl.loop(0, TILE // HALF)
    def _(i):
        rows = pl.ds(pl.multiple_of(i * HALF, HALF), HALF)
        at = pl.ds(pl.multiple_of(i * HALF + HALF, HALF), HALF)
        for p in range(2):
            low_h[0, p, rows, :] = canvas[p, 0, at, :].astype(BF16)
            low_h[1, p, rows, :] = canvas[p, PANELS + 1, at, :].astype(BF16)

    for p in range(2):
        for corner in range(4):
            at = slice(0, HALF) if corner < 2 else slice(EXT - HALF, EXT)
            low_c[corner, p] = canvas[p, (corner % 2) * (PANELS + 1), at, :].astype(BF16)
        for k in range(PANELS):
            low_v[0, p, k] = canvas[p, k + 1, 0:HALF, :].astype(BF16)
            low_v[1, p, k] = canvas[p, k + 1, EXT - HALF :, :].astype(BF16)
    opposite = (1, 0, 3, 2, 7, 6, 5, 4)
    third, pairs = TILE // 3, PANELS // 3
    parts = {}
    for part in range(3):
        some, few = slice(part * third, (part + 1) * third), slice(part * pairs, (part + 1) * pairs)
        for i in range(2):
            parts[i, part] = low_v.at[i, :, few], got_v.at[1 - i, :, few]
            parts[2 + i, part] = low_h.at[i, :, some], got_h.at[1 - i, :, some]
    for i in range(4):
        parts[i // 2, 3 + i % 2] = low_c.at[i], got_c.at[i]
    places = sorted(parts)
    rims = []

    def send_rims(*chosen):
        for i, part in chosen:
            source, target = parts[i, part]
            arrival = recv.at[places.index((1 - i if part > 2 else opposite[i], part))]
            rims.append(remote(source, target, send.at[places.index((i, part))], arrival, tiles[i]))
            rims[-1].start()

    squares = probe[0, 0] * probe[0, 0] + probe[0, 1] * probe[0, 1]
    squares = squares + probe[1, 0] * probe[1, 0] + probe[1, 1] * probe[1, 1]
    most = jnp.max(squares, keepdims=True) + 1e-06
    peak[...] = jnp.broadcast_to(most, peak.shape)

    send_rims((0, 3), (0, 4), (1, 3), (1, 4), (2, 1), (3, 1), (0, 0), (1, 0))

    def rows_of(block):
        return pl.ds(pl.multiple_of(16 * block, 16), 16)

    inward = []
    for i, d in enumerate((2, 1, 3, 0)):
        to_pair[i].wait()
        for q in range(PLANES + 1):
            half[q, quarters[i], :] = (sums[q, core, quarters[i], :] + pair[q, quarters[i], :]).astype(BF16)
        for e in (2, 1, 3, 0):
            j = 4 * d + e
            if j:
                block = half.at[:, rows_of(plane[j][1])]
                copy = remote(block, from_plane.at[j - 1], in_send.at[j], in_recv.at[j], plane[j][0])
                copy.start()
                inward.append(copy)
    for copy in rims[:4]:
        copy.wait()
    have = inside(row, col)
    for p in range(2):
        for side in range(2):
            k = side * (PANELS + 1)
            above = jnp.where(have[0], got_c[2 + side, p].astype(F32), 0.0)
            below = jnp.where(have[1], got_c[side, p].astype(F32), 0.0)
            low_h[side, p, 0:HALF, :] = (canvas[p, k, HALF : 2 * HALF, :] + above).astype(BF16)
            low_h[side, p, TILE - HALF :, :] = (canvas[p, k, TILE : TILE + HALF, :] + below).astype(BF16)
    send_rims((2, 0), (3, 0), (0, 1), (1, 1))
    scale = jnp.broadcast_to(1.0 / most, (1, LANES))

    @pl.loop(0, TILE // HALF)
    def _(i):
        rows = pl.ds(pl.multiple_of(i * HALF, HALF), HALF)
        at = pl.ds(pl.multiple_of(i * HALF + HALF, HALF), HALF)
        for p in range(2):
            for k in range(PANELS):
                ahead[p, k, rows, :] = held[p, k, rows, :] + canvas[p, k + 1, at, :] * scale

    for copy in reversed(inward):
        copy.wait()
    for q in range(PLANES + 1):
        total = half[q, rows_of(4 * x + z), :].astype(F32)
        for j in range(15):
            total = total + from_plane[j, q].astype(F32)
        lines[y, q] = total.astype(BF16)
    across = [
        remote(lines.at[y], lines.at[y], in_send.at[15 + j], in_recv.at[15 + j], line[j]) for j in (2, 1, 3)
    ]
    for copy in across:
        copy.start()
    send_rims((0, 2), (1, 2))
    for copy in across:
        copy.wait()
    sums_here = []
    for q in range(PLANES + 1):
        total = lines[0, q].astype(F32)
        for j in range(1, 4):
            total = total + lines[j, q].astype(F32)
        sums_here.append(total)
    spread = lax.rsqrt(sums_here[PLANES])
    for q in range(PLANES):
        update[mine, q] = (sums_here[q] * spread).astype(BF16)
    block = update.at[mine]
    outward = {j: remote(block, block, out_send.at[j], out_recv.at[j], plane[j][0]) for j in order}
    for j in order:
        outward[j].start()
    send_rims((2, 2), (3, 2))
    over = []
    for j in [0] + order[::-1]:
        came = 4 * ((4 - j // 4) % 4) + (4 - j % 4) % 4
        block = update.at[16 * core + plane[came][1]]
        if j:
            outward[j].wait()
        over.append(remote(block, block, pair_send.at[j], pair_recv.at[j], sibling))
        over[-1].start()
    for copy in over:
        copy.wait()
    for copy in rims[4:]:
        copy.wait()


def write_results(ahead, got_v, got_h, update, peak, probe, new_object, new_probe, rows_out, sides_out, probe_out, store):
    row, col = lax.axis_index("row"), lax.axis_index("col")
    have = inside(row, col)
    scale = 1.0 / peak[0:1, :]
    low_edge, high_edge = HALF, TILE - HALF
    stores = []

    def write(source, target):
        copy = pltpu.make_async_copy(source, target, store.at[len(stores)])
        copy.start()
        stores.append(copy)

    def lanes_of(k):
        return slice(k * LANES, (k + 1) * LANES)

    def keep(i, value):
        return jnp.where(have[i], value.astype(F32), 0.0) * scale

    for k in range(1, PANELS - 1):
        write(ahead.at[:, k, low_edge:high_edge], new_object.at[:, low_edge:high_edge, lanes_of(k)])
    for side, k in ((0, 0), (1, PANELS - 1)):
        for p in range(2):
            sides_out[side, p] = ahead[p, k, low_edge:high_edge, :] + keep(2 + side, got_h[side, p, low_edge:high_edge, :])
        write(sides_out.at[side], new_object.at[:, low_edge:high_edge, lanes_of(k)])
    for end, rows in ((0, slice(0, HALF)), (1, slice(high_edge, TILE))):
        for k in range(PANELS):
            for p in range(2):
                value = ahead[p, k, rows, :] + keep(end, got_v[end, p, k])
                if k == 0:
                    value = value + keep(2, got_h[0, p, rows, :])
                if k == PANELS - 1:
                    value = value + keep(3, got_h[1, p, rows, :])
                rows_out[end, p, k] = value
            write(rows_out.at[end, :, k], new_object.at[:, rows, lanes_of(k)])

    @pl.loop(0, SIZE // 16)
    def _(i):
        rows = pl.ds(pl.multiple_of(i * 16, 16), 16)
        for k in range(2):
            for q in range(PLANES):
                gained = update[k * 16 + i, q].astype(F32)
                probe_out[q // 2, q % 2, rows, lanes_of(k)] = probe[q // 2, q % 2, rows, lanes_of(k)] + gained

    write(probe_out, new_probe)
    for copy in stores:
        copy.wait()


def on_device(object_field, probe_modes, counts, centers, patterns):
    waves = pltpu.with_memory_space_constraint(jnp.asarray(dft_tables()), pltpu.HBM)
    dma = pltpu.SemaphoreType.DMA
    probe = pltpu.with_memory_space_constraint(probe_modes, pltpu.VMEM)
    strips = [
        pltpu.VMEM((2, 2, PANELS, HALF, LANES), BF16),
        pltpu.VMEM((2, 2, TILE, LANES), BF16),
        pltpu.VMEM((4, 2, HALF, LANES), BF16),
    ]

    def inner(*arrays):
        return [pltpu.with_memory_space_constraint(a, pltpu.VMEM) for a in arrays]

    extended = pltpu.VMEM((2, PANELS + 2, EXT, LANES), F32)
    summed = pltpu.VMEM((PLANES + 1, 2, SIZE, LANES), F32)
    work = [
        pltpu.VMEM((BATCH, 2, SIZE, SIZE), F32),
        pltpu.VMEM((BATCH, MODES, SIZE, 2 * SIZE), BF16),
        pltpu.VMEM((BATCH, MODES, 2 * SIZE, SIZE), BF16),
        pltpu.VMEM((BATCH, MODES, SIZE, 2 * SIZE), BF16),
        pltpu.VMEM((BATCH, MODES, 2 * SIZE, SIZE), BF16),
    ]
    spots = centers[0, 0]
    wide, held, amplitudes, tables, canvas, low, sums, terms = pl.pallas_call(
        exchange_object,
        out_shape=[
            extended,
            pltpu.VMEM((2, PANELS, TILE, LANES), F32),
            pltpu.VMEM(patterns.shape[2:], BF16),
            pltpu.VMEM((2, 2 * SIZE, 2 * SIZE), BF16),
            extended,
            pltpu.VMEM(probe_modes.shape, F32),
            summed,
            pltpu.VMEM((4, 2, SIZE, SIZE), F32),
        ],
        in_specs=[HBM] * 6,
        out_specs=[VMEM] * 8,
        scratch_shapes=strips[:2]
        + strips
        + [pltpu.VMEM((2, SIZE, SIZE), F32), pltpu.VMEM(probe_modes.shape, F32)]
        + [pltpu.SMEM(counts.shape, jnp.int32), pltpu.SMEM(spots.shape, jnp.int32)]
        + work
        + [dma((PANELS + 5,)), dma((12,)), dma((12,))],
        compiler_params=pltpu.CompilerParams(collective_id=0, has_side_effects=True, vmem_limit_bytes=14 * MIB),
        name="exchange_object",
    )(
        pltpu.with_memory_space_constraint(counts, pltpu.HBM),
        pltpu.with_memory_space_constraint(spots, pltpu.HBM),
        pltpu.with_memory_space_constraint(object_field, pltpu.HBM),
        pltpu.with_memory_space_constraint(patterns[0, 0], pltpu.HBM),
        waves,
        pltpu.with_memory_space_constraint(probe_modes, pltpu.HBM),
    )
    wide, held, amplitudes, tables, canvas, low, sums, terms = inner(
        wide, held, amplitudes, tables, canvas, low, sums, terms
    )
    sums, canvas = pl.pallas_call(
        process_slots,
        out_shape=[summed, extended],
        in_specs=[SMEM, SMEM] + [VMEM] * 7,
        out_specs=[VMEM, VMEM],
        scratch_shapes=[pltpu.SMEM((SLOTS + 1,), jnp.int32)] + work,
        input_output_aliases={7: 1, 8: 0},
        compiler_params=pltpu.CompilerParams(vmem_limit_bytes=10 * MIB),
        name="process_slots",
    )(counts, spots, wide, low, amplitudes, tables, terms, canvas, sums)
    sums, canvas = inner(sums, canvas)
    got_v, got_h, update, peak, ahead = pl.pallas_call(
        exchange_sums,
        out_shape=strips[:2]
        + [
            pltpu.VMEM((BLOCKS, PLANES, 16, LANES), BF16),
            pltpu.VMEM((8, LANES), F32),
            pltpu.VMEM((2, PANELS, TILE, LANES), F32),
        ],
        in_specs=[VMEM] * 4,
        out_specs=[VMEM] * 5,
        scratch_shapes=strips
        + [
            strips[2],
            pltpu.VMEM((PLANES + 1, SIZE, LANES), F32),
            pltpu.VMEM((PLANES + 1, SIZE, LANES), BF16),
            pltpu.VMEM((15, PLANES + 1, 16, LANES), BF16),
            pltpu.VMEM((4, PLANES + 1, 16, LANES), BF16),
            dma((16,)), dma((16,)), dma((20,)), dma((20,)), dma((19,)), dma((19,)), dma((16,)), dma((16,)),
        ],
        compiler_params=pltpu.CompilerParams(collective_id=1, has_side_effects=True, vmem_limit_bytes=9 * MIB),
        name="exchange_sums",
    )(canvas, sums, probe, held)
    new_object, new_probe = pl.pallas_call(
        write_results,
        out_shape=[
            jax.ShapeDtypeStruct(object_field.shape, F32),
            jax.ShapeDtypeStruct(probe_modes.shape, F32),
        ],
        in_specs=[VMEM] * 6,
        out_specs=[HBM, HBM],
        scratch_shapes=[
            pltpu.VMEM((2, 2, PANELS, HALF, LANES), F32),
            pltpu.VMEM((2, 2, TILE - 2 * HALF, LANES), F32),
            pltpu.VMEM(probe_modes.shape, F32),
            dma((3 * PANELS + 1,)),
        ],
        compiler_params=pltpu.CompilerParams(vmem_limit_bytes=8 * MIB),
        name="write_results",
    )(*inner(ahead, got_v, got_h, update, peak), probe)
    return new_object, new_probe


def solution(mesh):
    placed = (
        P(None, "row", "col"),
        P(),
        P(),
        P("row", "col", None, None),
        P("row", "col", None, None, None),
    )
    return jax.shard_map(
        on_device,
        mesh=mesh,
        in_specs=placed,
        out_specs=(P(None, "row", "col"), P()),
        check_vma=False,
    )
```

```python
import functools
import math

import jax
import jax.numpy as jnp
import ml_dtypes
import numpy as np
from jax import lax
from jax.experimental import pallas as pl
from jax.experimental.pallas import tpu as pltpu
from jax.sharding import PartitionSpec as P

MESH = pl.DeviceIdType.MESH
F32, BF16 = jnp.float32, jnp.bfloat16
SIZE, TILE, HALF, LANES = 256, 768, 128, 128
EXT = TILE + 2 * HALF
PANELS = TILE // LANES
MODES = 2
PLANES = 2 * MODES
N_ROW, N_COL = 8, 16
SLOTS = 12
BLOCKS = 32
BATCH = 2
VMEM = pl.BlockSpec(memory_space=pltpu.VMEM)
SMEM = pl.BlockSpec(memory_space=pltpu.SMEM)
HBM = pl.BlockSpec(memory_space=pltpu.HBM)
MIB = 2**20


def dft_tables():
    indices = np.arange(SIZE)
    product = indices[:, None] * indices[None, :] % SIZE
    angles = product.astype(np.float32) * np.float32(2.0 * np.pi / SIZE)
    scale = np.float32(1.0 / math.sqrt(SIZE))
    both = np.stack([np.cos(angles) * scale, np.sin(angles) * scale])
    return both.astype(ml_dtypes.bfloat16).astype(np.float32)


def around(row, col):
    up, down = lax.rem(row + N_ROW - 1, N_ROW), lax.rem(row + 1, N_ROW)
    left, right = lax.rem(col + N_COL - 1, N_COL), lax.rem(col + 1, N_COL)
    return [(up, col), (down, col), (row, left), (row, right), (up, left), (up, right), (down, left), (down, right)]


def greet(targets):
    barrier = pltpu.get_barrier_semaphore()
    for target in targets:
        pl.semaphore_signal(barrier, inc=1, device_id=target, device_id_type=MESH)
    return barrier


def remote(src, dst, send, recv, target):
    return pltpu.make_async_remote_copy(
        src_ref=src, dst_ref=dst, send_sem=send, recv_sem=recv, device_id=target, device_id_type=MESH
    )


def inside(row, col):
    up, down, left, right = row > 0, row < N_ROW - 1, col > 0, col < N_COL - 1
    return [up, down, left, right, up & left, up & right, down & left, down & right]


def choose_slots(counts, centers):
    count = counts[lax.axis_index("row"), lax.axis_index("col")]
    picks, found, taken = [0] * 4, [0] * 4, []
    inner_seen, calm_seen = 0, 0
    for s in range(SLOTS):
        row, col = centers[0, s], centers[1, s]
        live = jnp.where(s < count, 1, 0)
        calm = live * jnp.where(col >= HALF, 1, 0) * jnp.where(col <= TILE - HALF, 1, 0)
        inner = calm * jnp.where(row >= HALF, 1, 0) * jnp.where(row <= TILE - HALF, 1, 0)
        first = inner * jnp.where(inner_seen < 2, 1, 0)
        second = (calm - first) * jnp.where(calm_seen < 2, 1, 0)
        for i in range(2):
            here = first * jnp.where(inner_seen == i, 1, 0)
            picks[i], found[i] = picks[i] + s * here, found[i] + here
            here = second * jnp.where(calm_seen == i, 1, 0)
            picks[2 + i], found[2 + i] = picks[2 + i] + s * here, found[2 + i] + here
        inner_seen, calm_seen = inner_seen + first, calm_seen + second
        taken.append((live, first + second))
    slots = []
    for s, flag in zip(picks, found):
        row = jnp.where(flag == 1, centers[0, s], HALF)
        col = jnp.where(flag == 1, centers[1, s], HALF)
        slots.append((row, col, s, jnp.where(flag == 1, 1.0, 0.0).astype(F32)))
    return slots, taken


def exchange_object(
    all_counts, all_centers, obj, patterns, waves, probe, wide, held, amplitudes, tables, canvas, low, sums, terms,
    low_v, low_h, got_v, got_h, got_c, held_waves, held_probe, counts, centers, patch, wave, half, shift, back,
    load, send, recv,
):
    row, col = lax.axis_index("row"), lax.axis_index("col")
    order = (0, PANELS - 1) + tuple(range(1, PANELS - 1))
    loads = [
        pltpu.make_async_copy(obj.at[:, :, k * LANES : (k + 1) * LANES], held.at[:, k], load.at[k])
        for k in range(PANELS)
    ]
    fetches = [
        pltpu.make_async_copy(waves, held_waves, load.at[PANELS]),
        pltpu.make_async_copy(probe, held_probe, load.at[PANELS + 1]),
        pltpu.make_async_copy(patterns, amplitudes, load.at[PANELS + 2]),
        pltpu.make_async_copy(all_counts, counts, load.at[PANELS + 3]),
        pltpu.make_async_copy(all_centers, centers, load.at[PANELS + 4]),
    ]
    for copy in [loads[k] for k in order[:2]] + fetches[:2] + [loads[k] for k in order[2:]] + fetches[2:]:
        copy.start()
    tiles = around(row, col)
    barrier = greet(tiles[:4])
    ends = (slice(0, HALF), slice(TILE - HALF, TILE), slice(HALF, TILE - HALF))
    upright = [
        remote(low_v.at[i], got_v.at[1 - i], send.at[i], recv.at[1 - i], tiles[i]) for i in range(2)
    ]
    sides = [
        remote(
            low_h.at[i, :, ends[part]], got_h.at[1 - i, :, ends[part]],
            send.at[2 + 3 * i + part], recv.at[5 - 3 * i + part], tiles[2 + i],
        )
        for part in range(3)
        for i in range(2)
    ]
    corners = [
        remote(got_h.at[c % 2, :, ends[1 - c // 2]], got_c.at[c], send.at[8 + c], recv.at[8 + c], tiles[1 - c // 2])
        for c in range(4)
    ]
    @pl.loop(0, EXT // 32)
    def _(i):
        rows = pl.ds(pl.multiple_of(i * 32, 32), 32)
        for p in range(2):
            for k in range(PANELS + 2):
                canvas[p, k, rows, :] = jnp.zeros((32, LANES), F32)

    sums[...] = jnp.zeros_like(sums)
    for step, k in enumerate(order):
        loads[k].wait()

        @pl.loop(0, TILE // HALF)
        def _(i, k=k):
            rows = pl.ds(pl.multiple_of(i * HALF, HALF), HALF)
            for p in range(2):
                rounded = held[p, k, rows, :].astype(BF16)
                wide[p, k + 1, pl.ds(pl.multiple_of(i * HALF + HALF, HALF), HALF), :] = rounded.astype(F32)
                if k == 0:
                    low_h[0, p, rows, :] = rounded
                if k == PANELS - 1:
                    low_h[1, p, rows, :] = rounded

        for p in range(2):
            low_v[0, p, k] = held[p, k, 0:HALF, :].astype(BF16)
            low_v[1, p, k] = held[p, k, TILE - HALF :, :].astype(BF16)
        if step == 1:
            pl.semaphore_wait(barrier, 4)
            for copy in sides:
                copy.start()
            for fetch in fetches[:2]:
                fetch.wait()
            real, imag = slice(0, SIZE), slice(SIZE, 2 * SIZE)
            cosine, sine = held_waves[0].astype(BF16), held_waves[1].astype(BF16)
            minus = (-held_waves[1]).astype(BF16)
            for t in range(2):
                tables[t, real, real] = cosine
                tables[t, imag, imag] = cosine
                tables[t, real, imag] = sine if t else minus
                tables[t, imag, real] = minus if t else sine
            low[...] = held_probe[...].astype(BF16).astype(F32)
    for copy in upright:
        copy.start()
    have = inside(row, col)

    def keep(i, value):
        return jnp.where(have[i], value.astype(F32), 0.0)

    for fetch in fetches[2:]:
        fetch.wait()
    slots, _ = choose_slots(counts, centers)

    def run(i):
        made = transform_slots(
            slots[i : i + 2], low, wide, amplitudes, tables, sums, patch, wave, half, shift, back
        )
        for b in range(2):
            for p in range(2):
                terms[i + b, p] = made[b][p].astype(BF16).astype(F32)

    run(0)
    for copy in sides[:4]:
        copy.wait()
    for copy in corners:
        copy.start()
    for copy in upright:
        copy.wait()
    for p in range(2):
        for k in range(PANELS):
            wide[p, k + 1, 0:HALF, :] = keep(0, got_v[0, p, k])
            wide[p, k + 1, EXT - HALF :, :] = keep(1, got_v[1, p, k])
    run(2)

    for copy in corners + sides[4:]:
        copy.wait()
    for p in range(2):
        for corner in range(4):
            rows = slice(0, HALF) if corner < 2 else slice(EXT - HALF, EXT)
            wide[p, (corner % 2) * (PANELS + 1), rows, :] = keep(4 + corner, got_c[corner, p])

    @pl.loop(0, TILE // HALF)
    def _(i):
        rows = pl.ds(pl.multiple_of(i * HALF, HALF), HALF)
        to = pl.ds(pl.multiple_of(i * HALF + HALF, HALF), HALF)
        for p in range(2):
            wide[p, 0, to, :] = keep(2, got_h[0, p, rows, :])
            wide[p, PANELS + 1, to, :] = keep(3, got_h[1, p, rows, :])


def transform_slots(slots, low, wide, patterns, tables, sums, patch, wave, half, shift, back):
    lane = lax.broadcasted_iota(jnp.int32, (SIZE, LANES), 1)
    real, imag = slice(0, SIZE), slice(SIZE, 2 * SIZE)
    covered = 0.0
    for b, (row, col, s, weight) in enumerate(slots):
        panel = col // LANES
        turn = col - panel * LANES
        rows = pl.ds(row, SIZE)
        field = []
        for p in range(2):
            parts = [pltpu.roll(wide[p, panel + k, rows, :], lax.rem(LANES - turn, LANES), 1) for k in range(3)]
            whole = jnp.concatenate([jnp.where(lane < LANES - turn, parts[k], parts[k + 1]) for k in range(2)], 1)
            patch[b, p] = whole
            field.append(whole)
        covered = covered + weight * (field[0] * field[0] + field[1] * field[1])
        for m in range(MODES):
            wave[b, m, :, real] = (low[m, 0] * field[0] - low[m, 1] * field[1]).astype(BF16)
            wave[b, m, :, imag] = (low[m, 0] * field[1] + low[m, 1] * field[0]).astype(BF16)
    for k in range(2):
        sums[PLANES, k] += covered[:, k * LANES : (k + 1) * LANES]
    for b in range(len(slots)):
        for m in range(MODES):
            product = jnp.dot(wave[b, m], tables[0], preferred_element_type=F32)
            half[b, m, real, :] = product[:, real].astype(BF16)
            half[b, m, imag, :] = product[:, imag].astype(BF16)
    for b, (_, _, s, weight) in enumerate(slots):
        spectra = [
            [jnp.dot(tables[1, part, :], half[b, m], preferred_element_type=F32) for part in (real, imag)]
            for m in range(MODES)
        ]
        power = (
            spectra[0][0] * spectra[0][0]
            + spectra[0][1] * spectra[0][1]
            + spectra[1][0] * spectra[1][0]
            + spectra[1][1] * spectra[1][1]
        )
        factor = weight * (patterns[s].astype(F32) * lax.rsqrt(jnp.maximum(power, 0.5)) - 1.0)
        for m in range(MODES):
            shift[b, m, :, real] = (factor * spectra[m][0]).astype(BF16)
            shift[b, m, :, imag] = (factor * spectra[m][1]).astype(BF16)
    for b in range(len(slots)):
        for m in range(MODES):
            product = jnp.dot(shift[b, m], tables[1], preferred_element_type=F32)
            back[b, m, real, :] = product[:, real].astype(BF16)
            back[b, m, imag, :] = product[:, imag].astype(BF16)
    terms = [[0.0, 0.0] for _ in slots]
    for m in range(MODES):
        gained = [0.0, 0.0]
        for b in range(len(slots)):
            change_real = jnp.dot(tables[0, real, :], back[b, m], preferred_element_type=F32)
            change_imag = jnp.dot(tables[0, imag, :], back[b, m], preferred_element_type=F32)
            terms[b][0] = terms[b][0] + low[m, 0] * change_real + low[m, 1] * change_imag
            terms[b][1] = terms[b][1] + low[m, 0] * change_imag - low[m, 1] * change_real
            gained[0] = gained[0] + patch[b, 0] * change_real + patch[b, 1] * change_imag
            gained[1] = gained[1] + patch[b, 0] * change_imag - patch[b, 1] * change_real
        for part in range(2):
            for k in range(2):
                sums[2 * m + part, k] += gained[part][:, k * LANES : (k + 1) * LANES]
    return terms


def place_term(canvas, row, col, term):
    lane = lax.broadcasted_iota(jnp.int32, (SIZE, LANES), 1)
    panel = col // LANES
    turn = col - panel * LANES
    rows = pl.ds(row, SIZE)
    for p in range(2):
        rounded = term[p].astype(BF16).astype(F32)
        first = pltpu.roll(rounded[:, :LANES], turn, 1)
        second = pltpu.roll(rounded[:, LANES:], turn, 1)
        canvas[p, panel, rows, :] += jnp.where(lane < turn, 0.0, first)
        canvas[p, panel + 1, rows, :] += jnp.where(lane < turn, first, second)
        canvas[p, panel + 2, rows, :] += jnp.where(lane < turn, second, 0.0)


def process_slots(
    counts, centers, wide, low, patterns, tables, terms, blank, begun, sums, canvas, left, patch, wave, half, shift, back
):
    slots, taken = choose_slots(counts, centers)
    for i, (row, col, _, _) in enumerate(slots):
        place_term(canvas, row, col, terms[i])
    count = 0
    for s, (live, done) in enumerate(taken):
        left[count] = s
        count = count + live - done

    @pl.loop(0, (count + BATCH - 1) // BATCH)
    def _(i):
        slots = []
        for b in range(BATCH):
            s = left[jnp.minimum(BATCH * i + b, count - 1)]
            weight = jnp.where(BATCH * i + b < count, 1.0, 0.0).astype(F32)
            slots.append((centers[0, s], centers[1, s], s, weight))
        made = transform_slots(slots, low, wide, patterns, tables, sums, patch, wave, half, shift, back)
        for (row, col, _, _), term in zip(slots, made):
            place_term(canvas, row, col, term)


def exchange_sums(
    canvas, sums, probe, held, got_v, got_h, update, peak, ahead,
    low_v, low_h, low_c, got_c, pair, half, from_plane, lines,
    send, recv, pair_send, pair_recv, in_send, in_recv, out_send, out_recv,
):
    row, col = lax.axis_index("row"), lax.axis_index("col")
    x, core, z, y = row // 2, lax.rem(row, 2), col // 4, lax.rem(col, 4)
    sibling = (row + 1 - 2 * core, col)
    tiles = around(row, col)
    other = jnp.where(core == 0, tiles[0][0], tiles[1][0])
    along_x = [lax.rem(x + d, 4) for d in range(4)]
    along_z = [4 * lax.rem(z + d, 4) for d in range(4)]
    along_y = [lax.rem(y + d, 4) for d in range(4)]
    cols = [along_z[d // 4] + along_y[d % 4] for d in range(16)]
    plane = [((2 * along_x[j // 4] + core, along_z[j % 4] + y), 4 * along_x[j // 4] + along_z[j % 4] // 4) for j in range(16)]
    line = [(row, 4 * z + along_y[j]) for j in range(4)]
    hops = (0, 1, 2, 1)
    order = sorted(range(1, 16), key=lambda j: -(hops[j // 4] + hops[j % 4]))
    barrier = greet([sibling, (other, col)] + tiles[2:4] + [plane[j][0] for j in order] + [line[j] for j in (2, 1, 3)])
    pl.semaphore_wait(barrier, 22)

    mine = 16 * core + 4 * x + z
    quarters = [pl.ds(pl.multiple_of(64 * along_x[d], 64), 64) for d in (2, 1, 3, 0)]
    to_pair = [
        remote(sums.at[:, 1 - core, rows], pair.at[:, rows], pair_send.at[16 + i], pair_recv.at[16 + i], sibling)
        for i, rows in enumerate(quarters)
    ]
    for copy in to_pair:
        copy.start()

    @pl.loop(0, TILE // HALF)
    def _(i):
        rows = pl.ds(pl.multiple_of(i * HALF, HALF), HALF)
        at = pl.ds(pl.multiple_of(i * HALF + HALF, HALF), HALF)
        for p in range(2):
            low_h[0, p, rows, :] = canvas[p, 0, at, :].astype(BF16)
            low_h[1, p, rows, :] = canvas[p, PANELS + 1, at, :].astype(BF16)

    for p in range(2):
        for corner in range(4):
            at = slice(0, HALF) if corner < 2 else slice(EXT - HALF, EXT)
            low_c[corner, p] = canvas[p, (corner % 2) * (PANELS + 1), at, :].astype(BF16)
        for k in range(PANELS):
            low_v[0, p, k] = canvas[p, k + 1, 0:HALF, :].astype(BF16)
            low_v[1, p, k] = canvas[p, k + 1, EXT - HALF :, :].astype(BF16)
    opposite = (1, 0, 3, 2, 7, 6, 5, 4)
    third, pairs = TILE // 3, PANELS // 3
    parts = {}
    for part in range(3):
        some, few = slice(part * third, (part + 1) * third), slice(part * pairs, (part + 1) * pairs)
        for i in range(2):
            parts[i, part] = low_v.at[i, :, few], got_v.at[1 - i, :, few]
            parts[2 + i, part] = low_h.at[i, :, some], got_h.at[1 - i, :, some]
    for i in range(4):
        parts[i // 2, 3 + i % 2] = low_c.at[i], got_c.at[i]
    places = sorted(parts)
    rims = []

    def send_rims(*chosen):
        for i, part in chosen:
            source, target = parts[i, part]
            arrival = recv.at[places.index((1 - i if part > 2 else opposite[i], part))]
            rims.append(remote(source, target, send.at[places.index((i, part))], arrival, tiles[i]))
            rims[-1].start()

    squares = probe[0, 0] * probe[0, 0] + probe[0, 1] * probe[0, 1]
    squares = squares + probe[1, 0] * probe[1, 0] + probe[1, 1] * probe[1, 1]
    most = jnp.max(squares, keepdims=True) + 1e-06
    peak[...] = jnp.broadcast_to(most, peak.shape)

    send_rims((0, 3), (0, 4), (1, 3), (1, 4), (2, 1), (3, 1), (0, 0), (1, 0))

    def rows_of(block):
        return pl.ds(pl.multiple_of(16 * block, 16), 16)

    inward = []
    for i, d in enumerate((2, 1, 3, 0)):
        to_pair[i].wait()
        for q in range(PLANES + 1):
            half[q, quarters[i], :] = (sums[q, core, quarters[i], :] + pair[q, quarters[i], :]).astype(BF16)
        for e in (2, 1, 3, 0):
            j = 4 * d + e
            if j:
                block = half.at[:, rows_of(plane[j][1])]
                copy = remote(block, from_plane.at[j - 1], in_send.at[j], in_recv.at[j], plane[j][0])
                copy.start()
                inward.append(copy)
    for copy in rims[:4]:
        copy.wait()
    have = inside(row, col)
    for p in range(2):
        for side in range(2):
            k = side * (PANELS + 1)
            above = jnp.where(have[0], got_c[2 + side, p].astype(F32), 0.0)
            below = jnp.where(have[1], got_c[side, p].astype(F32), 0.0)
            low_h[side, p, 0:HALF, :] = (canvas[p, k, HALF : 2 * HALF, :] + above).astype(BF16)
            low_h[side, p, TILE - HALF :, :] = (canvas[p, k, TILE : TILE + HALF, :] + below).astype(BF16)
    send_rims((2, 0), (3, 0), (0, 1), (1, 1))
    scale = jnp.broadcast_to(1.0 / most, (1, LANES))

    @pl.loop(0, TILE // HALF)
    def _(i):
        rows = pl.ds(pl.multiple_of(i * HALF, HALF), HALF)
        at = pl.ds(pl.multiple_of(i * HALF + HALF, HALF), HALF)
        for p in range(2):
            for k in range(PANELS):
                ahead[p, k, rows, :] = held[p, k, rows, :] + canvas[p, k + 1, at, :] * scale

    for copy in reversed(inward):
        copy.wait()
    for q in range(PLANES + 1):
        total = half[q, rows_of(4 * x + z), :].astype(F32)
        for j in range(15):
            total = total + from_plane[j, q].astype(F32)
        lines[y, q] = total.astype(BF16)
    across = [
        remote(lines.at[y], lines.at[y], in_send.at[15 + j], in_recv.at[15 + j], line[j]) for j in (2, 1, 3)
    ]
    for copy in across:
        copy.start()
    send_rims((0, 2), (1, 2))
    for copy in across:
        copy.wait()
    sums_here = []
    for q in range(PLANES + 1):
        total = lines[0, q].astype(F32)
        for j in range(1, 4):
            total = total + lines[j, q].astype(F32)
        sums_here.append(total)
    spread = lax.rsqrt(sums_here[PLANES])
    for q in range(PLANES):
        update[mine, q] = (sums_here[q] * spread).astype(BF16)
    block = update.at[mine]
    outward = {j: remote(block, block, out_send.at[j], out_recv.at[j], plane[j][0]) for j in order}
    for j in order:
        outward[j].start()
    send_rims((2, 2), (3, 2))
    over = []
    for j in [0] + order[::-1]:
        came = 4 * ((4 - j // 4) % 4) + (4 - j % 4) % 4
        block = update.at[16 * core + plane[came][1]]
        if j:
            outward[j].wait()
        over.append(remote(block, block, pair_send.at[j], pair_recv.at[j], sibling))
        over[-1].start()
    for copy in over:
        copy.wait()
    for copy in rims[4:]:
        copy.wait()


def write_results(ahead, got_v, got_h, update, peak, probe, new_object, new_probe, rows_out, sides_out, probe_out, store):
    row, col = lax.axis_index("row"), lax.axis_index("col")
    have = inside(row, col)
    scale = 1.0 / peak[0:1, :]
    low_edge, high_edge = HALF, TILE - HALF
    stores = []

    def write(source, target):
        copy = pltpu.make_async_copy(source, target, store.at[len(stores)])
        copy.start()
        stores.append(copy)

    def lanes_of(k):
        return slice(k * LANES, (k + 1) * LANES)

    def keep(i, value):
        return jnp.where(have[i], value.astype(F32), 0.0) * scale

    for k in range(1, PANELS - 1):
        write(ahead.at[:, k, low_edge:high_edge], new_object.at[:, low_edge:high_edge, lanes_of(k)])
    for side, k in ((0, 0), (1, PANELS - 1)):
        for p in range(2):
            sides_out[side, p] = ahead[p, k, low_edge:high_edge, :] + keep(2 + side, got_h[side, p, low_edge:high_edge, :])
        write(sides_out.at[side], new_object.at[:, low_edge:high_edge, lanes_of(k)])
    for end, rows in ((0, slice(0, HALF)), (1, slice(high_edge, TILE))):
        for k in range(PANELS):
            for p in range(2):
                value = ahead[p, k, rows, :] + keep(end, got_v[end, p, k])
                if k == 0:
                    value = value + keep(2, got_h[0, p, rows, :])
                if k == PANELS - 1:
                    value = value + keep(3, got_h[1, p, rows, :])
                rows_out[end, p, k] = value
            write(rows_out.at[end, :, k], new_object.at[:, rows, lanes_of(k)])

    @pl.loop(0, SIZE // 16)
    def _(i):
        rows = pl.ds(pl.multiple_of(i * 16, 16), 16)
        for k in range(2):
            for q in range(PLANES):
                gained = update[k * 16 + i, q].astype(F32)
                probe_out[q // 2, q % 2, rows, lanes_of(k)] = probe[q // 2, q % 2, rows, lanes_of(k)] + gained

    write(probe_out, new_probe)
    for copy in stores:
        copy.wait()


def on_device(object_field, probe_modes, counts, centers, patterns):
    waves = pltpu.with_memory_space_constraint(jnp.asarray(dft_tables()), pltpu.HBM)
    dma = pltpu.SemaphoreType.DMA
    probe = pltpu.with_memory_space_constraint(probe_modes, pltpu.VMEM)
    strips = [
        pltpu.VMEM((2, 2, PANELS, HALF, LANES), BF16),
        pltpu.VMEM((2, 2, TILE, LANES), BF16),
        pltpu.VMEM((4, 2, HALF, LANES), BF16),
    ]

    def inner(*arrays):
        return [pltpu.with_memory_space_constraint(a, pltpu.VMEM) for a in arrays]

    extended = pltpu.VMEM((2, PANELS + 2, EXT, LANES), F32)
    summed = pltpu.VMEM((PLANES + 1, 2, SIZE, LANES), F32)
    work = [
        pltpu.VMEM((BATCH, 2, SIZE, SIZE), F32),
        pltpu.VMEM((BATCH, MODES, SIZE, 2 * SIZE), BF16),
        pltpu.VMEM((BATCH, MODES, 2 * SIZE, SIZE), BF16),
        pltpu.VMEM((BATCH, MODES, SIZE, 2 * SIZE), BF16),
        pltpu.VMEM((BATCH, MODES, 2 * SIZE, SIZE), BF16),
    ]
    spots = centers[0, 0]
    wide, held, amplitudes, tables, canvas, low, sums, terms = pl.pallas_call(
        exchange_object,
        out_shape=[
            extended,
            pltpu.VMEM((2, PANELS, TILE, LANES), F32),
            pltpu.VMEM(patterns.shape[2:], BF16),
            pltpu.VMEM((2, 2 * SIZE, 2 * SIZE), BF16),
            extended,
            pltpu.VMEM(probe_modes.shape, F32),
            summed,
            pltpu.VMEM((4, 2, SIZE, SIZE), F32),
        ],
        in_specs=[HBM] * 6,
        out_specs=[VMEM] * 8,
        scratch_shapes=strips[:2]
        + strips
        + [pltpu.VMEM((2, SIZE, SIZE), F32), pltpu.VMEM(probe_modes.shape, F32)]
        + [pltpu.SMEM(counts.shape, jnp.int32), pltpu.SMEM(spots.shape, jnp.int32)]
        + work
        + [dma((PANELS + 5,)), dma((12,)), dma((12,))],
        compiler_params=pltpu.CompilerParams(collective_id=0, has_side_effects=True, vmem_limit_bytes=14 * MIB),
        name="exchange_object",
    )(
        pltpu.with_memory_space_constraint(counts, pltpu.HBM),
        pltpu.with_memory_space_constraint(spots, pltpu.HBM),
        pltpu.with_memory_space_constraint(object_field, pltpu.HBM),
        pltpu.with_memory_space_constraint(patterns[0, 0], pltpu.HBM),
        waves,
        pltpu.with_memory_space_constraint(probe_modes, pltpu.HBM),
    )
    wide, held, amplitudes, tables, canvas, low, sums, terms = inner(
        wide, held, amplitudes, tables, canvas, low, sums, terms
    )
    sums, canvas = pl.pallas_call(
        process_slots,
        out_shape=[summed, extended],
        in_specs=[SMEM, SMEM] + [VMEM] * 7,
        out_specs=[VMEM, VMEM],
        scratch_shapes=[pltpu.SMEM((SLOTS + 1,), jnp.int32)] + work,
        input_output_aliases={7: 1, 8: 0},
        compiler_params=pltpu.CompilerParams(vmem_limit_bytes=10 * MIB),
        name="process_slots",
    )(counts, spots, wide, low, amplitudes, tables, terms, canvas, sums)
    sums, canvas = inner(sums, canvas)
    got_v, got_h, update, peak, ahead = pl.pallas_call(
        exchange_sums,
        out_shape=strips[:2]
        + [
            pltpu.VMEM((BLOCKS, PLANES, 16, LANES), BF16),
            pltpu.VMEM((8, LANES), F32),
            pltpu.VMEM((2, PANELS, TILE, LANES), F32),
        ],
        in_specs=[VMEM] * 4,
        out_specs=[VMEM] * 5,
        scratch_shapes=strips
        + [
            strips[2],
            pltpu.VMEM((PLANES + 1, SIZE, LANES), F32),
            pltpu.VMEM((PLANES + 1, SIZE, LANES), BF16),
            pltpu.VMEM((15, PLANES + 1, 16, LANES), BF16),
            pltpu.VMEM((4, PLANES + 1, 16, LANES), BF16),
            dma((16,)), dma((16,)), dma((20,)), dma((20,)), dma((19,)), dma((19,)), dma((16,)), dma((16,)),
        ],
        compiler_params=pltpu.CompilerParams(collective_id=1, has_side_effects=True, vmem_limit_bytes=9 * MIB),
        name="exchange_sums",
    )(canvas, sums, probe, held)
    new_object, new_probe = pl.pallas_call(
        write_results,
        out_shape=[
            jax.ShapeDtypeStruct(object_field.shape, F32),
            jax.ShapeDtypeStruct(probe_modes.shape, F32),
        ],
        in_specs=[VMEM] * 6,
        out_specs=[HBM, HBM],
        scratch_shapes=[
            pltpu.VMEM((2, 2, PANELS, HALF, LANES), F32),
            pltpu.VMEM((2, 2, TILE - 2 * HALF, LANES), F32),
            pltpu.VMEM(probe_modes.shape, F32),
            dma((3 * PANELS + 1,)),
        ],
        compiler_params=pltpu.CompilerParams(vmem_limit_bytes=8 * MIB),
        name="write_results",
    )(*inner(ahead, got_v, got_h, update, peak), probe)
    return new_object, new_probe


def solution(mesh):
    placed = (
        P(None, "row", "col"),
        P(),
        P(),
        P("row", "col", None, None),
        P("row", "col", None, None, None),
    )
    return jax.shard_map(
        on_device,
        mesh=mesh,
        in_specs=placed,
        out_specs=(P(None, "row", "col"), P()),
        check_vma=False,
    )
```
